128 devices in a mesh: grp: 8 (over x_lo, y), ctx: 16 (over z, x_hi, core).
Axes of the slice: x: 4 (x_hi: 2, x_lo: 2; x = x_hi * 2 + x_lo), y: 4, z: 4, core: 2. Of those that a mesh axis runs over, the one named last changes fastest.
Arguments:
- tokens: bfloat16 [8, 2048, 1024], P('grp', 'ctx'), may hold values from -6 to 6
- blocks: int32 [8, 2048], P('grp'), may hold values from 0 to 15, never falling along the last dimension, each value on 1 to 256 neighbouring positions
- w_query: bfloat16 [1024, 1024], P(('grp', 'ctx')), may hold values from -0.1875 to 0.1875
- w_key: bfloat16 [1024, 1024], P(('grp', 'ctx')), may hold values from -0.1875 to 0.1875
- w_value: bfloat16 [1024, 1024], P(('grp', 'ctx')), may hold values from -0.1875 to 0.1875
- w_out: bfloat16 [1024, 1024], P(('grp', 'ctx')), may hold values from -1 to 1
- w_gate: bfloat16 [1024, 2816], P(('grp', 'ctx')), may hold values from -0.1875 to 0.1875
- w_up: bfloat16 [1024, 2816], P(('grp', 'ctx')), may hold values from -0.1875 to 0.1875
- w_down: bfloat16 [2816, 1024], P(None, ('grp', 'ctx')), may hold values from -0.109375 to 0.109375
- norm_attn: bfloat16 [1024], P(('grp', 'ctx')), may hold values from 0.099609375 to 1.8984375
- norm_mlp: bfloat16 [1024], P(('grp', 'ctx')), may hold values from 0.099609375 to 1.8984375
- cotangent: bfloat16 [8, 2048, 1024], P('grp', 'ctx'), may hold values from -6 to 6
Outputs:
- output: bfloat16 [8, 2048, 1024], P('grp', 'ctx')
- grad_tokens: float32 [8, 2048, 1024], P('grp', 'ctx')
- grad_query: float32 [1024, 1024], P('ctx')
- grad_key: float32 [1024, 1024], P('ctx')
- grad_value: float32 [1024, 1024], P('ctx')
- grad_out: float32 [1024, 1024], P('ctx')
- grad_gate: float32 [1024, 2816], P('ctx')
- grad_up: float32 [1024, 2816], P('ctx')
- grad_down: float32 [2816, 1024], P(None, 'ctx')
- grad_norm_attn: float32 [1024], P('ctx')
- grad_norm_mlp: float32 [1024], P('ctx')
The draws below stay inside these ranges and needn't reach their ends.
Inputs may be any that keep to these rules, and one draw needn't show every extreme that they name: `blocks`: along each sequence the ids never fall; each id covers 1 to 256 consecutive tokens, and some id covers exactly 256.
All inputs are finite; a program needn't handle non-finite values.
Results may differ from the reference program's by a relative error of at most 0.025.
Values may be sent and summed in bfloat16 or wider, within the bound.
A program may use at most 256 MiB of HBM per device.

```python
import math
import jax
import jax.numpy as jnp
import numpy as np
from jax import lax

D = 1024
H = 16
HD = 64
FF = 2816
SEQ_LEN = 2048
BLK = 256
SEQS = 8


def steps_of(key, extent, pieces, smallest, largest):
    gain = 1.0
    for axis_at, parts in pieces:
        draws = jax.random.uniform(jax.random.fold_in(jax.random.fold_in(key, 6), axis_at), (parts,), jnp.float32, smallest / len(pieces), largest / len(pieces))
        gain = gain * jnp.repeat(jnp.exp(draws), extent[axis_at] // parts).reshape((-1,) + (1,) * (len(extent) - 1 - axis_at))
    return gain


def profile(number_of, total, bound, lean):
    weights = [(1 << 20) // math.isqrt(rank ** lean) + 1 for rank in range(2, number_of + 1)]
    rest, given = total - bound - (number_of - 1), [1] * (number_of - 1)
    while rest > 0:
        movable = [i for i in range(number_of - 1) if given[i] < bound]
        whole, remaining = sum([weights[i] for i in movable]), rest
        for i in movable:
            extra = min(bound - given[i], max(1, remaining * weights[i] // whole), rest)
            given[i] = given[i] + extra
            rest = rest - extra
    return np.array([bound] + given)


def uneven(rng, count, total, most, skew):
    if count == 2:
        one = jax.random.randint(rng, (), max(1, total - most), min(most, total - 1) + 1)
        return jnp.stack([one, total - one])
    tallies = jnp.asarray(profile(count, total, most, skew), jnp.int32)
    twos = (count - 1) // 2
    donor, taker = tallies[1:1 + 2 * twos:2], tallies[2:2 + 2 * twos:2]
    slack = jnp.minimum(donor - 1, most - taker)
    shifted = jax.random.randint(jax.random.fold_in(rng, 1), (twos,), 0, 1 << 20) % (slack + 1)
    tallies = tallies.at[1:1 + 2 * twos:2].set(donor - shifted).at[2:2 + 2 * twos:2].set(taker + shifted)
    return tallies[jax.random.permutation(jax.random.fold_in(rng, 2), count)]


def bell_draw(key, extent, scale, bound, cuts=(), dtype=jnp.bfloat16):
    gain = steps_of(key, extent, cuts, -0.22, 0.18) if cuts else 1.0
    result = jax.random.normal(key, extent, jnp.float32) * scale * gain
    return jnp.minimum(jnp.maximum(result, -bound), bound).astype(dtype)


def setup_inputs(seed: int = 0) -> dict:
    streams_of = jax.random.split(jax.random.key(seed), 13)
    return {
        "tokens": bell_draw(streams_of[0], (SEQS, SEQ_LEN, D), 1.0, 6.0, ((0, 8), (1, 16))),
        "blocks": jax.vmap(lambda own: jnp.searchsorted(jnp.cumsum(uneven(own, 2 * SEQ_LEN // BLK, SEQ_LEN, BLK, 0)), jnp.arange(SEQ_LEN), side="right"))(jax.random.split(streams_of[1], SEQS)).reshape((SEQS, SEQ_LEN)).astype(jnp.int32),
        "w_query": bell_draw(streams_of[2], (D, D), D ** -0.5, 0.1875, ((0, 128),)),
        "w_key": bell_draw(streams_of[3], (D, D), D ** -0.5, 0.1875, ((0, 128),)),
        "w_value": bell_draw(streams_of[4], (D, D), D ** -0.5, 0.1875, ((0, 128),)),
        "w_out": bell_draw(streams_of[5], (D, D), (D // 32) ** -0.5, 1.0, ((0, 128),)),
        "w_gate": bell_draw(streams_of[6], (D, FF), D ** -0.5, 0.1875, ((0, 128),)),
        "w_up": bell_draw(streams_of[7], (D, FF), D ** -0.5, 0.1875, ((0, 128),)),
        "w_down": bell_draw(streams_of[8], (FF, D), FF ** -0.5, 0.109375, ((1, 128),)),
        "norm_attn": jnp.clip(1.0 + 0.18 * jax.random.normal(streams_of[9], (D,), jnp.float32), 0.099609375, 1.8984375).astype(jnp.bfloat16),
        "norm_mlp": jnp.clip(1.0 + 0.18 * jax.random.normal(streams_of[10], (D,), jnp.float32), 0.099609375, 1.8984375).astype(jnp.bfloat16),
        "cotangent": bell_draw(streams_of[11], (SEQS, SEQ_LEN, D), 1.0, 6.0, ((0, 8), (1, 16))),
    }


@jax.custom_vjp
def low(v):
    return lax.optimization_barrier(v.astype(jnp.bfloat16)).astype(jnp.float32)

@jax.custom_vjp
def low_back(v):
    return v

def low_keep(v):
    return (low(v), None)

def low_pass(kept, grad):
    return (grad,)

def back_keep(v):
    return (v, None)

def back_low(kept, grad):
    return (low(grad),)
low.defvjp(low_keep, low_pass)
low_back.defvjp(back_keep, back_low)
epsilon = 1e-05
highest = lax.Precision.HIGHEST

def product(left, right):
    return jnp.dot(left, right, precision=highest)

def rms_scale(values):
    return values * lax.rsqrt(lax.optimization_barrier(jnp.mean(values * values, axis=-1, keepdims=True)) + epsilon)

def rotary(values, positions):
    half_size = values.shape[-1] // 2
    frequency = 10000.0 ** (-2.0 * jnp.arange(half_size).astype(jnp.float32) / values.shape[-1])
    angles = positions.astype(jnp.float32)[:, None] * frequency[None, :]
    cosine = jnp.cos(angles)[:, None, :]
    sine_turn = jnp.sin(angles)[:, None, :]
    first_half = values[..., :half_size]
    second_half = values[..., half_size:]
    return jnp.concatenate([first_half * cosine - second_half * sine_turn, second_half * cosine + first_half * sine_turn], axis=-1)

def attend(queries, key_heads, value_heads, query_ids, key_ids):
    raw_scores = low_back(HD ** (-0.5) * jnp.einsum('qhd,khd->hqk', queries, key_heads, precision=highest))
    visible = key_ids[None, None, :] <= query_ids[None, :, None]
    scores = jnp.where(visible, raw_scores, -1e+30)
    top_score = lax.optimization_barrier(jnp.max(scores, axis=-1, keepdims=True))
    log_total = jnp.log(lax.optimization_barrier(jnp.sum(jnp.exp(scores - top_score), axis=-1, keepdims=True))) + top_score
    probabilities = low(jnp.exp(scores - log_total))
    return low(low_back(jnp.einsum('hqk,khd->qhd', probabilities, value_heads, precision=highest)))

def layer_step(layer_weights, layer_tokens, seq_blocks):
    w_query, w_key, w_value, w_out, w_gate, w_up, w_down, norm_attn, norm_mlp = layer_weights
    positions = jnp.arange(SEQ_LEN)
    normed = low(rms_scale(layer_tokens) * norm_attn)
    query_heads = low(rotary(low_back(product(normed, w_query)).reshape(SEQ_LEN, H, HD), positions))
    key_heads = low(rotary(low_back(product(normed, w_key)).reshape(SEQ_LEN, H, HD), positions))
    value_heads = low(low_back(product(normed, w_value))).reshape(SEQ_LEN, H, HD)
    block_rows = min(512, SEQ_LEN)

    def query_block(row_start):
        queries = lax.dynamic_slice_in_dim(query_heads, row_start, block_rows, 0)
        query_ids = lax.dynamic_slice_in_dim(seq_blocks, row_start, block_rows, 0)
        return attend(queries, key_heads, value_heads, query_ids, seq_blocks)
    row_starts = (jnp.arange(SEQ_LEN // block_rows) * block_rows).astype(jnp.int32)
    mixed_rows = lax.map(jax.checkpoint(query_block), row_starts).reshape(SEQ_LEN, H * HD)
    hidden = layer_tokens + low_back(product(mixed_rows, w_out))
    normed_mid = low(rms_scale(hidden) * norm_mlp)
    gate_sums = low_back(product(normed_mid, w_gate))
    up_sums = low_back(product(normed_mid, w_up))
    activation = low(jax.nn.silu(gate_sums) * up_sums)
    return hidden + low_back(product(activation, w_down))

def reference(tokens, blocks, w_query, w_key, w_value, w_out, w_gate, w_up, w_down, norm_attn, norm_mlp, cotangent):
    weights = tuple((member.astype(jnp.float32) for member in (w_query, w_key, w_value, w_out, w_gate, w_up, w_down, norm_attn, norm_mlp)))

    def one_sequence(running, inputs):
        seq_tokens, seq_blocks, seq_grad = inputs

        def forward(layer_weights, layer_tokens):
            return layer_step(layer_weights, layer_tokens, seq_blocks)
        output, pullback = jax.vjp(forward, weights, seq_tokens.astype(jnp.float32))
        weight_grads, token_grads = pullback(seq_grad.astype(jnp.float32))
        running = jax.tree.map(jnp.add, running, weight_grads)
        return (running, (output.astype(jnp.bfloat16), token_grads))
    start_sums = tuple((jnp.zeros(member.shape, jnp.float32) for member in weights))
    totals, (outputs, token_grads) = lax.scan(one_sequence, start_sums, (tokens, blocks, cotangent))
    return (outputs, token_grads, totals[0], totals[1], totals[2], totals[3], totals[4], totals[5], totals[6], totals[7], totals[8])
```

```python
import functools

import jax
import jax.numpy as jnp
import numpy as np
from jax import lax
from jax.experimental import pallas as pl
from jax.experimental.pallas import tpu as pltpu
from jax.sharding import PartitionSpec as P

MESH = pl.DeviceIdType.MESH
F32 = jnp.float32
BF16 = jnp.bfloat16
EPS = 1e-05
HD = 64
SLICE = 352
WIDE = 384
QKV, GATE, DOWN, OUT = 0, 384, 1152, 1536
NEAR = (0, 1, 3, 2)


def mm(left, right):
    return jnp.dot(left, right, preferred_element_type=F32)


def mt(left, right):
    return lax.dot_general(left, right, (((1,), (1,)), ((), ())), preferred_element_type=F32)


def tm(left, right):
    return lax.dot_general(left, right, (((0,), (0,)), ((), ())), preferred_element_type=F32)


def turn(values, cosine, sine):
    lane = lax.broadcasted_iota(jnp.int32, values.shape, 1)
    ahead = pltpu.roll(values, 96, 1)
    behind = pltpu.roll(values, 32, 1)
    return values * cosine + jnp.where(lax.rem(lane, 64) < 32, ahead, behind) * sine


HELD = {
    "pair": ((16, 6656), F32),
    "wz": ((4, 16, 2048), BF16),
    "wrow": ((4, 16, 2048), BF16),
    "w": ((8, 4, 2, 16, 1536), BF16),
    "wo": ((2, 8, 4, 2, 16, 512), BF16),
    "u1": ((4, 2, 128, 1024), BF16),
    "gg": ((4, 2, 128, 1024), BF16),
    "u2": ((4, 2, 128, 1024), BF16),
    "db": ((4, 2, 128, 1024), BF16),
    "cos": ((4, 256, 128), F32),
    "sin": ((4, 256, 128), F32),
    "q": ((4, 256, 128), BF16),
    "kv": ((4, 2, 2, 256, 128), BF16),
    "score": ((2, 8, 256, 256), F32),
    "top": ((2, 256, 128), F32),
    "acc": ((2, 256, 128), F32),
    "mix": ((4, 256, 128), F32),
    "mixb": ((4, 2, 128, 128), BF16),
    "mixin": ((4, 2, 128, 128), BF16),
    "lse": ((4, 256, 128), F32),
    "hidden": ((128, 1024), F32),
    "unit2": ((128, 1024), F32),
    "r2": ((128, 1), F32),
    "dgu": ((4, 256, 2 * WIDE), BF16),
    "act": ((4, 256, WIDE), BF16),
    "gh": ((128, 1024), F32),
    "dmixb": ((4, 2, 128, 128), BF16),
    "dmix": ((4, 2, 128, 128), BF16),
    "dq": ((4, 256, 128), F32),
    "dkvs": ((4, 2, 256, 128), BF16),
    "dkvr": ((4, 2, 256, 128), BF16),
    "dqkv": ((4, 256, 384), BF16),
    "gf": ((16, 64, 1152), BF16),
    "gfr": ((16, 64, 1152), BF16),
    "gq": ((16, 64, 512), BF16),
    "gqr": ((16, 64, 512), BF16),
    "go": ((2, 8, 64, 128), BF16),
    "gor": ((16, 64, 128), BF16),
    "sf": ((64, 1152), BF16),
    "sq": ((64, 512), BF16),
    "so": ((64, 128), BF16),
}
for kind in ("e2", "out", "e1"):
    HELD[kind + "p"] = ((4, 2, 128, 1024), BF16)
    HELD[kind + "d"] = ((4, 128, 1024), BF16)
    HELD[kind + "r"] = ((3, 128, 1024), BF16)

INPUTS = ("x", "g", "wsrc", "idrow", "idcol", "cosines", "sines")
OUTPUTS = {
    "y": ((128, 1024), BF16),
    "gx": ((128, 1024), F32),
    "ff": ((8, 64, 1152), BF16),
    "fq": ((8, 64, 512), BF16),
    "fo": ((8, 64, 128), BF16),
}
COPIES = 320


def device(at):
    return (at["xl"] * 4 + at["y"], at["z"] * 4 + at["xh"] * 2 + at["e"])


class Links:
    def __init__(self, send, recv, near):
        self.send, self.recv, self.near = send, recv, near
        self.count = self.count_near = 0
        self.started = []

    def slots(self, many):
        self.count += many
        return self.count - many

    def make(self, src, dst, peer, slot=None, landing=None):
        slot = self.slots(1) if slot is None else slot
        landing = slot if landing is None else landing
        return pltpu.make_async_remote_copy(
            src_ref=src,
            dst_ref=dst,
            send_sem=self.send.at[slot],
            recv_sem=self.recv.at[landing],
            device_id=device(peer),
            device_id_type=MESH,
        )

    def go(self, src, dst, peer):
        copy = self.make(src, dst, peer)
        copy.start()
        self.started.append(copy)
        return copy

    def here(self, src, dst):
        copy = pltpu.make_async_copy(src, dst, self.near.at[self.count_near])
        self.count_near += 1
        copy.start()
        return copy


def kernel(*refs):
    n_in, n_out = len(INPUTS), len(OUTPUTS)
    r = dict(zip(INPUTS, refs[:n_in]))
    r.update(zip(OUTPUTS, refs[n_in : n_in + n_out]))
    r.update(zip(HELD, refs[n_in + n_out : n_in + n_out + len(HELD)]))
    links = Links(*refs[n_in + n_out + len(HELD) :])
    grp, ctx = lax.axis_index("grp"), lax.axis_index("ctx")
    me = {
        "xl": lax.div(grp, 4),
        "y": lax.rem(grp, 4),
        "z": lax.div(ctx, 4),
        "xh": lax.rem(lax.div(ctx, 2), 2),
        "e": lax.rem(ctx, 2),
    }
    xl, y, z, xh, e = (me[k] for k in ("xl", "y", "z", "xh", "e"))
    x = xh * 2 + xl

    def other_core(at):
        return {**at, "e": 1 - at["e"]}

    def along_z(by):
        return {**me, "z": lax.rem(z + by + 4, 4)}

    def in_plane(dx, dy):
        to = lax.rem(x + dx, 4)
        return {**me, "xl": lax.rem(to, 2), "xh": lax.div(to, 2), "y": lax.rem(y + dy, 4)}

    def group(dxl, dy):
        return {**me, "xl": lax.rem(xl + dxl, 2), "y": lax.rem(y + dy, 4)}

    partner = other_core(me)
    across = in_plane(2, 0)
    plane = sorted(
        ((dx, dy) for dx in range(4) for dy in range(4) if dx or dy),
        key=lambda d: -min(d[0], 4 - d[0]) - min(d[1], 4 - d[1]),
    )
    groups = [(dxl, dy) for dxl in range(2) for dy in range(4)]

    tables = [
        links.here(r["cosines"].at[:, xh], r["cos"]),
        links.here(r["sines"].at[:, xh], r["sin"]),
    ]
    rows = r["x"][...].astype(F32)
    r1 = lax.rsqrt(jnp.mean(rows * rows, axis=-1, keepdims=True) + EPS)
    r["u1"].at[z, e][...] = (rows * r1).astype(BF16)
    r["gg"].at[z, e][...] = r["g"][...]
    own_rows = pl.ds(pl.multiple_of(e * 8, 8), 8)
    r["pair"][own_rows, :] = r["wsrc"].at[e][...]

    sem = pltpu.get_barrier_semaphore()

    def greet(peer):
        pl.semaphore_signal(sem, inc=1, device_id=device(peer), device_id_type=MESH)

    fin_self = jnp.logical_and(z == y, e == xl)
    out_self = e == xh
    peers = [partner] + [along_z(i) for i in (1, 2, 3)] + [other_core(along_z(i)) for i in (1, 2, 3)]
    peers += [in_plane(*d) for d in plane]
    for peer in peers:
        greet(peer)
    for dz in range(4):
        for de in range(2):
            source = {**me, "xl": e, "y": z, "z": lax.rem(z + dz, 4), "e": lax.rem(e + de, 2)}
            if dz or de:
                greet(source)
            else:
                pl.when(jnp.logical_not(fin_self))(functools.partial(greet, source))
    for d in groups:
        source = {**group(*d), "xh": e, "e": xh}
        if d != (0, 0):
            greet(source)
        else:
            pl.when(jnp.logical_not(out_self))(functools.partial(greet, source))
    extra = 16 - fin_self.astype(jnp.int32) - out_self.astype(jnp.int32)
    pl.semaphore_wait(sem, len(peers) + extra)

    class Gather:
        def __init__(self, buf):
            self.buf = buf
            self.out = {0: None}
            self.over = {}

        def start(self):
            mine = self.buf.at[z, e]
            for i in NEAR[1:]:
                self.out[i] = links.go(mine, mine, along_z(i))
            self.over[0] = links.go(mine, mine, partner)

        def pass_on(self, i):
            self.out[i].wait_recv()
            block = self.buf.at[lax.rem(z - i + 4, 4), e]
            self.over[i] = links.go(block, block, partner)

        def ready(self, i):
            self.over[i].wait_recv()

    class Scatter:
        def __init__(self, kind):
            self.p, self.d, self.r = (r[kind + k] for k in "pdr")
            self.over, self.out = {}, {}

        def put(self, i, value):
            zz = lax.rem(z - i + 4, 4)
            self.p.at[zz][...] = value.astype(BF16).reshape(2, 128, 1024)
            self.over[i] = links.go(self.p.at[zz, 1 - e], self.d.at[zz], partner)

        def send(self, i):
            zz = lax.rem(z - i + 4, 4)
            if i:
                self.over[i].wait_recv()
                mine = self.p.at[zz, e]
                mine[...] = (mine[...].astype(F32) + self.d.at[zz][...].astype(F32)).astype(BF16)
                self.out[i] = links.go(mine, self.r.at[i - 1], along_z(-i))

        def total(self):
            self.over[0].wait_recv()
            result = self.p.at[z, e][...].astype(F32) + self.d.at[z][...].astype(F32)
            for i in NEAR[1:]:
                self.out[i].wait_recv()
                result = result + self.r[i - 1].astype(F32)
            return result

    swap = links.go(r["wsrc"].at[1 - e], r["pair"].at[own_rows, :], partner)
    gather1 = Gather(r["u1"])
    gather1.start()
    swap.wait_recv()
    for zz in range(4):
        r["wz"][zz, :, :OUT] = r["pair"][:, zz * OUT : (zz + 1) * OUT].astype(BF16)
        r["wz"][zz, :, OUT:] = r["pair"][:, 4 * OUT :].astype(BF16)
    column = [
        links.go(r["wz"].at[lax.rem(z + i, 4)], r["wrow"].at[z], along_z(i)) for i in NEAR[1:]
    ]
    r["wrow"].at[z][...] = r["wz"].at[z][...]
    for copy in column:
        copy.wait_recv()
    gather_g = Gather(r["gg"])

    def spread(lo, hi, dst):
        part = r["wrow"].at[:, :, pl.ds(lo, hi - lo)]
        return [links.go(part, dst, in_plane(*d)) for d in plane]

    came_qkv = spread(QKV, GATE, r["w"].at[grp, :, xh, :, pl.ds(QKV, GATE)])
    r["w"].at[grp, :, xh][...] = r["wrow"][:, :, :OUT]
    r["wo"].at[e, grp, :, xh][...] = r["wrow"][:, :, OUT:]
    for i in NEAR[1:]:
        gather1.pass_on(i)
    gather_g.start()
    came_out = spread(OUT, 2048, r["wo"].at[e, grp, :, xh])
    came_feed = spread(GATE, OUT, r["w"].at[grp, :, xh, :, pl.ds(GATE, OUT - GATE)])
    for copy in tables:
        copy.wait()
    for copy in came_qkv:
        copy.wait_recv()

    w_qkv = r["w"][:, :, :, :, QKV:GATE].reshape(1024, GATE - QKV)
    came_kv = []
    for i in NEAR:
        gather1.ready(i)
        zz = lax.rem(z - i + 4, 4)
        qkv = mm(r["u1"].at[zz][...].reshape(256, 1024), w_qkv)
        cosine, sine = r["cos"].at[zz][...], r["sin"].at[zz][...]
        r["q"].at[zz][...] = (turn(qkv[:, :128], cosine, sine).astype(BF16) * 0.125).astype(BF16)
        r["kv"].at[zz, xh, 0][...] = turn(qkv[:, 128:256], cosine, sine).astype(BF16)
        r["kv"].at[zz, xh, 1][...] = qkv[:, 256:].astype(BF16)
        tile = r["kv"].at[zz, xh]
        came_kv.append(links.go(tile, tile, across))
    for copy in came_kv:
        copy.wait_recv()

    first = lax.broadcasted_iota(jnp.int32, (256, 128), 1) < HD

    def halves(pair):
        zero = jnp.zeros_like(pair)
        return jnp.where(first, pair, zero), jnp.where(first, zero, pair)

    def tiles_of(qi):
        own = 2 * qi + xh
        return own, jnp.minimum(own + 2, 8)

    mix_over = links.slots(4)
    mix_here = links.slots(4)

    def mix_copy(i, at_e, base):
        to = {**me, "z": lax.rem(z + i, 4), "e": at_e}
        return links.make(
            r["mixb"].at[lax.rem(z + i, 4), at_e], r["mixin"].at[z, e], to, base + i
        )

    def attend(i, _):
        qi = lax.rem(z + i, 4)
        own, many = tiles_of(qi)
        queries = halves(r["q"].at[qi][...])
        query_ids = r["idcol"].at[own][...]
        r["top"][...] = jnp.full((2, 256, 128), -3e38, F32)

        def one(j, _):
            keys = r["kv"].at[lax.div(j, 2), lax.rem(j, 2), 0][...]
            seen = r["idrow"].at[j][...] <= query_ids
            for h in range(2):
                score = jnp.where(seen, mt(queries[h], keys), -1e30)
                r["score"].at[h, j][...] = score
                r["top"][h] = jnp.maximum(
                    r["top"][h], jnp.maximum(score[:, :128], score[:, 128:])
                )
            return 0

        lax.fori_loop(0, many, one, 0)
        tops = [jnp.max(r["top"][h], axis=1, keepdims=True) for h in range(2)]
        r["top"][...] = jnp.zeros((2, 256, 128), F32)
        r["acc"][...] = jnp.zeros((2, 256, 128), F32)

        def two(j, _):
            values = r["kv"].at[lax.div(j, 2), lax.rem(j, 2), 1][...]
            for h in range(2):
                weight = jnp.exp(r["score"].at[h, j][...] - tops[h])
                r["top"][h] += weight[:, :128] + weight[:, 128:]
                r["acc"][h] += mm(weight.astype(BF16), values)
            return 0

        lax.fori_loop(0, many, two, 0)
        sums = [jnp.sum(r["top"][h], axis=1, keepdims=True) for h in range(2)]
        mixed = jnp.where(first, r["acc"][0] / sums[0], r["acc"][1] / sums[1])
        r["mix"].at[qi][...] = mixed
        r["lse"].at[qi][...] = jnp.where(
            first, tops[0] + jnp.log(sums[0]), tops[1] + jnp.log(sums[1])
        )
        r["mixb"].at[qi][...] = mixed.astype(BF16).reshape(2, 128, 128)
        mix_copy(i, 1 - e, mix_over).start()
        pl.when(i > 0)(lambda: mix_copy(i, e, mix_here).start())
        return 0

    lax.fori_loop(0, 4, attend, 0)
    r["mixin"].at[z, e][...] = r["mixb"].at[z, e][...]

    for copy in came_out:
        copy.wait_recv()
    half = links.go(r["wo"].at[e], r["wo"].at[e], partner)
    for i in NEAR[1:]:
        gather_g.pass_on(i)
    for copy in came_feed:
        copy.wait_recv()
    for i in NEAR:
        gather_g.ready(i)
    w_down = r["w"][:, :, :, :, DOWN:OUT].reshape(1024, WIDE)

    def down_back(zz, _):
        back = mm(r["gg"].at[zz][...].reshape(256, 1024), w_down)
        r["score"].at[0, zz][...] = back[:, :256]
        r["score"].at[1, zz, :, :128][...] = back[:, 256:]
        return 0

    half.wait_recv()
    for i in range(4):
        mix_copy(i, 1 - e, mix_over).wait_recv()
        if i:
            mix_copy(i, e, mix_here).wait_recv()
    mixed = jnp.concatenate([r["mixin"][s // 2, s % 2] for s in range(8)], axis=1)
    hidden = r["x"][...].astype(F32) + jnp.concatenate(
        [mm(mixed, r["wo"][h].reshape(1024, 512)) for h in range(2)], axis=1
    )
    r2 = lax.rsqrt(jnp.mean(hidden * hidden, axis=-1, keepdims=True) + EPS)
    unit2 = hidden * r2
    r["hidden"][...] = hidden
    r["unit2"][...] = unit2
    r["r2"][...] = r2
    r["u2"].at[z, e][...] = unit2.astype(BF16)
    gather2 = Gather(r["u2"])
    gather2.start()
    lax.fori_loop(0, 4, down_back, 0)

    w_up = r["w"][:, :, :, :, GATE:DOWN].reshape(1024, 2 * WIDE)
    real = lax.broadcasted_iota(jnp.int32, (256, WIDE), 1) < SLICE
    scatter2, scatter_y = Scatter("e2"), Scatter("out")
    for at, i in enumerate(NEAR):
        if i:
            gather2.pass_on(i)
        gather2.ready(i)
        zz = lax.rem(z - i + 4, 4)
        sums = mm(r["u2"].at[zz][...].reshape(256, 1024), w_up)
        gate, up = sums[:, :WIDE], sums[:, WIDE:]
        sigmoid = 1.0 / (1.0 + jnp.exp(-gate))
        swish = gate * sigmoid
        back = jnp.concatenate(
            [r["score"].at[0, zz][...], r["score"].at[1, zz, :, :128][...]], axis=1
        )
        r["act"].at[zz][...] = jnp.where(real, swish * up, 0.0).astype(BF16)
        d_gate = back * up * sigmoid * (1.0 + gate * (1.0 - sigmoid))
        d_gate = jnp.where(real, d_gate, 0.0).astype(BF16)
        d_up = jnp.where(real, back * swish, 0.0).astype(BF16)
        r["dgu"].at[zz][...] = jnp.concatenate([d_gate, d_up], axis=1)
        scatter2.put(i, mt(r["dgu"].at[zz][...], w_up))
        if at:
            scatter2.send(NEAR[at - 1])
    scatter2.send(NEAR[3])

    gain_lane = SLICE

    def feed_grads(b, _):
        cols = pl.ds(pl.multiple_of(b * 256, 256), 256)
        units = r["u2"][:, :, :, cols].reshape(1024, 256)
        grads = tm(units, r["dgu"][...].reshape(1024, 2 * WIDE))
        weights = r["w"][pl.ds(b * 2, 2), :, :, :, GATE:DOWN].reshape(256, 2 * WIDE).astype(F32)
        gain = weights[:, gain_lane : gain_lane + 1]
        lane = lax.broadcasted_iota(jnp.int32, (256, 2 * WIDE), 1)
        keep = lax.rem(lane, WIDE) < SLICE
        weighed = jnp.sum(jnp.where(keep, weights * grads, 0.0), axis=1, keepdims=True) / gain
        blocks = pl.ds(b * 4, 4)
        r["gf"][blocks, :, : 2 * WIDE] = (grads * gain).astype(BF16).reshape(4, 64, 2 * WIDE)
        downs = tm(
            r["gg"][:, :, :, cols].reshape(1024, 256), r["act"][...].reshape(1024, WIDE)
        )
        lane = lax.broadcasted_iota(jnp.int32, (256, WIDE), 1)
        downs = jnp.where(lane == gain_lane, weighed, downs)
        r["gf"][blocks, :, 2 * WIDE :] = downs.astype(BF16).reshape(4, 64, WIDE)
        return 0

    lax.fori_loop(0, 4, feed_grads, 0)

    def down_out(i):
        zz = lax.rem(z - i + 4, 4)
        scatter_y.put(i, mt(r["act"].at[zz][...], w_down))

    e2 = scatter2.total()
    unit2 = r["unit2"][...]
    grad_hidden = r["g"][...].astype(F32) + r["r2"][...] * (
        e2 - unit2 * jnp.mean(e2 * unit2, axis=-1, keepdims=True)
    )
    r["gh"][...] = grad_hidden
    branch = grad_hidden.astype(BF16)
    r["db"].at[z, e][...] = branch
    d_mixed = mt(branch[:, :512], r["wo"][0].reshape(1024, 512)) + mt(
        branch[:, 512:], r["wo"][1].reshape(1024, 512)
    )
    for s in range(8):
        r["dmixb"][s // 2, s % 2] = d_mixed[:, s * 128 : (s + 1) * 128].astype(BF16)
    came_mix = []
    for i in NEAR:
        to = along_z(i)
        for to_e, peer in ((1 - e, other_core(to)), (e, to)):
            if i or peer is not to:
                src = r["dmixb"].at[to["z"], to_e]
                came_mix.append(links.go(src, r["dmix"].at[z, e], peer))
    r["dmix"].at[z, e][...] = r["dmixb"].at[z, e][...]

    def plane_sum(kept, landed):
        copies = []
        for n, (dx, dy) in enumerate(plane):
            to = in_plane(dx, dy)
            block = 4 * to["y"] + 2 * to["xh"] + to["xl"]
            copies.append(links.go(kept.at[block], landed.at[n], to))
        return copies

    came_gf = plane_sum(r["gf"], r["gfr"])
    gather_b = Gather(r["db"])
    gather_b.start()
    for at, i in enumerate(NEAR):
        down_out(i)
        if at:
            scatter_y.send(NEAR[at - 1])
    scatter_y.send(NEAR[3])
    for i in NEAR[1:]:
        gather_b.pass_on(i)

    for copy in came_mix:
        copy.wait_recv()
    d_kv = r["score"].at[0]
    d_kv[...] = jnp.zeros((8, 256, 256), F32)
    came_dkv = links.slots(4)

    def dkv_copy(zz):
        return links.make(r["dkvs"].at[zz], r["dkvr"].at[zz], across, came_dkv + zz)

    def give(zz):
        both = d_kv.at[2 * zz + 1 - xh][...].astype(BF16)
        r["dkvs"].at[zz, 0][...] = both[:, :128]
        r["dkvs"].at[zz, 1][...] = both[:, 128:]
        dkv_copy(zz).start()

    def attend_back(step, _):
        qi = 3 - step
        own, many = tiles_of(qi)
        queries = halves(r["q"].at[qi][...])
        grads = r["dmix"].at[qi][...].reshape(256, 128)
        product = grads.astype(F32) * r["mix"].at[qi][...]
        grads = halves(grads)
        dots = [jnp.sum(part, axis=1, keepdims=True) for part in halves(product)]
        lse = r["lse"].at[qi][...]
        logs = [lse[:, :1], lse[:, HD : HD + 1]]
        query_ids = r["idcol"].at[own][...]
        r["acc"][0] = jnp.zeros((256, 128), F32)

        def one(j, _):
            jz, jx = lax.div(j, 2), lax.rem(j, 2)
            keys, values = r["kv"].at[jz, jx, 0][...], r["kv"].at[jz, jx, 1][...]
            key_halves = halves(keys)
            seen = r["idrow"].at[j][...] <= query_ids
            dq, dk, dv = 0.0, 0.0, 0.0
            for h in range(2):
                score = jnp.where(seen, mt(queries[h], keys), -1e30)
                prob = jnp.exp(score - logs[h])
                d_score = (prob * (mt(grads[h], values) - dots[h])).astype(BF16)
                dv += tm(prob.astype(BF16), grads[h])
                dk += tm(d_score, queries[h])
                dq += mm(d_score, key_halves[h])
            r["acc"][0] += dq
            d_kv.at[j][...] += jnp.concatenate([dk, dv], axis=1)
            return 0

        lax.fori_loop(0, many, one, 0)
        r["dq"].at[qi][...] = r["acc"][0] * 0.125
        pl.when(step > 0)(lambda: give(qi + 1))
        return 0

    lax.fori_loop(0, 4, attend_back, 0)
    give(0)

    scatter1 = Scatter("e1")
    for at, i in enumerate(NEAR):
        zz = lax.rem(z - i + 4, 4)
        dkv_copy(zz).wait_recv()
        cosine, sine = r["cos"].at[zz][...], -r["sin"].at[zz][...]
        d_tile = d_kv.at[2 * zz + xh][...]
        d_key = d_tile[:, :128] + r["dkvr"].at[zz, 0][...].astype(F32)
        d_value = d_tile[:, 128:] + r["dkvr"].at[zz, 1][...].astype(F32)
        r["dqkv"].at[zz][...] = jnp.concatenate(
            [
                turn(r["dq"].at[zz][...], cosine, sine).astype(BF16),
                turn(d_key, cosine, sine).astype(BF16),
                d_value.astype(BF16),
            ],
            axis=1,
        )
        scatter1.put(i, mt(r["dqkv"].at[zz][...], w_qkv))
        if at:
            scatter1.send(NEAR[at - 1])
    scatter1.send(NEAR[3])

    def qkv_grads(b, _):
        cols = pl.ds(pl.multiple_of(b * 256, 256), 256)
        units = r["u1"][:, :, :, cols].reshape(1024, 256)
        grads = tm(units, r["dqkv"][...].reshape(1024, 384))
        weights = r["w"][pl.ds(b * 2, 2), :, :, :, :GATE].reshape(256, 384).astype(F32)
        at = GATE + WIDE
        ups = r["w"][pl.ds(b * 2, 2), :, :, :, at + 256 : at + WIDE].reshape(256, 128)
        gain = ups.astype(F32)[:, gain_lane - 256 : gain_lane - 255]
        weighed = jnp.sum(weights * grads, axis=1, keepdims=True) / gain
        blocks = pl.ds(b * 4, 4)
        r["gq"][blocks, :, :384] = (grads * gain).astype(BF16).reshape(4, 64, 384)
        r["gq"][blocks, :, 384:] = (
            jnp.broadcast_to(weighed, (256, 128)).astype(BF16).reshape(4, 64, 128)
        )
        return 0

    lax.fori_loop(0, 4, qkv_grads, 0)
    came_gq = plane_sum(r["gq"], r["gqr"])

    for i in NEAR:
        gather_b.ready(i)
    go = tm(
        r["mixb"][...].reshape(1024, 128), r["db"][...].reshape(1024, 1024)
    ).astype(BF16)
    for j in range(2):
        for k in range(8):
            r["go"][j, k] = go[j * 64 : (j + 1) * 64, k * 128 : (k + 1) * 128]
    came_go = []
    for n, d in enumerate(plane):
        to = in_plane(*d)
        src = r["go"].at[to["xh"], to["xl"] * 4 + to["y"]]
        came_go.append(links.go(src, r["gor"].at[n], to))

    def add_up(copies, landed, mine):
        result = mine.astype(F32)
        for n, copy in enumerate(copies):
            copy.wait_recv()
            result = result + landed[n].astype(F32)
        return result.astype(BF16)

    def hand_out(src, dst, slot, self_is, place):
        first_send = links.slots(8)
        first_land = links.slots(8)
        copies = []
        for n, d in enumerate(groups):
            to = place(group(*d))
            copies.append(links.make(src, dst.at[slot], to, first_send + n, first_land + slot))
        near = pltpu.make_async_copy(src, dst.at[slot], links.near.at[links.count_near])
        links.count_near += 1
        pl.when(self_is)(near.start)
        pl.when(jnp.logical_not(self_is))(copies[0].start)
        for copy in copies[1:]:
            copy.start()

        def finish():
            for s in range(8):
                landing = links.make(src, dst.at[s], partner, first_send, first_land + s)
                mine = jnp.logical_and(self_is, slot == s)
                pl.when(jnp.logical_not(mine))(landing.wait_recv)
            pl.when(self_is)(near.wait)
            pl.when(jnp.logical_not(self_is))(copies[0].wait_send)
            for copy in copies[1:]:
                copy.wait_send()

        return finish

    own_block = 4 * y + x
    by_row = lambda at: {**at, "z": y, "e": xl}
    by_head = lambda at: {**at, "xh": e, "e": xh}
    r["sf"][...] = add_up(came_gf, r["gfr"], r["gf"].at[own_block][...])
    done_f = hand_out(r["sf"], r["ff"], z * 2 + e, fin_self, by_row)
    r["y"][...] = (r["hidden"][...] + scatter_y.total()).astype(BF16)
    r["sq"][...] = add_up(came_gq, r["gqr"], r["gq"].at[own_block][...])
    done_q = hand_out(r["sq"], r["fq"], z * 2 + e, fin_self, by_row)
    r["so"][...] = add_up(came_go, r["gor"], r["go"].at[xh, grp][...])
    done_o = hand_out(r["so"], r["fo"], grp, out_self, by_head)
    e1 = scatter1.total()
    rows = r["x"][...].astype(F32)
    r1 = lax.rsqrt(jnp.mean(rows * rows, axis=-1, keepdims=True) + EPS)
    unit1 = rows * r1
    r["gx"][...] = r["gh"][...] + r1 * (
        e1 - unit1 * jnp.mean(e1 * unit1, axis=-1, keepdims=True)
    )
    done_f()
    done_q()
    done_o()
    for i in range(4):
        mix_copy(i, 1 - e, mix_over).wait_send()
        if i:
            mix_copy(i, e, mix_here).wait_send()
        dkv_copy(i).wait_send()
    for copy in links.started:
        copy.wait_send()
    assert links.count <= COPIES and links.count_near <= 8


def rope_tables():
    positions = np.arange(2048, dtype=np.float32)[:, None]
    frequency = np.float32(10000.0) ** (
        np.float32(-2.0) * np.arange(32, dtype=np.float32) / np.float32(64)
    )
    angles = positions * frequency.astype(np.float32)[None, :]
    cosine, sine = np.cos(angles), np.sin(angles)
    cosines = np.concatenate([cosine] * 4, axis=1)
    sines = np.concatenate([-sine, sine, -sine, sine], axis=1)
    shape = (4, 2, 256, 128)
    return cosines.astype(np.float32).reshape(shape), sines.astype(np.float32).reshape(shape)


def per_device(
    tokens,
    blocks,
    w_query,
    w_key,
    w_value,
    w_out,
    w_gate,
    w_up,
    w_down,
    norm_attn,
    norm_mlp,
    cotangent,
):
    gain_attn = norm_attn.astype(F32)[:, None]
    gain_mlp = norm_mlp.astype(F32)[:, None]
    fill = WIDE - SLICE

    def heads(w):
        return (w.astype(F32) * gain_attn).reshape(8, 8, 128)

    def units(w, extra):
        last = jnp.pad(extra, ((0, 0), (0, fill - 1)))[:, None, :]
        return jnp.concatenate(
            [w.reshape(8, 8, SLICE), jnp.broadcast_to(last, (8, 8, fill))], axis=-1
        )

    slices = jnp.concatenate(
        [
            heads(w_query),
            heads(w_key),
            heads(w_value),
            units(w_gate.astype(F32) * gain_mlp, gain_mlp),
            units(w_up.astype(F32) * gain_mlp, gain_attn),
            units(w_down.T.astype(F32), jnp.zeros_like(gain_attn)),
        ],
        axis=-1,
    )
    slices = slices.reshape(8, 4, 2, OUT).transpose(2, 0, 1, 3).reshape(2, 8, 4 * OUT)
    outs = w_out.astype(F32).reshape(8, 2, 512).transpose(1, 0, 2)
    source = jnp.concatenate([slices, outs], axis=-1)
    cosines, sines = rope_tables()
    vmem = pl.BlockSpec(memory_space=pltpu.VMEM)
    anywhere = pl.BlockSpec(memory_space=pl.ANY)
    y, gx, ff, fq, fo = pl.pallas_call(
        kernel,
        out_shape=[jax.ShapeDtypeStruct(*spec) for spec in OUTPUTS.values()],
        in_specs=[vmem] * 5 + [anywhere] * 2,
        out_specs=[vmem] * len(OUTPUTS),
        scratch_shapes=[pltpu.VMEM(*spec) for spec in HELD.values()]
        + [
            pltpu.SemaphoreType.DMA((COPIES,)),
            pltpu.SemaphoreType.DMA((COPIES,)),
            pltpu.SemaphoreType.DMA((8,)),
        ],
        compiler_params=pltpu.CompilerParams(
            collective_id=0, has_side_effects=True, vmem_limit_bytes=63 * 2**20
        ),
    )(
        tokens[0],
        cotangent[0],
        source,
        blocks.reshape(8, 1, 256),
        blocks.reshape(8, 256, 1),
        jnp.asarray(cosines),
        jnp.asarray(sines),
    )

    def rows(part):
        return part.astype(F32).transpose(1, 0, 2).reshape(64, -1)

    return (
        y[None],
        gx[None],
        rows(fq[:, :, :128]),
        rows(fq[:, :, 128:256]),
        rows(fq[:, :, 256:384]),
        rows(fo),
        rows(ff[:, :, :SLICE]),
        rows(ff[:, :, WIDE : WIDE + SLICE]),
        rows(ff[:, :, 2 * WIDE : 2 * WIDE + SLICE]).T,
        jnp.sum(fq[:, :, 384].astype(F32), axis=0),
        jnp.sum(ff[:, :, 2 * WIDE + SLICE].astype(F32), axis=0),
    )


def solution(mesh):
    both = ("grp", "ctx")
    row = P(both, None)
    tokens = P("grp", "ctx", None)
    shard = P("ctx", None)
    return jax.shard_map(
        per_device,
        mesh=mesh,
        in_specs=(
            tokens,
            P("grp", None),
            *[row] * 6,
            P(None, both),
            P(both),
            P(both),
            tokens,
        ),
        out_specs=(tokens, tokens, *[shard] * 6, P(None, "ctx"), P("ctx"), P("ctx")),
        check_vma=False,
    )
```

```python
import functools

import jax
import jax.numpy as jnp
import numpy as np
from jax import lax
from jax.experimental import pallas as pl
from jax.experimental.pallas import tpu as pltpu
from jax.sharding import PartitionSpec as P

MESH = pl.DeviceIdType.MESH
F32 = jnp.float32
BF16 = jnp.bfloat16
EPS = 1e-05
HD = 64
SLICE = 352
WIDE = 384
QKV, GATE, DOWN, OUT = 0, 384, 1152, 1536
NEAR = (0, 1, 3, 2)


def mm(left, right):
    return jnp.dot(left, right, preferred_element_type=F32)


def mt(left, right):
    return lax.dot_general(left, right, (((1,), (1,)), ((), ())), preferred_element_type=F32)


def tm(left, right):
    return lax.dot_general(left, right, (((0,), (0,)), ((), ())), preferred_element_type=F32)


def turn(values, cosine, sine):
    lane = lax.broadcasted_iota(jnp.int32, values.shape, 1)
    ahead = pltpu.roll(values, 96, 1)
    behind = pltpu.roll(values, 32, 1)
    return values * cosine + jnp.where(lax.rem(lane, 64) < 32, ahead, behind) * sine


HELD = {
    "pair": ((16, 6656), F32),
    "wz": ((4, 16, 2048), BF16),
    "wrow": ((4, 16, 2048), BF16),
    "w": ((2, 4, 4, 2, 16, 1536), BF16),
    "wo": ((2, 2, 4, 4, 2, 16, 512), BF16),
    "u1": ((4, 2, 128, 1024), BF16),
    "gg": ((4, 2, 128, 1024), BF16),
    "u2": ((4, 2, 128, 1024), BF16),
    "db": ((4, 2, 128, 1024), BF16),
    "cos": ((4, 256, 128), F32),
    "sin": ((4, 256, 128), F32),
    "q": ((4, 256, 128), BF16),
    "kv": ((4, 2, 2, 256, 128), BF16),
    "score": ((2, 8, 256, 256), F32),
    "top": ((2, 256, 128), F32),
    "acc": ((2, 256, 128), F32),
    "mix": ((4, 256, 128), F32),
    "mixb": ((4, 2, 128, 128), BF16),
    "mixin": ((4, 2, 128, 128), BF16),
    "lse": ((4, 256, 128), F32),
    "hidden": ((128, 1024), F32),
    "unit2": ((128, 1024), F32),
    "r2": ((128, 1), F32),
    "dgu": ((4, 256, 2 * WIDE), BF16),
    "act": ((4, 256, WIDE), BF16),
    "gh": ((128, 1024), F32),
    "dmixb": ((4, 2, 128, 128), BF16),
    "dmix": ((4, 2, 128, 128), BF16),
    "dq": ((4, 256, 128), F32),
    "dkvs": ((4, 2, 256, 128), BF16),
    "dkvr": ((4, 2, 256, 128), BF16),
    "dqkv": ((4, 256, 384), BF16),
    "go": ((2, 8, 64, 128), BF16),
    "gor": ((16, 64, 128), BF16),
    "so": ((64, 128), BF16),
}
for kind in ("e2", "out", "e1"):
    HELD[kind + "p"] = ((4, 2, 128, 1024), BF16)
    HELD[kind + "d"] = ((4, 128, 1024), BF16)
    HELD[kind + "r"] = ((3, 128, 1024), BF16)
SPLIT = {"f": (640, 512), "q": (256, 256)}
for kind, (by_x, by_y) in SPLIT.items():
    HELD["g" + kind] = ((4, 4, 4, 16, by_x + by_y), BF16)
    HELD["s" + kind] = ((4, 16, by_x + by_y), BF16)
    HELD["z" + kind] = ((4, 16, by_x + by_y), BF16)
    for axis, width in (("x", by_x), ("y", by_y)):
        HELD["r1" + axis + kind] = ((3, 4, 4, 16, width), BF16)
        HELD["r2" + axis + kind] = ((3, 4, 16, width), BF16)

INPUTS = ("x", "g", "wsrc", "ids", "cosines", "sines")
OUTPUTS = {
    "y": ((128, 1024), BF16),
    "gx": ((128, 1024), F32),
    "ff": ((4, 2, 4, 16, 1152), BF16),
    "fq": ((4, 2, 4, 16, 512), BF16),
    "fo": ((8, 64, 128), BF16),
}
COPIES = 320


def device(at):
    return (at["xl"] * 4 + at["y"], at["z"] * 4 + at["xh"] * 2 + at["e"])


class Links:
    def __init__(self, send, recv, near):
        self.send, self.recv, self.near = send, recv, near
        self.count = self.count_near = 0
        self.started = []

    def slots(self, many):
        self.count += many
        return self.count - many

    def make(self, src, dst, peer, slot=None, landing=None):
        slot = self.slots(1) if slot is None else slot
        landing = slot if landing is None else landing
        return pltpu.make_async_remote_copy(
            src_ref=src,
            dst_ref=dst,
            send_sem=self.send.at[slot],
            recv_sem=self.recv.at[landing],
            device_id=device(peer),
            device_id_type=MESH,
        )

    def go(self, src, dst, peer):
        copy = self.make(src, dst, peer)
        copy.start()
        self.started.append(copy)
        return copy

    def here(self, src, dst):
        copy = pltpu.make_async_copy(src, dst, self.near.at[self.count_near])
        self.count_near += 1
        copy.start()
        return copy


def kernel(*refs):
    n_in, n_out = len(INPUTS), len(OUTPUTS)
    r = dict(zip(INPUTS, refs[:n_in]))
    r.update(zip(OUTPUTS, refs[n_in : n_in + n_out]))
    r.update(zip(HELD, refs[n_in + n_out : n_in + n_out + len(HELD)]))
    links = Links(*refs[n_in + n_out + len(HELD) :])
    grp, ctx = lax.axis_index("grp"), lax.axis_index("ctx")
    me = {
        "xl": lax.div(grp, 4),
        "y": lax.rem(grp, 4),
        "z": lax.div(ctx, 4),
        "xh": lax.rem(lax.div(ctx, 2), 2),
        "e": lax.rem(ctx, 2),
    }
    xl, y, z, xh, e = (me[k] for k in ("xl", "y", "z", "xh", "e"))
    x = xh * 2 + xl

    def other_core(at):
        return {**at, "e": 1 - at["e"]}

    def along_z(by):
        return {**me, "z": lax.rem(z + by + 4, 4)}

    def in_plane(dx, dy):
        to = lax.rem(x + dx, 4)
        return {**me, "xl": lax.rem(to, 2), "xh": lax.div(to, 2), "y": lax.rem(y + dy, 4)}

    def group(dxl, dy):
        return {**me, "xl": lax.rem(xl + dxl, 2), "y": lax.rem(y + dy, 4)}

    partner = other_core(me)
    across = in_plane(2, 0)
    plane = sorted(
        ((dx, dy) for dx in range(4) for dy in range(4) if dx or dy),
        key=lambda d: -min(d[0], 4 - d[0]) - min(d[1], 4 - d[1]),
    )
    groups = [(dxl, dy) for dxl in range(2) for dy in range(4)]

    tables = [
        links.here(r["cosines"].at[:, xh], r["cos"]),
        links.here(r["sines"].at[:, xh], r["sin"]),
    ]
    rows = r["x"][...].astype(F32)
    r1 = lax.rsqrt(jnp.mean(rows * rows, axis=-1, keepdims=True) + EPS)
    r["u1"].at[z, e][...] = (rows * r1).astype(BF16)
    r["gg"].at[z, e][...] = r["g"][...]
    own_rows = pl.ds(pl.multiple_of(e * 8, 8), 8)
    r["pair"][own_rows, :] = r["wsrc"].at[e][...]

    sem = pltpu.get_barrier_semaphore()

    def greet(peer):
        pl.semaphore_signal(sem, inc=1, device_id=device(peer), device_id_type=MESH)

    row_self = xl == e
    head_self = xh == e
    peers = [partner] + [along_z(i) for i in (1, 2, 3)] + [other_core(along_z(i)) for i in (1, 2, 3)]
    peers += [in_plane(*d) for d in plane]
    for peer in peers:
        greet(peer)
    for d in groups:
        source = group(*d)
        for own, change in ((row_self, {"xl": e}), (head_self, {"xh": e, "e": xh})):
            if "xl" in change:
                source = {**me, **change, "y": lax.rem(y + d[1], 4), "e": lax.rem(e + d[0], 2)}
            else:
                source = {**group(*d), **change}
            if d != (0, 0):
                greet(source)
            else:
                pl.when(jnp.logical_not(own))(functools.partial(greet, source))
    extra = 16 - row_self.astype(jnp.int32) - head_self.astype(jnp.int32)
    pl.semaphore_wait(sem, len(peers) + extra)

    class Gather:
        def __init__(self, buf):
            self.buf = buf
            self.out = {0: None}
            self.over = {}

        def start(self):
            mine = self.buf.at[z, e]
            for i in NEAR[1:]:
                self.out[i] = links.go(mine, mine, along_z(i))
            self.over[0] = links.go(mine, mine, partner)

        def pass_on(self, i):
            self.out[i].wait_recv()
            block = self.buf.at[lax.rem(z - i + 4, 4), e]
            self.over[i] = links.go(block, block, partner)

        def ready(self, i):
            self.over[i].wait_recv()

    class Scatter:
        def __init__(self, kind):
            self.p, self.d, self.r = (r[kind + k] for k in "pdr")
            self.over, self.out = {}, {}

        def put(self, i, value):
            zz = lax.rem(z - i + 4, 4)
            self.p.at[zz][...] = value.astype(BF16).reshape(2, 128, 1024)
            self.over[i] = links.go(self.p.at[zz, 1 - e], self.d.at[zz], partner)

        def send(self, i):
            zz = lax.rem(z - i + 4, 4)
            if i:
                self.over[i].wait_recv()
                mine = self.p.at[zz, e]
                mine[...] = (mine[...].astype(F32) + self.d.at[zz][...].astype(F32)).astype(BF16)
                self.out[i] = links.go(mine, self.r.at[i - 1], along_z(-i))

        def total(self):
            self.over[0].wait_recv()
            result = self.p.at[z, e][...].astype(F32) + self.d.at[z][...].astype(F32)
            for i in NEAR[1:]:
                self.out[i].wait_recv()
                result = result + self.r[i - 1].astype(F32)
            return result

    class Spread:
        def __init__(self, buf, along_x, along_y):
            self.own = [buf.at[xl, y, :, xh, :, along_x], buf.at[xl, y, :, xh, :, along_y]]
            self.line = [buf.at[:, y, :, :, :, along_x], buf.at[xl, :, :, xh, :, along_y]]

        def start(self):
            self.came = []
            for d in (2, 1, 3):
                self.came.append(links.go(self.own[0], self.own[0], in_plane(d, 0)))
                self.came.append(links.go(self.own[1], self.own[1], in_plane(0, d)))

        def pass_on(self):
            self.wait()
            self.came = []
            for d in (2, 1, 3):
                self.came.append(links.go(self.line[0], self.line[0], in_plane(0, d)))
                self.came.append(links.go(self.line[1], self.line[1], in_plane(d, 0)))

        def wait(self):
            for copy in self.came:
                copy.wait_recv()

    class PlaneSum:
        def __init__(self, kind):
            self.by_x = pl.ds(0, SPLIT[kind][0])
            self.by_y = pl.ds(*SPLIT[kind])
            self.g, self.s, self.z = (r[k + kind] for k in "gsz")
            self.one = r["r1x" + kind], r["r1y" + kind]
            self.two = r["r2x" + kind], r["r2y" + kind]
            self.dst = r["f" + kind]

        def start(self):
            self.came = []
            for d in (2, 1, 3):
                there = self.g.at[:, lax.rem(x + d, 4), :, :, self.by_x]
                self.came.append(links.go(there, self.one[0].at[d - 1], in_plane(d, 0)))
                there = self.g.at[:, :, lax.rem(y + d, 4), :, self.by_y]
                self.came.append(links.go(there, self.one[1].at[d - 1], in_plane(0, d)))

        def add(self, mine, landed):
            result = mine[...].astype(F32)
            for d in range(3):
                result = result + landed[d].astype(F32)
            return result.astype(BF16)

        def middle(self):
            for copy in self.came:
                copy.wait_recv()
            mine = self.g.at[:, x, :, :, self.by_x]
            mine[...] = self.add(mine, self.one[0])
            mine = self.g.at[:, :, y, :, self.by_y]
            mine[...] = self.add(mine, self.one[1])
            self.came = []
            for d in (2, 1, 3):
                there = self.g.at[:, x, lax.rem(y + d, 4), :, self.by_x]
                self.came.append(links.go(there, self.two[0].at[d - 1], in_plane(0, d)))
                there = self.g.at[:, lax.rem(x + d, 4), y, :, self.by_y]
                self.came.append(links.go(there, self.two[1].at[d - 1], in_plane(d, 0)))

        def last(self):
            for copy in self.came:
                copy.wait_recv()
            self.s[:, :, self.by_x] = self.add(self.g.at[:, x, y, :, self.by_x], self.two[0])
            self.s[:, :, self.by_y] = self.add(self.g.at[:, x, y, :, self.by_y], self.two[1])
            self.came = []
            for i in NEAR[1:]:
                to = along_z(i)
                self.came.append(links.go(self.s.at[to["z"]], self.z.at[z], to))
            self.z.at[z][...] = self.s.at[z][...]

        def out(self):
            for copy in self.came:
                copy.wait_recv()
            return hand_out(self.z, self.dst.at[y, e], y * 2 + e, row_self, lambda at: {**at, "e": xl})

    def hand_out(src, dst, slot, self_is, place):
        first_send = links.slots(8)
        first_land = links.slots(8)
        copies = [
            links.make(src, dst, place(group(*d)), first_send + n, first_land + slot)
            for n, d in enumerate(groups)
        ]
        near = pltpu.make_async_copy(src, dst, links.near.at[links.count_near])
        links.count_near += 1
        for copy in copies[1:]:
            copy.start()
        pl.when(self_is)(near.start)
        pl.when(jnp.logical_not(self_is))(copies[0].start)

        def finish():
            for s in range(8):
                landing = links.make(src, dst, partner, first_send, first_land + s)
                mine = jnp.logical_and(self_is, slot == s)
                pl.when(jnp.logical_not(mine))(landing.wait_recv)
            pl.when(self_is)(near.wait)
            pl.when(jnp.logical_not(self_is))(copies[0].wait_send)
            for copy in copies[1:]:
                copy.wait_send()

        return finish

    swap = links.go(r["wsrc"].at[1 - e], r["pair"].at[own_rows, :], partner)
    swap.wait_recv()
    for zz in range(4):
        r["wz"][zz, :, :OUT] = r["pair"][:, zz * OUT : (zz + 1) * OUT].astype(BF16)
        r["wz"][zz, :, OUT:] = r["pair"][:, 4 * OUT :].astype(BF16)
    column = [
        links.go(r["wz"].at[lax.rem(z + i, 4)], r["wrow"].at[z], along_z(i)) for i in (2, 1, 3)
    ]
    gather1 = Gather(r["u1"])
    gather1.start()
    r["wrow"].at[z][...] = r["wz"].at[z][...]
    for copy in column:
        copy.wait_recv()
    part = r["wrow"].at[:, :, pl.ds(QKV, GATE)]
    there = r["w"].at[xl, y, :, xh, :, pl.ds(QKV, GATE)]
    came_qkv = [links.go(part, there, in_plane(*d)) for d in plane]
    r["w"].at[xl, y, :, xh][...] = r["wrow"][:, :, :OUT]
    r["wo"].at[e, xl, y, :, xh][...] = r["wrow"][:, :, OUT:]
    spread_out = Spread(r["wo"].at[e], pl.ds(0, 256), pl.ds(256, 256))
    spread_feed = Spread(r["w"], pl.ds(GATE, 640), pl.ds(GATE + 640, 512))
    spread_out.start()
    for i in NEAR[1:]:
        gather1.pass_on(i)
    gather_g = Gather(r["gg"])
    gather_g.start()
    for copy in tables:
        copy.wait()
    for i in NEAR:
        gather1.ready(i)
    for copy in came_qkv:
        copy.wait_recv()

    w_qkv = r["w"][:, :, :, :, :, QKV:GATE].reshape(1024, GATE - QKV)
    came_kv = []
    for zz in range(4):
        qkv = mm(r["u1"][zz].reshape(256, 1024), w_qkv)
        cosine, sine = r["cos"][zz], r["sin"][zz]
        r["kv"].at[zz, xh, 0][...] = turn(qkv[:, 128:256], cosine, sine).astype(BF16)
        r["kv"].at[zz, xh, 1][...] = qkv[:, 256:].astype(BF16)
        tile = r["kv"].at[zz, xh]
        came_kv.append(links.go(tile, tile, across))
        r["q"][zz] = (turn(qkv[:, :128], cosine, sine).astype(BF16) * 0.125).astype(BF16)
    spread_out.pass_on()
    spread_feed.start()

    first = lax.broadcasted_iota(jnp.int32, (256, 128), 1) < HD

    def halves(pair):
        zero = jnp.zeros_like(pair)
        return jnp.where(first, pair, zero), jnp.where(first, zero, pair)

    def tiles_of(qi):
        own = 2 * qi + xh
        return own, jnp.minimum(own + 2, 8)

    def ids_of(tile):
        row = r["ids"].at[tile][...].astype(F32)
        return jnp.broadcast_to(row, (128, 256)).T[:, :1], row

    mix_over = links.slots(4)
    mix_here = links.slots(4)

    def mix_copy(qi, at_e, base, source=z):
        to = {**me, "z": qi, "e": at_e}
        return links.make(
            r["mixb"].at[qi, at_e], r["mixin"].at[z, e], to, base + qi, base + source
        )

    def attend(qi):
        own, many = tiles_of(qi)
        queries = halves(r["q"].at[qi][...])
        query_ids, _ = ids_of(own)
        r["top"][...] = jnp.full((2, 256, 128), -3e38, F32)

        def one(j, _):
            keys = r["kv"].at[lax.div(j, 2), lax.rem(j, 2), 0][...]
            seen = ids_of(j)[1] <= query_ids
            for h in range(2):
                score = jnp.where(seen, mt(queries[h], keys), -1e30)
                r["score"].at[h, j][...] = score
                r["top"][h] = jnp.maximum(
                    r["top"][h], jnp.maximum(score[:, :128], score[:, 128:])
                )
            return 0

        lax.fori_loop(0, many, one, 0)
        tops = [jnp.max(r["top"][h], axis=1, keepdims=True) for h in range(2)]
        r["top"][...] = jnp.zeros((2, 256, 128), F32)
        r["acc"][...] = jnp.zeros((2, 256, 128), F32)

        def two(j, _):
            values = r["kv"].at[lax.div(j, 2), lax.rem(j, 2), 1][...]
            for h in range(2):
                weight = jnp.exp(r["score"].at[h, j][...] - tops[h])
                r["top"][h] += weight[:, :128] + weight[:, 128:]
                r["acc"][h] += mm(weight.astype(BF16), values)
            return 0

        lax.fori_loop(0, many, two, 0)
        sums = [jnp.sum(r["top"][h], axis=1, keepdims=True) for h in range(2)]
        mixed = jnp.where(first, r["acc"][0] / sums[0], r["acc"][1] / sums[1])
        r["mix"].at[qi][...] = mixed
        r["lse"].at[qi][...] = jnp.where(
            first, tops[0] + jnp.log(sums[0]), tops[1] + jnp.log(sums[1])
        )
        r["mixb"].at[qi][...] = mixed.astype(BF16).reshape(2, 128, 128)
        mix_copy(qi, 1 - e, mix_over).start()
        pl.when(z != qi)(lambda: mix_copy(qi, e, mix_here).start())

    came_kv[0].wait_recv()
    for qi in range(4):
        if qi < 3:
            came_kv[qi + 1].wait_recv()
        attend(qi)
        if qi == 1:
            for i in NEAR[1:]:
                gather_g.pass_on(i)
            spread_feed.pass_on()
    r["mixin"].at[z, e][...] = r["mixb"].at[z, e][...]

    spread_out.wait()
    half = links.go(r["wo"].at[e], r["wo"].at[e], partner)
    for zz in range(4):
        mix_copy(zz, 1 - e, mix_over, zz).wait_recv()
        pl.when(z != zz)(lambda: mix_copy(zz, e, mix_here, zz).wait_recv())
    half.wait_recv()
    mixed = jnp.concatenate([r["mixin"][s // 2, s % 2] for s in range(8)], axis=1)
    hidden = r["x"][...].astype(F32) + jnp.concatenate(
        [mm(mixed, r["wo"][h].reshape(1024, 512)) for h in range(2)], axis=1
    )
    r2 = lax.rsqrt(jnp.mean(hidden * hidden, axis=-1, keepdims=True) + EPS)
    unit2 = hidden * r2
    r["hidden"][...] = hidden
    r["unit2"][...] = unit2
    r["r2"][...] = r2
    r["u2"].at[z, e][...] = unit2.astype(BF16)
    gather2 = Gather(r["u2"])
    gather2.start()
    spread_feed.wait()
    for i in NEAR:
        gather_g.ready(i)
    w_down = r["w"][:, :, :, :, :, DOWN:OUT].reshape(1024, WIDE)

    def down_back(zz, _):
        back = mm(r["gg"].at[zz][...].reshape(256, 1024), w_down)
        r["score"].at[0, zz][...] = back[:, :256]
        r["score"].at[1, zz, :, :128][...] = back[:, 256:]
        return 0

    lax.fori_loop(0, 4, down_back, 0)

    w_up = r["w"][:, :, :, :, :, GATE:DOWN].reshape(1024, 2 * WIDE)
    real = lax.broadcasted_iota(jnp.int32, (256, WIDE), 1) < SLICE
    scatter2, scatter_y = Scatter("e2"), Scatter("out")
    for at, i in enumerate(NEAR):
        if i:
            gather2.pass_on(i)
        gather2.ready(i)
        zz = lax.rem(z - i + 4, 4)
        sums = mm(r["u2"].at[zz][...].reshape(256, 1024), w_up)
        gate, up = sums[:, :WIDE], sums[:, WIDE:]
        sigmoid = 1.0 / (1.0 + jnp.exp(-gate))
        swish = gate * sigmoid
        back = jnp.concatenate(
            [r["score"].at[0, zz][...], r["score"].at[1, zz, :, :128][...]], axis=1
        )
        r["act"].at[zz][...] = jnp.where(real, swish * up, 0.0).astype(BF16)
        d_gate = back * up * sigmoid * (1.0 + gate * (1.0 - sigmoid))
        d_gate = jnp.where(real, d_gate, 0.0).astype(BF16)
        d_up = jnp.where(real, back * swish, 0.0).astype(BF16)
        r["dgu"].at[zz][...] = jnp.concatenate([d_gate, d_up], axis=1)
        scatter2.put(i, mt(r["dgu"].at[zz][...], w_up))
        if at:
            scatter2.send(NEAR[at - 1])
    scatter2.send(NEAR[3])

    gain_lane = SLICE

    def feed_grads(b, _):
        cols = pl.ds(pl.multiple_of(b * 256, 256), 256)
        units = r["u2"][:, :, :, cols].reshape(1024, 256)
        grads = tm(units, r["dgu"][...].reshape(1024, 2 * WIDE))
        weights = r["w"].at[lax.div(b, 2), pl.ds(2 * lax.rem(b, 2), 2), :, :, :, GATE:DOWN]
        weights = weights[...].reshape(256, 2 * WIDE).astype(F32)
        gain = weights[:, gain_lane : gain_lane + 1]
        lane = lax.broadcasted_iota(jnp.int32, (256, 2 * WIDE), 1)
        keep = lax.rem(lane, WIDE) < SLICE
        weighed = jnp.sum(jnp.where(keep, weights * grads, 0.0), axis=1, keepdims=True) / gain
        shape = (4, 4, 16, -1)
        r["gf"].at[b, :, :, :, : 2 * WIDE][...] = (grads * gain).astype(BF16).reshape(shape)
        downs = tm(
            r["gg"][:, :, :, cols].reshape(1024, 256), r["act"][...].reshape(1024, WIDE)
        )
        lane = lax.broadcasted_iota(jnp.int32, (256, WIDE), 1)
        downs = jnp.where(lane == gain_lane, weighed, downs)
        r["gf"].at[b, :, :, :, 2 * WIDE :][...] = downs.astype(BF16).reshape(shape)
        return 0

    lax.fori_loop(0, 4, feed_grads, 0)
    sum_f = PlaneSum("f")
    sum_f.start()

    def down_out(i):
        zz = lax.rem(z - i + 4, 4)
        scatter_y.put(i, mt(r["act"].at[zz][...], w_down))

    e2 = scatter2.total()
    unit2 = r["unit2"][...]
    grad_hidden = r["g"][...].astype(F32) + r["r2"][...] * (
        e2 - unit2 * jnp.mean(e2 * unit2, axis=-1, keepdims=True)
    )
    r["gh"][...] = grad_hidden
    branch = grad_hidden.astype(BF16)
    r["db"].at[z, e][...] = branch
    d_mixed = mt(branch[:, :512], r["wo"][0].reshape(1024, 512)) + mt(
        branch[:, 512:], r["wo"][1].reshape(1024, 512)
    )
    for s in range(8):
        r["dmixb"][s // 2, s % 2] = d_mixed[:, s * 128 : (s + 1) * 128].astype(BF16)
    came_mix = []
    for i in NEAR:
        to = along_z(i)
        for to_e, peer in ((1 - e, other_core(to)), (e, to)):
            if i or peer is not to:
                src = r["dmixb"].at[to["z"], to_e]
                came_mix.append(links.go(src, r["dmix"].at[z, e], peer))
    r["dmix"].at[z, e][...] = r["dmixb"].at[z, e][...]

    gather_b = Gather(r["db"])
    gather_b.start()
    for at, i in enumerate(NEAR):
        down_out(i)
        if at:
            scatter_y.send(NEAR[at - 1])
    scatter_y.send(NEAR[3])
    sum_f.middle()

    def out_grads():
        grads = tm(r["mixb"][...].reshape(1024, 128), r["db"][...].reshape(1024, 1024))
        grads = grads.astype(BF16)
        for j in range(2):
            for k in range(8):
                r["go"][j, k] = grads[j * 64 : (j + 1) * 64, k * 128 : (k + 1) * 128]
        came = []
        for n, d in enumerate(plane):
            to = in_plane(*d)
            src = r["go"].at[to["xh"], to["xl"] * 4 + to["y"]]
            came.append(links.go(src, r["gor"].at[n], to))
        return came

    for copy in came_mix:
        copy.wait_recv()
    d_kv = r["score"].at[0]
    d_kv[...] = jnp.zeros((8, 256, 256), F32)
    came_dkv = links.slots(4)

    def dkv_copy(zz):
        return links.make(r["dkvs"].at[zz], r["dkvr"].at[zz], across, came_dkv + zz)

    def give(zz):
        both = d_kv.at[2 * zz + 1 - xh][...].astype(BF16)
        r["dkvs"].at[zz, 0][...] = both[:, :128]
        r["dkvs"].at[zz, 1][...] = both[:, 128:]
        dkv_copy(zz).start()

    def attend_back(qi):
        own, many = tiles_of(qi)
        queries = halves(r["q"].at[qi][...])
        grads = r["dmix"].at[qi][...].reshape(256, 128)
        product = grads.astype(F32) * r["mix"].at[qi][...]
        grads = halves(grads)
        dots = [jnp.sum(part, axis=1, keepdims=True) for part in halves(product)]
        lse = r["lse"].at[qi][...]
        logs = [lse[:, :1], lse[:, HD : HD + 1]]
        query_ids, _ = ids_of(own)
        r["acc"][0] = jnp.zeros((256, 128), F32)

        def one(j, _):
            jz, jx = lax.div(j, 2), lax.rem(j, 2)
            keys, values = r["kv"].at[jz, jx, 0][...], r["kv"].at[jz, jx, 1][...]
            key_halves = halves(keys)
            seen = ids_of(j)[1] <= query_ids
            dq, dk, dv = 0.0, 0.0, 0.0
            for h in range(2):
                score = jnp.where(seen, mt(queries[h], keys), -1e30)
                prob = jnp.exp(score - logs[h])
                d_score = (prob * (mt(grads[h], values) - dots[h])).astype(BF16)
                dv += tm(prob.astype(BF16), grads[h])
                dk += tm(d_score, queries[h])
                dq += mm(d_score, key_halves[h])
            r["acc"][0] += dq
            d_kv.at[j][...] += jnp.concatenate([dk, dv], axis=1)
            return 0

        lax.fori_loop(0, many, one, 0)
        r["dq"].at[qi][...] = r["acc"][0] * 0.125
        if qi < 3:
            give(qi + 1)

    attend_back(3)
    sum_f.last()
    attend_back(2)
    done_f = sum_f.out()
    for i in NEAR[1:]:
        gather_b.pass_on(i)
    attend_back(1)
    for i in NEAR:
        gather_b.ready(i)
    sum_o = out_grads()
    attend_back(0)
    give(0)

    scatter1 = Scatter("e1")
    for at, i in enumerate(NEAR):
        zz = lax.rem(z - i + 4, 4)
        dkv_copy(zz).wait_recv()
        cosine, sine = r["cos"].at[zz][...], -r["sin"].at[zz][...]
        d_tile = d_kv.at[2 * zz + xh][...]
        d_key = d_tile[:, :128] + r["dkvr"].at[zz, 0][...].astype(F32)
        d_value = d_tile[:, 128:] + r["dkvr"].at[zz, 1][...].astype(F32)
        r["dqkv"].at[zz][...] = jnp.concatenate(
            [
                turn(r["dq"].at[zz][...], cosine, sine).astype(BF16),
                turn(d_key, cosine, sine).astype(BF16),
                d_value.astype(BF16),
            ],
            axis=1,
        )
        scatter1.put(i, mt(r["dqkv"].at[zz][...], w_qkv))
        if at:
            scatter1.send(NEAR[at - 1])
    scatter1.send(NEAR[3])

    def qkv_grads(b, _):
        cols = pl.ds(pl.multiple_of(b * 256, 256), 256)
        units = r["u1"][:, :, :, cols].reshape(1024, 256)
        grads = tm(units, r["dqkv"][...].reshape(1024, 384))
        rows = r["w"].at[lax.div(b, 2), pl.ds(2 * lax.rem(b, 2), 2)]
        weights = rows[:, :, :, :, :GATE].reshape(256, 384).astype(F32)
        at = GATE + WIDE
        ups = rows[:, :, :, :, at + 256 : at + WIDE].reshape(256, 128)
        gain = ups.astype(F32)[:, gain_lane - 256 : gain_lane - 255]
        weighed = jnp.sum(weights * grads, axis=1, keepdims=True) / gain
        both = jnp.concatenate([grads * gain, jnp.broadcast_to(weighed, (256, 128))], axis=1)
        r["gq"].at[b][...] = both.astype(BF16).reshape(4, 4, 16, 512)
        return 0

    lax.fori_loop(0, 4, qkv_grads, 0)
    sum_q = PlaneSum("q")
    sum_q.start()
    r["y"][...] = (r["hidden"][...] + scatter_y.total()).astype(BF16)

    total = r["go"].at[xh, grp][...].astype(F32)
    for n, copy in enumerate(sum_o):
        copy.wait_recv()
        total = total + r["gor"][n].astype(F32)
    r["so"][...] = total.astype(BF16)
    done_o = hand_out(
        r["so"], r["fo"].at[grp], grp, head_self, lambda at: {**at, "xh": e, "e": xh}
    )
    sum_q.middle()
    sum_q.last()
    e1 = scatter1.total()
    rows = r["x"][...].astype(F32)
    r1 = lax.rsqrt(jnp.mean(rows * rows, axis=-1, keepdims=True) + EPS)
    unit1 = rows * r1
    r["gx"][...] = r["gh"][...] + r1 * (
        e1 - unit1 * jnp.mean(e1 * unit1, axis=-1, keepdims=True)
    )
    done_q = sum_q.out()
    done_f()
    done_q()
    done_o()
    for zz in range(4):
        mix_copy(zz, 1 - e, mix_over).wait_send()
        pl.when(z != zz)(lambda: mix_copy(zz, e, mix_here).wait_send())
        dkv_copy(zz).wait_send()
    for copy in links.started:
        copy.wait_send()
    assert links.count <= COPIES and links.count_near <= 8


def rope_tables():
    positions = np.arange(2048, dtype=np.float32)[:, None]
    frequency = np.float32(10000.0) ** (
        np.float32(-2.0) * np.arange(32, dtype=np.float32) / np.float32(64)
    )
    angles = positions * frequency.astype(np.float32)[None, :]
    cosine, sine = np.cos(angles), np.sin(angles)
    cosines = np.concatenate([cosine] * 4, axis=1)
    sines = np.concatenate([-sine, sine, -sine, sine], axis=1)
    shape = (4, 2, 256, 128)
    return cosines.astype(np.float32).reshape(shape), sines.astype(np.float32).reshape(shape)


def per_device(
    tokens,
    blocks,
    w_query,
    w_key,
    w_value,
    w_out,
    w_gate,
    w_up,
    w_down,
    norm_attn,
    norm_mlp,
    cotangent,
):
    gain_attn = norm_attn.astype(F32)[:, None]
    gain_mlp = norm_mlp.astype(F32)[:, None]
    fill = WIDE - SLICE

    def heads(w):
        return (w.astype(F32) * gain_attn).reshape(8, 8, 128)

    def units(w, extra):
        last = jnp.pad(extra, ((0, 0), (0, fill - 1)))[:, None, :]
        return jnp.concatenate(
            [w.reshape(8, 8, SLICE), jnp.broadcast_to(last, (8, 8, fill))], axis=-1
        )

    slices = jnp.concatenate(
        [
            heads(w_query),
            heads(w_key),
            heads(w_value),
            units(w_gate.astype(F32) * gain_mlp, gain_mlp),
            units(w_up.astype(F32) * gain_mlp, gain_attn),
            units(w_down.T.astype(F32), jnp.zeros_like(gain_attn)),
        ],
        axis=-1,
    )
    slices = slices.reshape(8, 4, 2, OUT).transpose(2, 0, 1, 3).reshape(2, 8, 4 * OUT)
    outs = w_out.astype(F32).reshape(8, 2, 512).transpose(1, 0, 2)
    source = jnp.concatenate([slices, outs], axis=-1)
    cosines, sines = rope_tables()
    vmem = pl.BlockSpec(memory_space=pltpu.VMEM)
    anywhere = pl.BlockSpec(memory_space=pl.ANY)
    y, gx, ff, fq, fo = pl.pallas_call(
        kernel,
        out_shape=[jax.ShapeDtypeStruct(*spec) for spec in OUTPUTS.values()],
        in_specs=[vmem] * 4 + [anywhere] * 2,
        out_specs=[vmem] * len(OUTPUTS),
        scratch_shapes=[pltpu.VMEM(*spec) for spec in HELD.values()]
        + [
            pltpu.SemaphoreType.DMA((COPIES,)),
            pltpu.SemaphoreType.DMA((COPIES,)),
            pltpu.SemaphoreType.DMA((8,)),
        ],
        compiler_params=pltpu.CompilerParams(
            collective_id=0, has_side_effects=True, vmem_limit_bytes=63 * 2**20
        ),
    )(
        tokens[0],
        cotangent[0],
        source,
        blocks.reshape(8, 1, 256),
        jnp.asarray(cosines),
        jnp.asarray(sines),
    )

    def rows(part):
        return part.astype(F32).transpose(0, 3, 2, 1, 4).reshape(64, -1)

    def gains(part):
        return jnp.sum(part.astype(F32), axis=(1, 2)).reshape(64)

    return (
        y[None],
        gx[None],
        rows(fq[..., :128]),
        rows(fq[..., 128:256]),
        rows(fq[..., 256:384]),
        fo.astype(F32).transpose(1, 0, 2).reshape(64, -1),
        rows(ff[..., :SLICE]),
        rows(ff[..., WIDE : WIDE + SLICE]),
        rows(ff[..., 2 * WIDE : 2 * WIDE + SLICE]).T,
        gains(fq[..., 384]),
        gains(ff[..., 2 * WIDE + SLICE]),
    )


def solution(mesh):
    both = ("grp", "ctx")
    row = P(both, None)
    tokens = P("grp", "ctx", None)
    shard = P("ctx", None)
    return jax.shard_map(
        per_device,
        mesh=mesh,
        in_specs=(
            tokens,
            P("grp", None),
            *[row] * 6,
            P(None, both),
            P(both),
            P(both),
            tokens,
        ),
        out_specs=(tokens, tokens, *[shard] * 6, P(None, "ctx"), P("ctx"), P("ctx")),
        check_vma=False,
    )
```

```python
import functools
import types

import jax
import jax.numpy as jnp
import numpy as np
from jax import lax
from jax.experimental import pallas as pl
from jax.experimental.pallas import tpu as pltpu
from jax.sharding import PartitionSpec as P

MESH = pl.DeviceIdType.MESH
F32 = jnp.float32
BF16 = jnp.bfloat16
EPS = 1e-05
HD = 64
SLICE = 352
WIDE = 384
QKV, GATE, DOWN, OUT = 0, 384, 1152, 1536
NEAR = (0, 1, 3, 2)


def mm(left, right):
    return jnp.dot(left, right, preferred_element_type=F32)


def mt(left, right):
    return lax.dot_general(left, right, (((1,), (1,)), ((), ())), preferred_element_type=F32)


def tm(left, right):
    return lax.dot_general(left, right, (((0,), (0,)), ((), ())), preferred_element_type=F32)


def window(s):
    rest = s * SLICE % 128
    return s * SLICE - rest, WIDE if rest + SLICE <= WIDE else WIDE + 128, rest


def turn(values, cosine, sine):
    lane = lax.broadcasted_iota(jnp.int32, values.shape, 1)
    ahead = pltpu.roll(values, 96, 1)
    behind = pltpu.roll(values, 32, 1)
    return values * cosine + jnp.where(lax.rem(lane, 64) < 32, ahead, behind) * sine


HELD = dict(
    wsrc=((2, 8, 6656), F32),
    ff=((8, 4, 16, 1152), BF16),
    fq=((8, 64, 512), BF16),
    sq=((64, 512), BF16),
    sf=((4, 16, 1152), BF16),
    zf=((4, 16, 1152), BF16),
    fo=((8, 64, 128), BF16),
    relay=((4, 16, 1152), BF16),
    pair=((16, 6656), F32),
    wz=((4, 16, 2048), BF16),
    wrow=((4, 16, 2048), BF16),
    w=((2, 4, 4, 2, 16, 1536), BF16),
    wo=((2, 2, 4, 4, 2, 16, 512), BF16),
    u1=((4, 2, 128, 1024), BF16),
    gg=((4, 2, 128, 1024), BF16),
    u2=((4, 2, 128, 1024), BF16),
    db=((4, 2, 128, 1024), BF16),
    cos=((4, 256, 128), F32),
    sin=((4, 256, 128), F32),
    q=((4, 256, 128), BF16),
    kv=((4, 2, 2, 256, 128), BF16),
    score=((2, 4, 256, 512), F32),
    kt=((4, 128, 512), BF16),
    u1t=((1024, 1024), BF16),
    dkv=((4, 2, 256, 256), F32),
    top=((2, 256, 128), F32),
    acc=((2, 256, 128), F32),
    mix=((4, 256, 128), F32),
    mixb=((4, 2, 128, 128), BF16),
    mixin=((4, 2, 128, 128), BF16),
    lse=((4, 256, 128), F32),
    hidden=((128, 1024), F32),
    unit2=((128, 1024), F32),
    r2=((128, 1), F32),
    dgu=((4, 256, 2 * WIDE), BF16),
    act=((16, 64, WIDE), BF16),
    gh=((128, 1024), F32),
    dmixb=((4, 2, 128, 128), BF16),
    dmix=((4, 2, 128, 128), BF16),
    dq=((4, 256, 128), F32),
    dqt=((128, 256), F32),
    dkvs=((4, 2, 256, 128), BF16),
    dkvr=((4, 2, 256, 128), BF16),
    dqkv=((4, 256, 384), BF16),
    go=((2, 8, 64, 128), BF16),
    gor=((15, 64, 128), BF16),
    so=((64, 128), BF16),
)
for kind in ("e2", "out", "e1"):
    HELD[kind + "p"] = ((4, 2, 128, 1024), BF16)
    HELD[kind + "d"] = ((4, 128, 1024), BF16)
    HELD[kind + "r"] = ((3, 128, 1024), BF16)
SPLIT = {"f": (512, 640), "q": (128, 256)}
ROWS = {"f": (4, 4, 4, 16), "q": (4, 4, 64)}
for kind, (by_x, by_y) in SPLIT.items():
    HELD["g" + kind] = (ROWS[kind] + (by_x + by_y,), BF16)
    one, two = ((4, 4, 16), (4, 16)) if kind == "f" else ((4, 64), (64,))
    for axis, width in (("x", by_x), ("y", by_y)):
        HELD["r1" + axis + kind] = ((3,) + one + (width,), BF16)
        HELD["r2" + axis + kind] = ((3,) + two + (width,), BF16)
INPUTS = dict(
    x=((128, 1024), BF16),
    g=((128, 1024), BF16),
    wq=((8, 1024), BF16),
    wk=((8, 1024), BF16),
    wv=((8, 1024), BF16),
    wo8=((8, 1024), BF16),
    wg=((8, 8 * SLICE), BF16),
    wu=((8, 8 * SLICE), BF16),
    extra=((8, 8 * SLICE + 128), F32),
    ids=((8, 1, 256), jnp.int32),
    cosines=((4, 2, 256, 128), F32),
    sines=((4, 2, 256, 128), F32),
)
TABLES = ("cosines", "sines")
FEED = 8 * SLICE
OUTPUTS = dict(
    y=((128, 1024), BF16),
    gx=((128, 1024), F32),
    heads=((4, 64, 1024), BF16),
    feeds=((3, 64, FEED), BF16),
    grad_gains=((64, 128), F32),
)
for given in (INPUTS, OUTPUTS):
    HELD.update({name: spec for name, spec in given.items() if name not in TABLES})
RING, SENDS, LANDINGS, LOCAL = 48, 81, 65, 20


def device(at):
    return (at["xl"] * 4 + at["y"], at["z"] * 4 + at["xh"] * 2 + at["e"])


class Links:
    def __init__(self, send, recv, near):
        self.send, self.recv, self.near = send, recv, near
        self.fixed, self.landings, self.count_near = RING, 0, 0
        self.started = []

    def fixed_slots(self, many):
        self.fixed += many
        return self.fixed - many

    def landing(self, many=1):
        self.landings += many
        return self.landings - many

    def make(self, src, dst, peer, slot, land):
        return pltpu.make_async_remote_copy(
            src_ref=src,
            dst_ref=dst,
            send_sem=self.send.at[slot],
            recv_sem=self.recv.at[land],
            device_id=device(peer),
            device_id_type=MESH,
        )

    def go(self, src, dst, peer, land=None):
        at = len(self.started)
        if at >= RING:
            self.left(at - RING)
        copy = self.make(src, dst, peer, at % RING, self.landing() if land is None else land)
        copy.start()
        self.started.append(copy)
        return copy

    def left(self, at):
        if self.started[at] is not None:
            self.started[at].wait_send()
            self.started[at] = None

    def arrived(self, like, peer, land):
        self.make(like, like, peer, 0, land).wait_recv()

    def here(self, src, dst):
        copy = pltpu.make_async_copy(src, dst, self.near.at[self.count_near])
        self.count_near += 1
        copy.start()
        return copy


def kernel(*refs):
    n_in, n_out = len(INPUTS), len(OUTPUTS)
    given = dict(zip(INPUTS, refs[:n_in]))
    result = dict(zip(OUTPUTS, refs[n_in : n_in + n_out]))
    held = dict(zip(HELD, refs[n_in + n_out : n_in + n_out + len(HELD)]))
    r = types.SimpleNamespace(**held)
    links = Links(*refs[n_in + n_out + len(HELD) :])
    grp, ctx = lax.axis_index("grp"), lax.axis_index("ctx")
    me = {
        "xl": lax.div(grp, 4),
        "y": lax.rem(grp, 4),
        "z": lax.div(ctx, 4),
        "xh": lax.rem(lax.div(ctx, 2), 2),
        "e": lax.rem(ctx, 2),
    }
    xl, y, z, xh, e = (me[k] for k in ("xl", "y", "z", "xh", "e"))
    x = xh * 2 + xl

    def other_core(at):
        return {**at, "e": 1 - at["e"]}

    def along_z(by):
        return {**me, "z": lax.rem(z + by + 4, 4)}

    def in_plane(dx, dy):
        to = lax.rem(x + dx, 4)
        return {**me, "xl": lax.rem(to, 2), "xh": lax.div(to, 2), "y": lax.rem(y + dy, 4)}

    def group(dxl, dy):
        return {**me, "xl": lax.rem(xl + dxl, 2), "y": lax.rem(y + dy, 4)}

    partner = other_core(me)
    across = in_plane(2, 0)
    plane = sorted(
        ((dx, dy) for dx in range(4) for dy in range(4) if dx or dy),
        key=lambda d: -min(d[0], 4 - d[0]) - min(d[1], 4 - d[1]),
    )
    groups = [(dxl, dy) for dxl in range(2) for dy in range(4)]

    came_in = {
        name: links.here(given[name], held[name]) for name in INPUTS if name not in TABLES
    }
    written = []

    def write(name):
        written.append(links.here(held[name], result[name]))

    sem = pltpu.get_barrier_semaphore()

    def greet(peer):
        pl.semaphore_signal(sem, inc=1, device_id=device(peer), device_id_type=MESH)

    row_self = jnp.logical_and(z == y, xl == e)
    head_self = xh == e
    peers = [partner] + [along_z(i) for i in (1, 2, 3)] + [other_core(along_z(i)) for i in (1, 2, 3)]
    peers += [in_plane(*d) for d in plane]
    peers += [other_core(group(0, dy)) for dy in (1, 2, 3)]
    for peer in peers:
        greet(peer)
    for d in groups:
        by_head = {**group(*d), "xh": e, "e": xh}
        by_row = {**me, "xl": e, "y": z, "z": lax.rem(z + d[1], 4), "e": lax.rem(e + d[0], 2)}
        for own, source in ((row_self, by_row), (head_self, by_head)):
            if d != (0, 0):
                greet(source)
            else:
                pl.when(jnp.logical_not(own))(functools.partial(greet, source))
    others = 16 - row_self.astype(jnp.int32) - head_self.astype(jnp.int32)
    tables = [
        links.here(given["cosines"].at[:, xh], r.cos),
        links.here(given["sines"].at[:, xh], r.sin),
    ]
    for copy in came_in.values():
        copy.wait()
    extra = r.extra[...]
    gains = {"attn": extra[:, FEED : FEED + 1], "mlp": extra[:, FEED + 1 : FEED + 2]}
    lane = lax.broadcasted_iota(jnp.int32, (8, WIDE), 1)
    wide = {
        GATE: (r.wg[...].astype(F32) * gains["mlp"], gains["mlp"]),
        GATE + WIDE: (r.wu[...].astype(F32) * gains["mlp"], gains["attn"]),
        DOWN: (extra[:, :FEED], 0.0),
    }
    narrow = [w[...].astype(F32) * gains["attn"] for w in (r.wq, r.wk, r.wv)]
    for s in range(8):
        base = s // 2 * OUT
        for n, whole in enumerate(narrow):
            part = whole[:, s * 128 : (s + 1) * 128]
            r.wsrc[s % 2, :, base + n * 128 : base + (n + 1) * 128] = part
        start, many, rest = window(s)
        for at, (whole, fill) in wide.items():
            part = whole[:, start : start + many]
            if rest:
                part = pltpu.roll(part, many - rest, 1)[:, :WIDE]
            part = jnp.where(lane < SLICE, part, jnp.where(lane == SLICE, fill, 0.0))
            r.wsrc[s % 2, :, base + at : base + at + WIDE] = part
    for h in range(2):
        r.wsrc[h, :, 4 * OUT :] = r.wo8[:, h * 512 : (h + 1) * 512].astype(F32)
    own_rows = pl.ds(pl.multiple_of(e * 8, 8), 8)
    r.pair[own_rows, :] = r.wsrc.at[e][...]

    pl.semaphore_wait(sem, len(peers) + others)

    class Gather:
        def __init__(self, buf):
            self.buf = buf
            self.land = links.landing(2)

        def start(self):
            mine = self.buf.at[z, e]
            for i in (2, 1, 3):
                links.go(mine, mine, along_z(i), self.land)
            links.go(mine, mine, partner, self.land + 1)

        def pass_on(self):
            links.arrived(self.buf.at[pl.ds(0, 3), 0], partner, self.land)
            for i in (1, 2, 3):
                block = self.buf.at[lax.rem(z + i, 4), e]
                links.go(block, block, partner, self.land + 1)

        def ready(self):
            links.arrived(self.buf.at[:, 0], partner, self.land + 1)

    class QuickGather:
        def __init__(self, buf):
            self.buf = buf
            self.out = {0: None}
            self.over = {}

        def start(self):
            mine = self.buf.at[z, e]
            self.first = len(links.started)
            for i in (1, 3):
                self.out[i] = links.go(mine, mine, along_z(i))
            self.over[0] = links.go(mine, mine, partner)

        def far(self):
            for at in range(2):
                links.left(self.first + at)
            mine = self.buf.at[z, e]
            self.out[2] = links.go(mine, mine, along_z(2))

        def pass_on(self, i):
            self.out[i].wait_recv()
            block = self.buf.at[lax.rem(z - i + 4, 4), e]
            self.over[i] = links.go(block, block, partner)

        def ready(self, i):
            self.over[i].wait_recv()

    class Scatter:
        def __init__(self, kind):
            self.p, self.d, self.r = (held[kind + k] for k in "pdr")
            self.over = {}
            self.land = links.landing()

        def put(self, i, value):
            zz = lax.rem(z - i + 4, 4)
            self.p.at[zz][...] = value.astype(BF16).reshape(2, 128, 1024)
            self.over[i] = links.go(self.p.at[zz, 1 - e], self.d.at[zz], partner)

        def send(self, i):
            zz = lax.rem(z - i + 4, 4)
            if i:
                self.over[i].wait_recv()
                mine = self.p.at[zz, e]
                mine[...] = (mine[...].astype(F32) + self.d.at[zz][...].astype(F32)).astype(BF16)
                links.go(mine, self.r.at[i - 1], along_z(-i), self.land)

        def tile(self, zz, value):
            self.p[zz] = value.astype(BF16).reshape(2, 128, 1024)
            self.over[zz] = links.go(self.p.at[zz, 1 - e], self.d.at[zz], partner)

        def tile_copy(self, zz):
            by = lax.rem(z - zz + 4, 4)
            there = self.r.at[jnp.maximum(by - 1, 0)]
            return links.make(
                self.p.at[zz, e], there, {**me, "z": zz}, self.slots + zz, self.land
            )

        def tile_send(self, zz):
            self.over[zz].wait_recv()

            def away():
                mine = self.p.at[zz, e]
                mine[...] = (mine[...].astype(F32) + self.d[zz].astype(F32)).astype(BF16)
                self.tile_copy(zz).start()

            pl.when(z != zz)(away)

        def total(self, waited=False):
            if not waited:
                self.over[0].wait_recv()
            result = self.p.at[z, e][...].astype(F32) + self.d.at[z][...].astype(F32)
            links.arrived(self.r, partner, self.land)
            for i in range(3):
                result = result + self.r[i].astype(F32)
            return result

    class Spread:
        def __init__(self, buf, along_x, along_y):
            self.own = [buf.at[xl, y, :, xh, :, along_x], buf.at[xl, y, :, xh, :, along_y]]
            self.line = [buf.at[:, y, :, :, :, along_x], buf.at[xl, :, :, xh, :, along_y]]
            three, both = pl.ds(0, 3), (along_x, along_y)
            self.three_own = [buf.at[0, three, :, 0, :, cols] for cols in both]
            self.three_lines = [buf.at[:, three, :, :, :, cols] for cols in both]
            self.land = links.landing(4)

        def start(self):
            for d in (2, 1, 3):
                links.go(self.own[0], self.own[0], in_plane(d, 0), self.land)
                links.go(self.own[1], self.own[1], in_plane(0, d), self.land + 1)

        def pass_on(self, k):
            links.arrived(self.three_own[k], partner, self.land + k)
            for d in (2, 1, 3):
                to = in_plane(d, 0) if k else in_plane(0, d)
                links.go(self.line[k], self.line[k], to, self.land + 2 + k)

        def wait(self):
            for k in range(2):
                links.arrived(self.three_lines[k], partner, self.land + 2 + k)

    class PlaneSum:
        def __init__(self, kind):
            self.by_x = pl.ds(0, SPLIT[kind][0])
            self.by_y = pl.ds(*SPLIT[kind])
            self.g = held["g" + kind]
            self.one = held["r1x" + kind], held["r1y" + kind]
            self.two = held["r2x" + kind], held["r2y" + kind]
            self.feed = kind == "f"
            self.land = links.landing(4)

        def part(self, at_x, at_y, cols):
            if self.feed:
                return self.g.at[:, at_x, at_y, :, cols]
            return self.g.at[at_y, at_x, :, cols]

        def start(self):
            every = slice(None)
            for d in (2, 1, 3):
                there = self.part(lax.rem(x + d, 4), every, self.by_x)
                links.go(there, self.one[0].at[d - 1], in_plane(d, 0), self.land)
                there = self.part(every, lax.rem(y + d, 4), self.by_y)
                links.go(there, self.one[1].at[d - 1], in_plane(0, d), self.land + 1)

        def add(self, mine, landed):
            result = mine[...].astype(F32)
            for d in range(3):
                result = result + landed[d].astype(F32)
            return result

        def middle(self):
            every = slice(None)
            for k in range(2):
                links.arrived(self.one[k], partner, self.land + k)
            mine = self.part(x, every, self.by_x)
            mine[...] = self.add(mine, self.one[0]).astype(BF16)
            mine = self.part(every, y, self.by_y)
            mine[...] = self.add(mine, self.one[1]).astype(BF16)
            for d in (2, 1, 3):
                there = self.part(x, lax.rem(y + d, 4), self.by_x)
                links.go(there, self.two[0].at[d - 1], in_plane(0, d), self.land + 2)
                there = self.part(lax.rem(x + d, 4), y, self.by_y)
                links.go(there, self.two[1].at[d - 1], in_plane(d, 0), self.land + 3)

        def last(self):
            for k in range(2):
                links.arrived(self.two[k], partner, self.land + 2 + k)
            return [
                self.add(self.part(x, y, cols), landed)
                for cols, landed in zip((self.by_x, self.by_y), self.two)
            ]

    class StagedOut:
        def __init__(self, src, dst, relay):
            self.src, self.dst, self.relay = src, dst, relay
            self.slot = y * 2 + e
            self.land = links.landing(2)
            self.fixed = links.fixed_slots(1)
            self.near = links.near.at[links.count_near]
            links.count_near += 1

        def along_y(self, src, at_e):
            mine = self.dst.at[self.slot]
            for dy in (2, 1, 3):
                links.go(src, mine, {**group(0, dy), "e": at_e}, self.land + 1)
            near = pltpu.make_async_copy(src, mine, self.near)
            over = links.make(src, mine, partner, self.fixed, self.land + 1)
            pl.when(e == at_e)(near.start)
            pl.when(e != at_e)(over.start)
            return near, over

        def start(self):
            links.go(self.src, self.relay, group(1, 0), self.land)
            self.along_y(self.src, xl)

        def pass_on(self):
            links.arrived(self.relay, partner, self.land)
            self.local = self.along_y(self.relay, 1 - xl)

        def finish(self):
            near, over = self.local
            near.wait()
            over.wait_send()
            links.arrived(self.dst.at[pl.ds(0, 7)], partner, self.land + 1)

    def hand_out(src, dst, slot, self_is, place):
        first, land = links.fixed_slots(8), links.landing()
        mine = dst.at[slot]
        copies = [
            links.make(src, mine, place(group(*d)), first + n, land)
            for n, d in enumerate(groups)
        ]
        near = pltpu.make_async_copy(src, mine, links.near.at[links.count_near])
        links.count_near += 1
        for copy in copies[1:]:
            copy.start()
        pl.when(self_is)(near.start)
        pl.when(jnp.logical_not(self_is))(copies[0].start)

        def finish():
            def with_own():
                near.wait()
                links.arrived(dst.at[pl.ds(0, 7)], partner, land)

            def without():
                copies[0].wait_send()
                links.arrived(dst, partner, land)

            pl.when(self_is)(with_own)
            pl.when(jnp.logical_not(self_is))(without)
            for copy in copies[1:]:
                copy.wait_send()

        return finish

    swap = links.go(r.wsrc.at[1 - e], r.pair.at[own_rows, :], partner)
    rows = r.x[...].astype(F32)
    r1 = lax.rsqrt(jnp.mean(rows * rows, axis=-1, keepdims=True) + EPS)
    r.u1.at[z, e][...] = (rows * r1).astype(BF16)
    r.gg.at[z, e][...] = r.g[...]
    swap.wait_recv()
    for zz in range(4):
        r.wz[zz, :, :OUT] = r.pair[:, zz * OUT : (zz + 1) * OUT].astype(BF16)
        r.wz[zz, :, OUT:] = r.pair[:, 4 * OUT :].astype(BF16)
    land = links.landing()
    for i in (2, 1, 3):
        links.go(r.wz.at[lax.rem(z + i, 4)], r.wrow.at[z], along_z(i), land)
    gather1 = Gather(r.u1)
    gather1.start()
    r.wrow.at[z][...] = r.wz.at[z][...]
    links.arrived(r.wrow.at[pl.ds(0, 3)], partner, land)
    part = r.wrow.at[:, :, pl.ds(QKV, GATE)]
    there = r.w.at[xl, y, :, xh, :, pl.ds(QKV, GATE)]
    came_qkv = links.landing()
    for d in plane:
        links.go(part, there, in_plane(*d), came_qkv)
    r.w.at[xl, y, :, xh][...] = r.wrow[:, :, :OUT]
    r.wo.at[e, xl, y, :, xh][...] = r.wrow[:, :, OUT:]
    spread_out = Spread(r.wo.at[e], pl.ds(0, 256), pl.ds(256, 256))
    spread_feed = Spread(r.w, pl.ds(GATE, 768), pl.ds(GATE + 768, 384))
    spread_out.start()
    spread_feed.start()
    gather1.pass_on()
    gather_g = Gather(r.gg)
    gather_g.start()
    for copy in tables:
        copy.wait()
    gather1.ready()
    links.arrived(r.act.at[pl.ds(0, 15)], partner, came_qkv)

    w_qkv = r.w[:, :, :, :, :, QKV:GATE].reshape(1024, GATE - QKV)
    came_kv = []
    for zz in range(4):
        qkv = mm(r.u1[zz].reshape(256, 1024), w_qkv)
        cosine, sine = r.cos[zz], r.sin[zz]
        r.kv.at[zz, xh, 0][...] = turn(qkv[:, 128:256], cosine, sine).astype(BF16)
        r.kv.at[zz, xh, 1][...] = qkv[:, 256:].astype(BF16)
        tile = r.kv.at[zz, xh]
        came_kv.append(links.go(tile, tile, across))
        r.q[zz] = (turn(qkv[:, :128], cosine, sine).astype(BF16) * 0.125).astype(BF16)

    first = lax.broadcasted_iota(jnp.int32, (256, 128), 1) < HD

    def halves(pair):
        zero = jnp.zeros_like(pair)
        return jnp.where(first, pair, zero), jnp.where(first, zero, pair)

    def ids_of(row):
        row = row.astype(F32)
        return row, jnp.broadcast_to(row, (128, row.shape[1])).T[:, :1]

    def pair_ids(p):
        return jnp.concatenate([r.ids[2 * p], r.ids[2 * p + 1]], axis=1)

    def key_tiles(qi, body):
        def whole(p, _):
            body(p, 2, False)
            return 0

        if qi:
            lax.fori_loop(0, qi, whole, 0)
        body(qi, 2, True)
        if qi < 3:
            pl.when(xh == 1)(lambda: body(qi + 1, 1, True))

    mix_slots, mix_land = links.fixed_slots(8), links.landing(2)

    def mix_copy(qi, far):
        at_e = 1 - e if far else e
        to = {**me, "z": qi, "e": at_e}
        src = r.mixb.at[qi, at_e]
        return links.make(
            src, r.mixin.at[z, e], to, mix_slots + 2 * qi + far, mix_land + far
        )

    def attend(qi):
        queries = halves(r.q[qi])
        _, query_ids = ids_of(r.ids.at[2 * qi + xh][...])
        r.top[...] = jnp.full((2, 256, 128), -3e38, F32)

        def one(p, tiles, masked):
            wide = 256 * tiles
            keys = r.kv.at[p, pl.ds(0, tiles), 0][...].reshape(wide, 128)
            for h in range(2):
                score = mt(queries[h], keys)
                if masked:
                    seen = pair_ids(p)[:, :wide].astype(F32) <= query_ids
                    score = jnp.where(seen, score, -1e30)
                r.score.at[h, p, :, pl.ds(0, wide)][...] = score
                top = r.top[h]
                for k in range(wide // 128):
                    top = jnp.maximum(top, score[:, k * 128 : (k + 1) * 128])
                r.top[h] = top

        key_tiles(qi, one)
        tops = [jnp.max(r.top[h], axis=1, keepdims=True) for h in range(2)]
        r.top[...] = jnp.zeros((2, 256, 128), F32)
        r.acc[...] = jnp.zeros((2, 256, 128), F32)

        def two(p, tiles, masked):
            wide = 256 * tiles
            values = r.kv.at[p, pl.ds(0, tiles), 1][...].reshape(wide, 128)
            for h in range(2):
                weight = jnp.exp(r.score.at[h, p, :, pl.ds(0, wide)][...] - tops[h])
                total = r.top[h]
                for k in range(wide // 128):
                    total = total + weight[:, k * 128 : (k + 1) * 128]
                r.top[h] = total
                r.acc[h] += mm(weight.astype(BF16), values)

        key_tiles(qi, two)
        sums = [jnp.sum(r.top[h], axis=1, keepdims=True) for h in range(2)]
        mixed = jnp.where(first, r.acc[0] / sums[0], r.acc[1] / sums[1])
        r.mix.at[qi][...] = mixed
        r.lse.at[qi][...] = jnp.where(
            first, tops[0] + jnp.log(sums[0]), tops[1] + jnp.log(sums[1])
        )
        r.mixb.at[qi][...] = mixed.astype(BF16).reshape(2, 128, 128)
        mix_copy(qi, 1).start()
        pl.when(z != qi)(lambda: mix_copy(qi, 0).start())

    spread_out.pass_on(0)
    spread_feed.pass_on(0)

    def turn_units(b, _):
        cols = pl.ds(pl.multiple_of(b * 256, 256), 256)
        r.u1t[cols, :] = r.u1[:, :, :, cols].reshape(1024, 256).T
        return 0

    lax.fori_loop(0, 4, turn_units, 0)
    came_kv[0].wait_recv()
    for qi in range(4):
        if qi < 3:
            came_kv[qi + 1].wait_recv()
        if qi == 2:
            spread_out.pass_on(1)
            spread_feed.pass_on(1)
        attend(qi)
        if qi == 1:
            gather_g.pass_on()
    r.mixin.at[z, e][...] = r.mixb.at[z, e][...]

    spread_out.wait()
    half = links.go(r.wo.at[e], r.wo.at[e], partner)
    links.arrived(r.mixin.at[pl.ds(0, 3), 0], partner, mix_land)
    links.arrived(r.mixin.at[:, 0], partner, mix_land + 1)
    half.wait_recv()
    mixed = jnp.concatenate([r.mixin[s // 2, s % 2] for s in range(8)], axis=1)
    hidden = r.x[...].astype(F32) + jnp.concatenate(
        [mm(mixed, r.wo[h].reshape(1024, 512)) for h in range(2)], axis=1
    )
    r2 = lax.rsqrt(jnp.mean(hidden * hidden, axis=-1, keepdims=True) + EPS)
    unit2 = hidden * r2
    r.hidden[...] = hidden
    r.unit2[...] = unit2
    r.r2[...] = r2
    r.u2.at[z, e][...] = unit2.astype(BF16)
    gather2 = QuickGather(r.u2)
    gather2.start()
    spread_feed.wait()
    gather_g.ready()
    w_down = r.w[:, :, :, :, :, DOWN:OUT].reshape(1024, WIDE)

    def down_back(zz, _):
        back = mm(r.gg.at[zz][...].reshape(256, 1024), w_down)
        r.score.at[0, zz, :, :WIDE][...] = back
        return 0

    lax.fori_loop(0, 4, down_back, 0)
    gather2.far()

    w_up = r.w[:, :, :, :, :, GATE:DOWN].reshape(1024, 2 * WIDE)
    real = lax.broadcasted_iota(jnp.int32, (256, WIDE), 1) < SLICE
    scatter2, scatter_y = Scatter("e2"), Scatter("out")
    for at, i in enumerate(NEAR):
        if i:
            gather2.pass_on(i)
        gather2.ready(i)
        zz = lax.rem(z - i + 4, 4)
        sums = mm(r.u2.at[zz][...].reshape(256, 1024), w_up)
        gate, up = sums[:, :WIDE], sums[:, WIDE:]
        sigmoid = 1.0 / (1.0 + jnp.exp(-gate))
        swish = gate * sigmoid
        back = r.score.at[0, zz, :, :WIDE][...]
        act = jnp.where(real, swish * up, 0.0).astype(BF16)
        r.act.at[pl.ds(4 * zz, 4)][...] = act.reshape(4, 64, WIDE)
        d_gate = back * up * sigmoid * (1.0 + gate * (1.0 - sigmoid))
        d_gate = jnp.where(real, d_gate, 0.0).astype(BF16)
        d_up = jnp.where(real, back * swish, 0.0).astype(BF16)
        r.dgu.at[zz][...] = jnp.concatenate([d_gate, d_up], axis=1)
        scatter2.put(i, mt(r.dgu.at[zz][...], w_up))
        if at:
            scatter2.send(NEAR[at - 1])
    scatter2.send(NEAR[3])

    gain_lane = SLICE

    def feed_grads(b, _):
        cols = pl.ds(pl.multiple_of(b * 256, 256), 256)
        units = r.u2[:, :, :, cols].reshape(1024, 256)
        grads = tm(units, r.dgu[...].reshape(1024, 2 * WIDE))
        weights = r.w.at[lax.div(b, 2), pl.ds(2 * lax.rem(b, 2), 2), :, :, :, GATE:DOWN]
        weights = weights[...].reshape(256, 2 * WIDE).astype(F32)
        gain = weights[:, gain_lane : gain_lane + 1]
        lane = lax.broadcasted_iota(jnp.int32, (256, 2 * WIDE), 1)
        keep = lax.rem(lane, WIDE) < SLICE
        weighed = jnp.sum(jnp.where(keep, weights * grads, 0.0), axis=1, keepdims=True) / gain
        shape = (4, 4, 16, -1)
        r.gf.at[b, :, :, :, : 2 * WIDE][...] = (grads * gain).astype(BF16).reshape(shape)
        downs = tm(
            r.gg[:, :, :, cols].reshape(1024, 256), r.act[...].reshape(1024, WIDE)
        )
        lane = lax.broadcasted_iota(jnp.int32, (256, WIDE), 1)
        downs = jnp.where(lane == gain_lane, weighed, downs)
        r.gf.at[b, :, :, :, 2 * WIDE :][...] = downs.astype(BF16).reshape(shape)
        return 0

    lax.fori_loop(0, 4, feed_grads, 0)
    sum_f = PlaneSum("f")
    sum_f.start()

    def down_out(i):
        zz = lax.rem(z - i + 4, 4)
        scatter_y.put(i, mt(r.act.at[pl.ds(4 * zz, 4)][...].reshape(256, WIDE), w_down))

    e2 = scatter2.total()
    unit2 = r.unit2[...]
    grad_hidden = r.g[...].astype(F32) + r.r2[...] * (
        e2 - unit2 * jnp.mean(e2 * unit2, axis=-1, keepdims=True)
    )
    r.gh[...] = grad_hidden
    branch = grad_hidden.astype(BF16)
    r.db.at[z, e][...] = branch
    d_mixed = mt(branch[:, :512], r.wo[0].reshape(1024, 512)) + mt(
        branch[:, 512:], r.wo[1].reshape(1024, 512)
    )
    for s in range(8):
        r.dmixb[s // 2, s % 2] = d_mixed[:, s * 128 : (s + 1) * 128].astype(BF16)
    came_mix = links.landing()
    for i in NEAR:
        to = along_z(i)
        for to_e, peer in ((1 - e, other_core(to)), (e, to)):
            if i or peer is not to:
                src = r.dmixb.at[to["z"], to_e]
                links.go(src, r.dmix.at[z, e], peer, came_mix)
    r.dmix.at[z, e][...] = r.dmixb.at[z, e][...]

    gather_b = Gather(r.db)
    gather_b.start()
    for at, i in enumerate(NEAR):
        down_out(i)

    def out_grads():
        grads = tm(r.mixb[...].reshape(1024, 128), r.db[...].reshape(1024, 1024))
        grads = grads.astype(BF16)
        for j in range(2):
            for k in range(8):
                r.go[j, k] = grads[j * 64 : (j + 1) * 64, k * 128 : (k + 1) * 128]
        land = links.landing()
        for n, d in enumerate(plane):
            to = in_plane(*d)
            src = r.go.at[to["xh"], to["xl"] * 4 + to["y"]]
            links.go(src, r.gor.at[n], to, land)
        return land

    for p in range(4):
        r.kt[p] = r.kv[p, :, 0].reshape(512, 128).T

    links.arrived(r.gor.at[pl.ds(0, 14)], partner, came_mix)
    r.dkv[...] = jnp.zeros((4, 2, 256, 256), F32)
    dkv_slots, dkv_land = links.fixed_slots(4), links.landing(4)

    def dkv_copy(zz):
        return links.make(
            r.dkvs.at[zz], r.dkvr.at[zz], across, dkv_slots + zz, dkv_land + zz
        )

    def give(zz):
        both = r.dkv.at[zz, 1 - xh][...].astype(BF16)
        r.dkvs.at[zz, 0][...] = both[:, :128]
        r.dkvs.at[zz, 1][...] = both[:, 128:]
        dkv_copy(zz).start()

    def attend_back(qi):
        queries = halves(r.q[qi])
        grads = r.dmix[qi].reshape(256, 128)
        product = (grads.astype(F32) * r.mix[qi]).T
        grads = halves(grads)
        dots = [jnp.sum(product[k : k + HD], axis=0, keepdims=True) for k in (0, HD)]
        logs = r.lse[qi].T
        logs = [logs[k : k + 1] for k in (0, HD)]
        query_ids = r.ids.at[2 * qi + xh][...].astype(F32)
        def one(p, tiles, masked):
            wide = 256 * tiles
            keys, values = (
                r.kv.at[p, pl.ds(0, tiles), k][...].reshape(wide, 128) for k in range(2)
            )
            keys_turned = r.kt.at[p, :, pl.ds(0, wide)][...]
            d_key, d_value = 0.0, 0.0
            for h in range(2):
                score = mt(keys, queries[h])
                if masked:
                    _, key_ids = ids_of(pair_ids(p)[:, :wide])
                    score = jnp.where(key_ids <= query_ids, score, -1e30)
                prob = jnp.exp(score - logs[h])
                d_score = (prob * (mt(values, grads[h]) - dots[h])).astype(BF16)
                d_value += mm(prob.astype(BF16), grads[h])
                d_key += mm(d_score, queries[h])
                r.dqt[h * HD : (h + 1) * HD] += mm(
                    keys_turned[h * HD : (h + 1) * HD], d_score
                )
            both = jnp.concatenate([d_key, d_value], axis=1).reshape(tiles, 256, 256)
            r.dkv.at[p, pl.ds(0, tiles)][...] += both

        r.dqt[...] = jnp.zeros((128, 256), F32)
        key_tiles(qi, one)
        r.dq[qi] = (r.dqt[...] * 0.125).T
        if qi < 3:
            give(qi + 1)

    attend_back(3)
    for i in NEAR[1:]:
        scatter_y.send(i)
    sum_f.middle()
    attend_back(2)
    r.sf[...] = jnp.concatenate(sum_f.last(), axis=-1).astype(BF16)
    land_sf = links.landing()
    for i in (2, 1, 3):
        to = along_z(i)
        links.go(r.sf.at[to["z"]], r.zf.at[z], to, land_sf)
    r.zf.at[z][...] = r.sf.at[z][...]
    gather_b.pass_on()
    attend_back(1)
    gather_b.ready()
    sum_o = out_grads()
    attend_back(0)
    give(0)
    links.arrived(r.zf.at[pl.ds(0, 3)], partner, land_sf)
    out_f = StagedOut(r.zf, r.ff, r.relay)
    out_f.start()

    scatter1 = Scatter("e1")
    scatter1.slots = links.fixed_slots(4)
    for zz in (3, 2, 1, 0):
        dkv_copy(zz).wait_recv()
        cosine, sine = r.cos[zz], -r.sin[zz]
        d_tile = r.dkv.at[zz, xh][...]
        d_key = d_tile[:, :128] + r.dkvr[zz, 0].astype(F32)
        d_value = d_tile[:, 128:] + r.dkvr[zz, 1].astype(F32)
        r.dqkv[zz] = jnp.concatenate(
            [
                turn(r.dq[zz], cosine, sine).astype(BF16),
                turn(d_key, cosine, sine).astype(BF16),
                d_value.astype(BF16),
            ],
            axis=1,
        )

    def attn_gains(rows):
        at = GATE + WIDE + 256
        last = rows[..., at : at + 128]
        return last.reshape(-1, 128).astype(F32)[:, gain_lane - 256 : gain_lane - 255]

    def qkv_grads(b, _):
        cols = pl.ds(pl.multiple_of(b * 256, 256), 256)
        grads = mm(r.u1t[cols, :], r.dqkv[...].reshape(1024, 384))
        rows = r.w.at[lax.div(b, 2), pl.ds(2 * lax.rem(b, 2), 2)]
        r.gq.at[b][...] = (grads * attn_gains(rows)).astype(BF16).reshape(4, 64, 384)
        return 0

    lax.fori_loop(0, 4, qkv_grads, 0)
    sum_q = PlaneSum("q")
    sum_q.start()
    for zz in (3, 2, 1, 0):
        scatter1.tile(zz, mt(r.dqkv[zz], w_qkv))
        if zz < 3:
            scatter1.tile_send(zz + 1)
    scatter1.tile_send(0)
    out_f.pass_on()
    sum_q.middle()
    r.y[...] = (r.hidden[...] + scatter_y.total()).astype(BF16)
    write("y")

    total = r.go.at[xh, grp][...].astype(F32)
    links.arrived(r.gor, partner, sum_o)
    for n in range(15):
        total = total + r.gor[n].astype(F32)
    r.so[...] = total.astype(BF16)
    done_o = hand_out(r.so, r.fo, grp, head_self, lambda at: {**at, "xh": e, "e": xh})
    summed = jnp.concatenate(sum_q.last(), axis=-1)
    block = 4 * y + x
    rows = r.w.at[lax.div(block, 8), lax.rem(lax.div(block, 2), 4), pl.ds(2 * lax.rem(block, 2), 2)]
    gain = attn_gains(rows)
    weights = rows[:, :, :, :GATE].reshape(64, GATE).astype(F32)
    weighed = jnp.sum(weights * summed, axis=1, keepdims=True) / (gain * gain)
    r.sq[:, :GATE] = summed.astype(BF16)
    r.sq[:, GATE:] = jnp.broadcast_to(weighed, (64, 128)).astype(BF16)
    done_q = hand_out(r.sq, r.fq, z * 2 + e, row_self, lambda at: {**at, "z": y, "e": xl})
    e1 = scatter1.total(True)
    rows = r.x[...].astype(F32)
    r1 = lax.rsqrt(jnp.mean(rows * rows, axis=-1, keepdims=True) + EPS)
    unit1 = rows * r1
    r.gx[...] = r.gh[...] + r1 * (
        e1 - unit1 * jnp.mean(e1 * unit1, axis=-1, keepdims=True)
    )
    write("gx")

    def rows_of(landed, s):
        pieces = [landed[2 * k + s % 2, s // 2] for k in range(4)]
        return jnp.concatenate(pieces, axis=0).astype(F32)

    out_f.finish()
    r.feeds[...] = jnp.zeros((3, 64, FEED), BF16)
    lane = lax.broadcasted_iota(jnp.int32, (64, WIDE), 1)
    for s in range(8):
        part = rows_of(r.ff, s)
        start, many, rest = window(s)
        for n in range(3):
            piece = jnp.where(lane < SLICE, part[:, n * WIDE : (n + 1) * WIDE], 0.0)
            if many > WIDE:
                piece = jnp.concatenate([piece, jnp.zeros((64, 128), F32)], axis=1)
            if rest:
                piece = pltpu.roll(piece, rest, 1)
            r.feeds[n, :, start : start + many] += piece.astype(BF16)
        weighed = part[:, 2 * WIDE + SLICE : 2 * WIDE + SLICE + 1]
        gain_mlp = weighed + (gain_mlp if s else 0.0)
    write("feeds")
    done_o()
    for k in range(8):
        r.heads[3, :, k * 128 : (k + 1) * 128] = r.fo[k]
    done_q()
    for s in range(8):
        part = r.fq[s].astype(F32)
        for n in range(3):
            piece = part[:, n * 128 : (n + 1) * 128]
            r.heads[n, :, s * 128 : (s + 1) * 128] = piece.astype(BF16)
        gain_attn = part[:, 384:] + (gain_attn if s else 0.0)
    lane = lax.broadcasted_iota(jnp.int32, (64, 128), 1)
    r.grad_gains[...] = jnp.where(lane == 0, gain_attn, gain_mlp)
    write("heads")
    write("grad_gains")
    for zz in range(4):
        mix_copy(zz, 1).wait_send()
        pl.when(z != zz)(lambda: mix_copy(zz, 0).wait_send())
        dkv_copy(zz).wait_send()
        pl.when(z != zz)(lambda: scatter1.tile_copy(zz).wait_send())
    for at in range(len(links.started) - RING, len(links.started)):
        links.left(at)
    for copy in written:
        copy.wait()
    counts = links.fixed, links.landings, links.count_near
    assert counts == (SENDS, LANDINGS, LOCAL), counts


def rope_tables():
    positions = np.arange(2048, dtype=np.float32)[:, None]
    frequency = np.float32(10000.0) ** (
        np.float32(-2.0) * np.arange(32, dtype=np.float32) / np.float32(64)
    )
    angles = positions * frequency.astype(np.float32)[None, :]
    cosine, sine = np.cos(angles), np.sin(angles)
    cosines = np.concatenate([cosine] * 4, axis=1)
    sines = np.concatenate([-sine, sine, -sine, sine], axis=1)
    shape = (4, 2, 256, 128)
    return cosines.astype(np.float32).reshape(shape), sines.astype(np.float32).reshape(shape)


def per_device(
    tokens,
    blocks,
    w_query,
    w_key,
    w_value,
    w_out,
    w_gate,
    w_up,
    w_down,
    norm_attn,
    norm_mlp,
    cotangent,
):
    gains = jnp.stack([norm_attn, norm_mlp], axis=1)
    extra = jnp.concatenate([w_down.T, jnp.pad(gains, ((0, 0), (0, 126)))], axis=1).astype(F32)
    cosines, sines = rope_tables()
    anywhere = pl.BlockSpec(memory_space=pl.ANY)
    y, gx, heads, feeds, gains = pl.pallas_call(
        kernel,
        out_shape=[jax.ShapeDtypeStruct(*spec) for spec in OUTPUTS.values()],
        in_specs=[anywhere] * len(INPUTS),
        out_specs=[anywhere] * len(OUTPUTS),
        scratch_shapes=[pltpu.VMEM(*spec) for spec in HELD.values()]
        + [
            pltpu.SemaphoreType.DMA((SENDS,)),
            pltpu.SemaphoreType.DMA((LANDINGS,)),
            pltpu.SemaphoreType.DMA((LOCAL,)),
        ],
        compiler_params=pltpu.CompilerParams(
            collective_id=0, has_side_effects=True, vmem_limit_bytes=63 * 2**20
        ),
    )(
        tokens[0],
        cotangent[0],
        w_query,
        w_key,
        w_value,
        w_out,
        w_gate,
        w_up,
        extra,
        blocks.reshape(8, 1, 256),
        jnp.asarray(cosines),
        jnp.asarray(sines),
    )

    return (
        y[None],
        gx[None],
        *[heads[n].astype(F32) for n in range(4)],
        feeds[0].astype(F32),
        feeds[1].astype(F32),
        feeds[2].astype(F32).T,
        gains[:, 0],
        gains[:, 1],
    )


def solution(mesh):
    both = ("grp", "ctx")
    row = P(both, None)
    tokens = P("grp", "ctx", None)
    shard = P("ctx", None)
    return jax.shard_map(
        per_device,
        mesh=mesh,
        in_specs=(
            tokens,
            P("grp", None),
            *[row] * 6,
            P(None, both),
            P(both),
            P(both),
            tokens,
        ),
        out_specs=(tokens, tokens, *[shard] * 6, P(None, "ctx"), P("ctx"), P("ctx")),
        check_vma=False,
    )
```

```python
import functools
import types

import jax
import jax.numpy as jnp
import numpy as np
from jax import lax
from jax.experimental import pallas as pl
from jax.experimental.pallas import tpu as pltpu
from jax.sharding import PartitionSpec as P

MESH = pl.DeviceIdType.MESH
F32 = jnp.float32
BF16 = jnp.bfloat16
EPS = 1e-05
HD = 64
SLICE = 352
WIDE = 384
QKV, GATE, DOWN, OUT = 0, 384, 1152, 1536
NEAR = (0, 1, 3, 2)


def mm(left, right):
    return jnp.dot(left, right, preferred_element_type=F32)


def mt(left, right):
    return lax.dot_general(left, right, (((1,), (1,)), ((), ())), preferred_element_type=F32)


def tm(left, right):
    return lax.dot_general(left, right, (((0,), (0,)), ((), ())), preferred_element_type=F32)


def window(s):
    rest = s * SLICE % 128
    return s * SLICE - rest, WIDE if rest + SLICE <= WIDE else WIDE + 128, rest


def turn(values, cosine, sine):
    lane = lax.broadcasted_iota(jnp.int32, values.shape, 1)
    ahead = pltpu.roll(values, 96, 1)
    behind = pltpu.roll(values, 32, 1)
    return values * cosine + jnp.where(lax.rem(lane, 64) < 32, ahead, behind) * sine


HELD = dict(
    wsrc=((2, 8, 6656), F32),
    ff=((8, 4, 16, 1152), BF16),
    fq=((8, 64, 512), BF16),
    sq=((64, 512), BF16),
    sf=((4, 16, 1152), BF16),
    zf=((4, 16, 1152), BF16),
    fo=((8, 64, 128), BF16),
    relay=((4, 16, 1152), BF16),
    pair=((16, 6656), F32),
    wz=((4, 16, 2048), BF16),
    wrow=((4, 16, 2048), BF16),
    w=((2, 4, 4, 2, 16, 1536), BF16),
    wo=((2, 2, 4, 4, 2, 16, 512), BF16),
    u1=((4, 2, 128, 1024), BF16),
    gg=((4, 2, 128, 1024), BF16),
    u2=((4, 2, 128, 1024), BF16),
    db=((4, 2, 128, 1024), BF16),
    cos=((4, 256, 128), F32),
    sin=((4, 256, 128), F32),
    q=((4, 256, 128), BF16),
    kv=((4, 2, 2, 256, 128), BF16),
    score=((2, 4, 256, 512), F32),
    kt=((4, 128, 512), BF16),
    u1t=((1024, 1024), BF16),
    dkv=((4, 2, 256, 256), F32),
    top=((2, 256, 128), F32),
    acc=((2, 256, 128), F32),
    mix=((4, 256, 128), F32),
    mixb=((4, 2, 128, 128), BF16),
    mixin=((4, 2, 128, 128), BF16),
    lse=((4, 256, 128), F32),
    hidden=((128, 1024), F32),
    unit2=((128, 1024), F32),
    r2=((128, 1), F32),
    dgu=((4, 256, 2 * WIDE), BF16),
    act=((16, 64, WIDE), BF16),
    gh=((128, 1024), F32),
    dmixb=((4, 2, 128, 128), BF16),
    dmix=((4, 2, 128, 128), BF16),
    dq=((4, 256, 128), F32),
    dqt=((128, 256), F32),
    dkvs=((4, 2, 256, 128), BF16),
    dkvr=((4, 2, 256, 128), BF16),
    dqkv=((4, 256, 384), BF16),
    go=((2, 8, 64, 128), BF16),
    gor=((15, 64, 128), BF16),
    so=((64, 128), BF16),
)
for kind in ("e2", "out", "e1"):
    HELD[kind + "p"] = ((4, 2, 128, 1024), BF16)
    HELD[kind + "d"] = ((4, 128, 1024), BF16)
    HELD[kind + "r"] = ((3, 128, 1024), BF16)
SPLIT = {"f": (512, 640), "q": (256, 128)}
ROWS = {"f": (4, 4, 4, 16), "q": (4, 4, 64)}
for kind, (by_x, by_y) in SPLIT.items():
    HELD["g" + kind] = (ROWS[kind] + (by_x + by_y,), BF16)
    one, two = ((4, 4, 16), (4, 16)) if kind == "f" else ((4, 64), (64,))
    for axis, width in (("x", by_x), ("y", by_y)):
        HELD["r1" + axis + kind] = ((3,) + one + (width,), BF16)
        HELD["r2" + axis + kind] = ((3,) + two + (width,), BF16)
INPUTS = dict(
    x=((128, 1024), BF16),
    g=((128, 1024), BF16),
    wq=((8, 1024), BF16),
    wk=((8, 1024), BF16),
    wv=((8, 1024), BF16),
    wo8=((8, 1024), BF16),
    wg=((8, 8 * SLICE), BF16),
    wu=((8, 8 * SLICE), BF16),
    extra=((8, 8 * SLICE + 128), F32),
    ids=((8, 1, 256), jnp.int32),
    cosines=((4, 2, 256, 128), F32),
    sines=((4, 2, 256, 128), F32),
)
TABLES = ("cosines", "sines")
FEED = 8 * SLICE
OUTPUTS = dict(
    y=((128, 1024), BF16),
    gx=((128, 1024), F32),
    heads=((4, 64, 1024), BF16),
    feeds=((3, 64, FEED), BF16),
    grad_gains=((64, 128), F32),
)
for given in (INPUTS, OUTPUTS):
    HELD.update({name: spec for name, spec in given.items() if name not in TABLES})
RING, SENDS, LANDINGS, LOCAL = 48, 81, 68, 20


def device(at):
    return (at["xl"] * 4 + at["y"], at["z"] * 4 + at["xh"] * 2 + at["e"])


class Links:
    def __init__(self, send, recv, near):
        self.send, self.recv, self.near = send, recv, near
        self.fixed, self.landings, self.count_near = RING, 0, 0
        self.started = []

    def fixed_slots(self, many):
        self.fixed += many
        return self.fixed - many

    def landing(self, many=1):
        self.landings += many
        return self.landings - many

    def make(self, src, dst, peer, slot, land):
        return pltpu.make_async_remote_copy(
            src_ref=src,
            dst_ref=dst,
            send_sem=self.send.at[slot],
            recv_sem=self.recv.at[land],
            device_id=device(peer),
            device_id_type=MESH,
        )

    def go(self, src, dst, peer, land=None):
        at = len(self.started)
        if at >= RING:
            self.left(at - RING)
        copy = self.make(src, dst, peer, at % RING, self.landing() if land is None else land)
        copy.start()
        self.started.append(copy)
        return copy

    def left(self, at):
        if self.started[at] is not None:
            self.started[at].wait_send()
            self.started[at] = None

    def arrived(self, like, peer, land):
        self.make(like, like, peer, 0, land).wait_recv()

    def here(self, src, dst):
        copy = pltpu.make_async_copy(src, dst, self.near.at[self.count_near])
        self.count_near += 1
        copy.start()
        return copy


def kernel(*refs):
    n_in, n_out = len(INPUTS), len(OUTPUTS)
    given = dict(zip(INPUTS, refs[:n_in]))
    result = dict(zip(OUTPUTS, refs[n_in : n_in + n_out]))
    held = dict(zip(HELD, refs[n_in + n_out : n_in + n_out + len(HELD)]))
    r = types.SimpleNamespace(**held)
    links = Links(*refs[n_in + n_out + len(HELD) :])
    grp, ctx = lax.axis_index("grp"), lax.axis_index("ctx")
    me = {
        "xl": lax.div(grp, 4),
        "y": lax.rem(grp, 4),
        "z": lax.div(ctx, 4),
        "xh": lax.rem(lax.div(ctx, 2), 2),
        "e": lax.rem(ctx, 2),
    }
    xl, y, z, xh, e = (me[k] for k in ("xl", "y", "z", "xh", "e"))
    x = xh * 2 + xl

    def other_core(at):
        return {**at, "e": 1 - at["e"]}

    def along_z(by):
        return {**me, "z": lax.rem(z + by + 4, 4)}

    def in_plane(dx, dy):
        to = lax.rem(x + dx, 4)
        return {**me, "xl": lax.rem(to, 2), "xh": lax.div(to, 2), "y": lax.rem(y + dy, 4)}

    def group(dxl, dy):
        return {**me, "xl": lax.rem(xl + dxl, 2), "y": lax.rem(y + dy, 4)}

    partner = other_core(me)
    across = in_plane(2, 0)
    plane = sorted(
        ((dx, dy) for dx in range(4) for dy in range(4) if dx or dy),
        key=lambda d: -min(d[0], 4 - d[0]) - min(d[1], 4 - d[1]),
    )
    groups = [(dxl, dy) for dxl in range(2) for dy in range(4)]

    came_in = {
        name: links.here(given[name], held[name]) for name in INPUTS if name not in TABLES
    }
    written = []

    def write(name):
        written.append(links.here(held[name], result[name]))

    sem = pltpu.get_barrier_semaphore()

    def greet(peer):
        pl.semaphore_signal(sem, inc=1, device_id=device(peer), device_id_type=MESH)

    row_self = jnp.logical_and(z == y, xl == e)
    head_self = xh == e
    peers = [partner] + [along_z(i) for i in (1, 2, 3)] + [other_core(along_z(i)) for i in (1, 2, 3)]
    peers += [in_plane(*d) for d in plane]
    peers += [other_core(group(0, dy)) for dy in (1, 2, 3)]
    for peer in peers:
        greet(peer)
    for d in groups:
        by_head = {**group(*d), "xh": e, "e": xh}
        by_row = {**me, "xl": e, "y": z, "z": lax.rem(z + d[1], 4), "e": lax.rem(e + d[0], 2)}
        for own, source in ((row_self, by_row), (head_self, by_head)):
            if d != (0, 0):
                greet(source)
            else:
                pl.when(jnp.logical_not(own))(functools.partial(greet, source))
    others = 16 - row_self.astype(jnp.int32) - head_self.astype(jnp.int32)
    tables = [
        links.here(given["cosines"].at[:, xh], r.cos),
        links.here(given["sines"].at[:, xh], r.sin),
    ]
    for copy in came_in.values():
        copy.wait()
    extra = r.extra[...]
    gains = {"attn": extra[:, FEED : FEED + 1], "mlp": extra[:, FEED + 1 : FEED + 2]}
    lane = lax.broadcasted_iota(jnp.int32, (8, WIDE), 1)
    wide = {
        GATE: (r.wg[...].astype(F32) * gains["mlp"], gains["mlp"]),
        GATE + WIDE: (r.wu[...].astype(F32) * gains["mlp"], gains["attn"]),
        DOWN: (extra[:, :FEED], 0.0),
    }
    narrow = [w[...].astype(F32) * gains["attn"] for w in (r.wq, r.wk, r.wv)]
    for s in range(8):
        base = s // 2 * OUT
        for n, whole in enumerate(narrow):
            part = whole[:, s * 128 : (s + 1) * 128]
            r.wsrc[s % 2, :, base + n * 128 : base + (n + 1) * 128] = part
        start, many, rest = window(s)
        for at, (whole, fill) in wide.items():
            part = whole[:, start : start + many]
            if rest:
                part = pltpu.roll(part, many - rest, 1)[:, :WIDE]
            part = jnp.where(lane < SLICE, part, jnp.where(lane == SLICE, fill, 0.0))
            r.wsrc[s % 2, :, base + at : base + at + WIDE] = part
    for h in range(2):
        r.wsrc[h, :, 4 * OUT :] = r.wo8[:, h * 512 : (h + 1) * 512].astype(F32)
    own_rows = pl.ds(pl.multiple_of(e * 8, 8), 8)
    r.pair[own_rows, :] = r.wsrc.at[e][...]

    rows = r.x[...].astype(F32)
    r1 = lax.rsqrt(jnp.mean(rows * rows, axis=-1, keepdims=True) + EPS)
    r.u1.at[z, e][...] = (rows * r1).astype(BF16)
    r.gg.at[z, e][...] = r.g[...]
    pl.semaphore_wait(sem, len(peers) + others)

    class Gather:
        def __init__(self, buf):
            self.buf = buf
            self.land = links.landing(2)

        def start(self):
            mine = self.buf.at[z, e]
            for i in (2, 1, 3):
                links.go(mine, mine, along_z(i), self.land)
            links.go(mine, mine, partner, self.land + 1)

        def pass_on(self):
            links.arrived(self.buf.at[pl.ds(0, 3), 0], partner, self.land)
            for i in (1, 2, 3):
                block = self.buf.at[lax.rem(z + i, 4), e]
                links.go(block, block, partner, self.land + 1)

        def ready(self):
            links.arrived(self.buf.at[:, 0], partner, self.land + 1)

    class QuickGather:
        def __init__(self, buf):
            self.buf = buf
            self.out = {0: None}
            self.over = {}

        def start(self):
            mine = self.buf.at[z, e]
            for i in (1, 3):
                self.out[i] = links.go(mine, mine, along_z(i))
            self.over[0] = links.go(mine, mine, partner)
            self.land = links.landing()

        def pass_on(self, i):
            block = self.buf.at[lax.rem(z - i + 4, 4), e]
            if i == 2:
                links.arrived(block, partner, self.land)
            else:
                self.out[i].wait_recv()
                half = block.at[pl.ds(0 if i == 1 else 64, 64)]
                links.go(half, half, along_z(i), self.land)
            self.over[i] = links.go(block, block, partner)

        def ready(self, i):
            self.over[i].wait_recv()

    class Scatter:
        def __init__(self, kind):
            self.p, self.d, self.r = (held[kind + k] for k in "pdr")
            self.over = {}
            self.land = links.landing()

        def put(self, i, value):
            zz = lax.rem(z - i + 4, 4)
            self.p.at[zz][...] = value.astype(BF16).reshape(2, 128, 1024)
            self.over[i] = links.go(self.p.at[zz, 1 - e], self.d.at[zz], partner)

        def send(self, i):
            zz = lax.rem(z - i + 4, 4)
            if i:
                self.over[i].wait_recv()
                mine = self.p.at[zz, e]
                mine[...] = (mine[...].astype(F32) + self.d.at[zz][...].astype(F32)).astype(BF16)
                links.go(mine, self.r.at[i - 1], along_z(-i), self.land)

        def tile(self, zz, value):
            self.p[zz] = value.astype(BF16).reshape(2, 128, 1024)
            self.over[zz] = links.go(self.p.at[zz, 1 - e], self.d.at[zz], partner)

        def tile_copy(self, zz):
            by = lax.rem(z - zz + 4, 4)
            there = self.r.at[jnp.maximum(by - 1, 0)]
            return links.make(
                self.p.at[zz, e], there, {**me, "z": zz}, self.slots + zz, self.land
            )

        def tile_send(self, zz):
            self.over[zz].wait_recv()

            def away():
                mine = self.p.at[zz, e]
                mine[...] = (mine[...].astype(F32) + self.d[zz].astype(F32)).astype(BF16)
                self.tile_copy(zz).start()

            pl.when(z != zz)(away)

        def total(self, waited=False):
            if not waited:
                self.over[0].wait_recv()
            result = self.p.at[z, e][...].astype(F32) + self.d.at[z][...].astype(F32)
            links.arrived(self.r, partner, self.land)
            for i in range(3):
                result = result + self.r[i].astype(F32)
            return result

    class Spread:
        def __init__(self, buf, along_x, along_y):
            self.own = [buf.at[xl, y, :, xh, :, along_x], buf.at[xl, y, :, xh, :, along_y]]
            self.line = [buf.at[:, y, :, :, :, along_x], buf.at[xl, :, :, xh, :, along_y]]
            three, both = pl.ds(0, 3), (along_x, along_y)
            self.three_own = [buf.at[0, three, :, 0, :, cols] for cols in both]
            self.three_lines = [buf.at[:, three, :, :, :, cols] for cols in both]
            self.land = links.landing(4)

        def start(self):
            for d in (2, 1, 3):
                links.go(self.own[0], self.own[0], in_plane(d, 0), self.land)
                links.go(self.own[1], self.own[1], in_plane(0, d), self.land + 1)

        def pass_on(self, k):
            links.arrived(self.three_own[k], partner, self.land + k)
            for d in (2, 1, 3):
                to = in_plane(d, 0) if k else in_plane(0, d)
                links.go(self.line[k], self.line[k], to, self.land + 2 + k)

        def wait(self):
            for k in range(2):
                links.arrived(self.three_lines[k], partner, self.land + 2 + k)

    class PlaneSum:
        def __init__(self, kind):
            self.by_x = pl.ds(0, SPLIT[kind][0])
            self.by_y = pl.ds(*SPLIT[kind])
            self.g = held["g" + kind]
            self.one = held["r1x" + kind], held["r1y" + kind]
            self.two = held["r2x" + kind], held["r2y" + kind]
            self.feed = kind == "f"
            self.land = links.landing(4)

        def part(self, at_x, at_y, cols):
            if self.feed:
                return self.g.at[:, at_x, at_y, :, cols]
            return self.g.at[at_y, at_x, :, cols]

        def start(self):
            every = slice(None)
            for d in (2, 1, 3):
                there = self.part(lax.rem(x + d, 4), every, self.by_x)
                links.go(there, self.one[0].at[d - 1], in_plane(d, 0), self.land)
                there = self.part(every, lax.rem(y + d, 4), self.by_y)
                links.go(there, self.one[1].at[d - 1], in_plane(0, d), self.land + 1)

        def add(self, mine, landed):
            result = mine[...].astype(F32)
            for d in range(3):
                result = result + landed[d].astype(F32)
            return result

        def middle(self):
            every = slice(None)
            for k in range(2):
                links.arrived(self.one[k], partner, self.land + k)
            mine = self.part(x, every, self.by_x)
            mine[...] = self.add(mine, self.one[0]).astype(BF16)
            mine = self.part(every, y, self.by_y)
            mine[...] = self.add(mine, self.one[1]).astype(BF16)
            for d in (2, 1, 3):
                there = self.part(x, lax.rem(y + d, 4), self.by_x)
                links.go(there, self.two[0].at[d - 1], in_plane(0, d), self.land + 2)
                there = self.part(lax.rem(x + d, 4), y, self.by_y)
                links.go(there, self.two[1].at[d - 1], in_plane(d, 0), self.land + 3)

        def last(self):
            for k in range(2):
                links.arrived(self.two[k], partner, self.land + 2 + k)
            return [
                self.add(self.part(x, y, cols), landed)
                for cols, landed in zip((self.by_x, self.by_y), self.two)
            ]

    class StagedOut:
        def __init__(self, src, dst, relay):
            self.src, self.dst, self.relay = src, dst, relay
            self.slot = y * 2 + e
            self.land = links.landing(2)
            self.fixed = links.fixed_slots(1)
            self.near = links.near.at[links.count_near]
            links.count_near += 1

        def along_y(self, src, at_e):
            mine = self.dst.at[self.slot]
            for dy in (2, 1, 3):
                links.go(src, mine, {**group(0, dy), "e": at_e}, self.land + 1)
            near = pltpu.make_async_copy(src, mine, self.near)
            over = links.make(src, mine, partner, self.fixed, self.land + 1)
            pl.when(e == at_e)(near.start)
            pl.when(e != at_e)(over.start)
            return near, over

        def start(self):
            links.go(self.src, self.relay, group(1, 0), self.land)
            self.along_y(self.src, xl)

        def pass_on(self):
            links.arrived(self.relay, partner, self.land)
            self.local = self.along_y(self.relay, 1 - xl)

        def finish(self):
            near, over = self.local
            near.wait()
            over.wait_send()
            links.arrived(self.dst.at[pl.ds(0, 7)], partner, self.land + 1)

    def hand_out(src, dst, slot, self_is, place):
        first, land = links.fixed_slots(8), links.landing()
        mine = dst.at[slot]
        copies = [
            links.make(src, mine, place(group(*d)), first + n, land)
            for n, d in enumerate(groups)
        ]
        near = pltpu.make_async_copy(src, mine, links.near.at[links.count_near])
        links.count_near += 1
        for copy in copies[1:]:
            copy.start()
        pl.when(self_is)(near.start)
        pl.when(jnp.logical_not(self_is))(copies[0].start)

        def finish():
            def with_own():
                near.wait()
                links.arrived(dst.at[pl.ds(0, 7)], partner, land)

            def without():
                copies[0].wait_send()
                links.arrived(dst, partner, land)

            pl.when(self_is)(with_own)
            pl.when(jnp.logical_not(self_is))(without)
            for copy in copies[1:]:
                copy.wait_send()

        return finish

    swap = links.go(r.wsrc.at[1 - e], r.pair.at[own_rows, :], partner)
    swap.wait_recv()
    for zz in range(4):
        r.wz[zz, :, :OUT] = r.pair[:, zz * OUT : (zz + 1) * OUT].astype(BF16)
        r.wz[zz, :, OUT:] = r.pair[:, 4 * OUT :].astype(BF16)
    land = links.landing()
    for i in (2, 1, 3):
        links.go(r.wz.at[lax.rem(z + i, 4)], r.wrow.at[z], along_z(i), land)
    gather1 = Gather(r.u1)
    gather1.start()
    r.wrow.at[z][...] = r.wz.at[z][...]
    links.arrived(r.wrow.at[pl.ds(0, 3)], partner, land)
    r.w.at[xl, y, :, xh][...] = r.wrow[:, :, :OUT]
    r.wo.at[e, xl, y, :, xh][...] = r.wrow[:, :, OUT:]
    spread_qkv = Spread(r.w, pl.ds(QKV, 128), pl.ds(QKV + 128, 256))
    spread_out = Spread(r.wo.at[e], pl.ds(0, 384), pl.ds(384, 128))
    spread_feed = Spread(r.w, pl.ds(GATE, 768), pl.ds(GATE + 768, 384))
    for spread in (spread_qkv, spread_out, spread_feed):
        spread.start()
    spread_qkv.pass_on(0)
    spread_qkv.pass_on(1)
    gather1.pass_on()
    spread_out.pass_on(0)
    spread_feed.pass_on(0)
    gather_g = Gather(r.gg)
    gather_g.start()
    for copy in tables:
        copy.wait()
    gather1.ready()
    spread_qkv.wait()

    w_qkv = r.w[:, :, :, :, :, QKV:GATE].reshape(1024, GATE - QKV)
    came_kv = []
    for zz in range(4):
        qkv = mm(r.u1[zz].reshape(256, 1024), w_qkv)
        cosine, sine = r.cos[zz], r.sin[zz]
        r.kv.at[zz, xh, 0][...] = turn(qkv[:, 128:256], cosine, sine).astype(BF16)
        r.kv.at[zz, xh, 1][...] = qkv[:, 256:].astype(BF16)
        tile = r.kv.at[zz, xh]
        came_kv.append(links.go(tile, tile, across))
        r.q[zz] = (turn(qkv[:, :128], cosine, sine).astype(BF16) * 0.125).astype(BF16)

    first = lax.broadcasted_iota(jnp.int32, (256, 128), 1) < HD

    def halves(pair):
        zero = jnp.zeros_like(pair)
        return jnp.where(first, pair, zero), jnp.where(first, zero, pair)

    def ids_of(row):
        row = row.astype(F32)
        return row, jnp.broadcast_to(row, (128, row.shape[1])).T[:, :1]

    def pair_ids(p):
        return jnp.concatenate([r.ids[2 * p], r.ids[2 * p + 1]], axis=1)

    def key_tiles(qi, body):
        def whole(p, _):
            body(p, 2, False)
            return 0

        if qi:
            lax.fori_loop(0, qi, whole, 0)
        body(qi, 2, True)
        if qi < 3:
            pl.when(xh == 1)(lambda: body(qi + 1, 1, True))

    mix_slots, mix_land = links.fixed_slots(8), links.landing(2)

    def mix_copy(qi, far):
        at_e = 1 - e if far else e
        to = {**me, "z": qi, "e": at_e}
        src = r.mixb.at[qi, at_e]
        return links.make(
            src, r.mixin.at[z, e], to, mix_slots + 2 * qi + far, mix_land + far
        )

    def attend(qi):
        queries = halves(r.q[qi])
        _, query_ids = ids_of(r.ids.at[2 * qi + xh][...])
        r.top[...] = jnp.full((2, 256, 128), -3e38, F32)

        def one(p, tiles, masked):
            wide = 256 * tiles
            keys = r.kv.at[p, pl.ds(0, tiles), 0][...].reshape(wide, 128)
            for h in range(2):
                score = mt(queries[h], keys)
                if masked:
                    seen = pair_ids(p)[:, :wide].astype(F32) <= query_ids
                    score = jnp.where(seen, score, -1e30)
                r.score.at[h, p, :, pl.ds(0, wide)][...] = score
                top = r.top[h]
                for k in range(wide // 128):
                    top = jnp.maximum(top, score[:, k * 128 : (k + 1) * 128])
                r.top[h] = top

        key_tiles(qi, one)
        tops = [jnp.max(r.top[h], axis=1, keepdims=True) for h in range(2)]
        r.top[...] = jnp.zeros((2, 256, 128), F32)
        r.acc[...] = jnp.zeros((2, 256, 128), F32)

        def two(p, tiles, masked):
            wide = 256 * tiles
            values = r.kv.at[p, pl.ds(0, tiles), 1][...].reshape(wide, 128)
            for h in range(2):
                weight = jnp.exp(r.score.at[h, p, :, pl.ds(0, wide)][...] - tops[h])
                total = r.top[h]
                for k in range(wide // 128):
                    total = total + weight[:, k * 128 : (k + 1) * 128]
                r.top[h] = total
                r.acc[h] += mm(weight.astype(BF16), values)

        key_tiles(qi, two)
        sums = [jnp.sum(r.top[h], axis=1, keepdims=True) for h in range(2)]
        mixed = jnp.where(first, r.acc[0] / sums[0], r.acc[1] / sums[1])
        r.mix.at[qi][...] = mixed
        r.lse.at[qi][...] = jnp.where(
            first, tops[0] + jnp.log(sums[0]), tops[1] + jnp.log(sums[1])
        )
        r.mixb.at[qi][...] = mixed.astype(BF16).reshape(2, 128, 128)
        mix_copy(qi, 1).start()
        pl.when(z != qi)(lambda: mix_copy(qi, 0).start())


    def turn_units(b, _):
        cols = pl.ds(pl.multiple_of(b * 256, 256), 256)
        r.u1t[cols, :] = r.u1[:, :, :, cols].reshape(1024, 256).T
        return 0

    lax.fori_loop(0, 4, turn_units, 0)
    came_kv[0].wait_recv()
    for qi in range(4):
        if qi < 3:
            came_kv[qi + 1].wait_recv()
        if qi == 2:
            spread_out.pass_on(1)
            spread_feed.pass_on(1)
        attend(qi)
        if qi == 1:
            gather_g.pass_on()
    r.mixin.at[z, e][...] = r.mixb.at[z, e][...]

    spread_out.wait()
    half = links.go(r.wo.at[e], r.wo.at[e], partner)
    links.arrived(r.mixin.at[pl.ds(0, 3), 0], partner, mix_land)
    links.arrived(r.mixin.at[:, 0], partner, mix_land + 1)
    half.wait_recv()
    mixed = jnp.concatenate([r.mixin[s // 2, s % 2] for s in range(8)], axis=1)
    hidden = r.x[...].astype(F32) + jnp.concatenate(
        [mm(mixed, r.wo[h].reshape(1024, 512)) for h in range(2)], axis=1
    )
    r2 = lax.rsqrt(jnp.mean(hidden * hidden, axis=-1, keepdims=True) + EPS)
    unit2 = hidden * r2
    r.hidden[...] = hidden
    r.unit2[...] = unit2
    r.r2[...] = r2
    r.u2.at[z, e][...] = unit2.astype(BF16)
    gather2 = QuickGather(r.u2)
    gather2.start()
    spread_feed.wait()
    gather_g.ready()
    w_down = r.w[:, :, :, :, :, DOWN:OUT].reshape(1024, WIDE)

    def down_back(zz, _):
        back = mm(r.gg.at[zz][...].reshape(256, 1024), w_down)
        r.score.at[0, zz, :, :WIDE][...] = back
        return 0

    lax.fori_loop(0, 4, down_back, 0)

    w_up = r.w[:, :, :, :, :, GATE:DOWN].reshape(1024, 2 * WIDE)
    real = lax.broadcasted_iota(jnp.int32, (256, WIDE), 1) < SLICE
    scatter2, scatter_y = Scatter("e2"), Scatter("out")
    for at, i in enumerate(NEAR):
        if at == 1:
            gather2.pass_on(1)
            gather2.pass_on(3)
        if at == 3:
            gather2.pass_on(2)
        gather2.ready(i)
        zz = lax.rem(z - i + 4, 4)
        sums = mm(r.u2.at[zz][...].reshape(256, 1024), w_up)
        gate, up = sums[:, :WIDE], sums[:, WIDE:]
        sigmoid = 1.0 / (1.0 + jnp.exp(-gate))
        swish = gate * sigmoid
        back = r.score.at[0, zz, :, :WIDE][...]
        act = jnp.where(real, swish * up, 0.0).astype(BF16)
        r.act.at[pl.ds(4 * zz, 4)][...] = act.reshape(4, 64, WIDE)
        d_gate = back * up * sigmoid * (1.0 + gate * (1.0 - sigmoid))
        d_gate = jnp.where(real, d_gate, 0.0).astype(BF16)
        d_up = jnp.where(real, back * swish, 0.0).astype(BF16)
        r.dgu.at[zz][...] = jnp.concatenate([d_gate, d_up], axis=1)
        scatter2.put(i, mt(r.dgu.at[zz][...], w_up))
        if at:
            scatter2.send(NEAR[at - 1])
    scatter2.send(NEAR[3])

    gain_lane = SLICE

    def feed_grads(b, _):
        cols = pl.ds(pl.multiple_of(b * 256, 256), 256)
        units = r.u2[:, :, :, cols].reshape(1024, 256)
        grads = tm(units, r.dgu[...].reshape(1024, 2 * WIDE))
        weights = r.w.at[lax.div(b, 2), pl.ds(2 * lax.rem(b, 2), 2), :, :, :, GATE:DOWN]
        weights = weights[...].reshape(256, 2 * WIDE).astype(F32)
        gain = weights[:, gain_lane : gain_lane + 1]
        lane = lax.broadcasted_iota(jnp.int32, (256, 2 * WIDE), 1)
        keep = lax.rem(lane, WIDE) < SLICE
        weighed = jnp.sum(jnp.where(keep, weights * grads, 0.0), axis=1, keepdims=True) / gain
        shape = (4, 4, 16, -1)
        r.gf.at[b, :, :, :, : 2 * WIDE][...] = (grads * gain).astype(BF16).reshape(shape)
        downs = tm(
            r.gg[:, :, :, cols].reshape(1024, 256), r.act[...].reshape(1024, WIDE)
        )
        lane = lax.broadcasted_iota(jnp.int32, (256, WIDE), 1)
        downs = jnp.where(lane == gain_lane, weighed, downs)
        r.gf.at[b, :, :, :, 2 * WIDE :][...] = downs.astype(BF16).reshape(shape)
        return 0

    lax.fori_loop(0, 4, feed_grads, 0)
    sum_f = PlaneSum("f")
    sum_f.start()

    def down_out(i):
        zz = lax.rem(z - i + 4, 4)
        scatter_y.put(i, mt(r.act.at[pl.ds(4 * zz, 4)][...].reshape(256, WIDE), w_down))

    e2 = scatter2.total()
    unit2 = r.unit2[...]
    grad_hidden = r.g[...].astype(F32) + r.r2[...] * (
        e2 - unit2 * jnp.mean(e2 * unit2, axis=-1, keepdims=True)
    )
    r.gh[...] = grad_hidden
    branch = grad_hidden.astype(BF16)
    r.db.at[z, e][...] = branch
    d_mixed = mt(branch[:, :512], r.wo[0].reshape(1024, 512)) + mt(
        branch[:, 512:], r.wo[1].reshape(1024, 512)
    )
    for s in range(8):
        r.dmixb[s // 2, s % 2] = d_mixed[:, s * 128 : (s + 1) * 128].astype(BF16)
    came_mix = links.landing()
    for i in NEAR:
        to = along_z(i)
        for to_e, peer in ((1 - e, other_core(to)), (e, to)):
            if i or peer is not to:
                src = r.dmixb.at[to["z"], to_e]
                links.go(src, r.dmix.at[z, e], peer, came_mix)
    r.dmix.at[z, e][...] = r.dmixb.at[z, e][...]

    gather_b = Gather(r.db)
    gather_b.start()
    for at, i in enumerate(NEAR):
        down_out(i)

    def out_grads():
        grads = tm(r.mixb[...].reshape(1024, 128), r.db[...].reshape(1024, 1024))
        grads = grads.astype(BF16)
        for j in range(2):
            for k in range(8):
                r.go[j, k] = grads[j * 64 : (j + 1) * 64, k * 128 : (k + 1) * 128]
        land = links.landing()
        for n, d in enumerate(plane):
            to = in_plane(*d)
            src = r.go.at[to["xh"], to["xl"] * 4 + to["y"]]
            links.go(src, r.gor.at[n], to, land)
        return land

    for p in range(4):
        r.kt[p] = r.kv[p, :, 0].reshape(512, 128).T

    links.arrived(r.gor.at[pl.ds(0, 14)], partner, came_mix)
    r.dkv[...] = jnp.zeros((4, 2, 256, 256), F32)
    dkv_slots, dkv_land = links.fixed_slots(4), links.landing(4)

    def dkv_copy(zz):
        return links.make(
            r.dkvs.at[zz], r.dkvr.at[zz], across, dkv_slots + zz, dkv_land + zz
        )

    def give(zz):
        both = r.dkv.at[zz, 1 - xh][...].astype(BF16)
        r.dkvs.at[zz, 0][...] = both[:, :128]
        r.dkvs.at[zz, 1][...] = both[:, 128:]
        dkv_copy(zz).start()

    def attend_back(qi):
        queries = halves(r.q[qi])
        grads = r.dmix[qi].reshape(256, 128)
        product = (grads.astype(F32) * r.mix[qi]).T
        grads = halves(grads)
        dots = [jnp.sum(product[k : k + HD], axis=0, keepdims=True) for k in (0, HD)]
        logs = r.lse[qi].T
        logs = [logs[k : k + 1] for k in (0, HD)]
        query_ids = r.ids.at[2 * qi + xh][...].astype(F32)
        def one(p, tiles, masked):
            wide = 256 * tiles
            keys, values = (
                r.kv.at[p, pl.ds(0, tiles), k][...].reshape(wide, 128) for k in range(2)
            )
            keys_turned = r.kt.at[p, :, pl.ds(0, wide)][...]
            d_key, d_value = 0.0, 0.0
            for h in range(2):
                score = mt(keys, queries[h])
                if masked:
                    _, key_ids = ids_of(pair_ids(p)[:, :wide])
                    score = jnp.where(key_ids <= query_ids, score, -1e30)
                prob = jnp.exp(score - logs[h])
                d_score = (prob * (mt(values, grads[h]) - dots[h])).astype(BF16)
                d_value += mm(prob.astype(BF16), grads[h])
                d_key += mm(d_score, queries[h])
                r.dqt[h * HD : (h + 1) * HD] += mm(
                    keys_turned[h * HD : (h + 1) * HD], d_score
                )
            both = jnp.concatenate([d_key, d_value], axis=1).reshape(tiles, 256, 256)
            r.dkv.at[p, pl.ds(0, tiles)][...] += both

        r.dqt[...] = jnp.zeros((128, 256), F32)
        key_tiles(qi, one)
        r.dq[qi] = (r.dqt[...] * 0.125).T
        if qi < 3:
            give(qi + 1)

    attend_back(3)
    for i in NEAR[1:]:
        scatter_y.send(i)
    sum_f.middle()
    attend_back(2)
    r.sf[...] = jnp.concatenate(sum_f.last(), axis=-1).astype(BF16)
    land_sf = links.landing()
    for i in (2, 1, 3):
        to = along_z(i)
        links.go(r.sf.at[to["z"]], r.zf.at[z], to, land_sf)
    r.zf.at[z][...] = r.sf.at[z][...]
    gather_b.pass_on()
    attend_back(1)
    gather_b.ready()
    sum_o = out_grads()
    attend_back(0)
    give(0)
    links.arrived(r.zf.at[pl.ds(0, 3)], partner, land_sf)
    out_f = StagedOut(r.zf, r.ff, r.relay)
    out_f.start()

    scatter1 = Scatter("e1")
    scatter1.slots = links.fixed_slots(4)
    for zz in (3, 2, 1, 0):
        dkv_copy(zz).wait_recv()
        cosine, sine = r.cos[zz], -r.sin[zz]
        d_tile = r.dkv.at[zz, xh][...]
        d_key = d_tile[:, :128] + r.dkvr[zz, 0].astype(F32)
        d_value = d_tile[:, 128:] + r.dkvr[zz, 1].astype(F32)
        r.dqkv[zz] = jnp.concatenate(
            [
                turn(r.dq[zz], cosine, sine).astype(BF16),
                turn(d_key, cosine, sine).astype(BF16),
                d_value.astype(BF16),
            ],
            axis=1,
        )

    def attn_gains(rows):
        at = GATE + WIDE + 256
        last = rows[..., at : at + 128]
        return last.reshape(-1, 128).astype(F32)[:, gain_lane - 256 : gain_lane - 255]

    def qkv_grads(b, _):
        cols = pl.ds(pl.multiple_of(b * 256, 256), 256)
        grads = mm(r.u1t[cols, :], r.dqkv[...].reshape(1024, 384))
        rows = r.w.at[lax.div(b, 2), pl.ds(2 * lax.rem(b, 2), 2)]
        r.gq.at[b][...] = (grads * attn_gains(rows)).astype(BF16).reshape(4, 64, 384)
        return 0

    lax.fori_loop(0, 4, qkv_grads, 0)
    sum_q = PlaneSum("q")
    sum_q.start()
    for zz in (3, 2, 1, 0):
        scatter1.tile(zz, mt(r.dqkv[zz], w_qkv))
        if zz < 3:
            scatter1.tile_send(zz + 1)
    scatter1.tile_send(0)
    out_f.pass_on()
    sum_q.middle()
    r.y[...] = (r.hidden[...] + scatter_y.total()).astype(BF16)
    write("y")

    total = r.go.at[xh, grp][...].astype(F32)
    links.arrived(r.gor, partner, sum_o)
    for n in range(15):
        total = total + r.gor[n].astype(F32)
    r.so[...] = total.astype(BF16)
    done_o = hand_out(r.so, r.fo, grp, head_self, lambda at: {**at, "xh": e, "e": xh})
    summed = jnp.concatenate(sum_q.last(), axis=-1)
    block = 4 * y + x
    rows = r.w.at[lax.div(block, 8), lax.rem(lax.div(block, 2), 4), pl.ds(2 * lax.rem(block, 2), 2)]
    gain = attn_gains(rows)
    weights = rows[:, :, :, :GATE].reshape(64, GATE).astype(F32)
    weighed = jnp.sum(weights * summed, axis=1, keepdims=True) / (gain * gain)
    r.sq[:, :GATE] = summed.astype(BF16)
    r.sq[:, GATE:] = jnp.broadcast_to(weighed, (64, 128)).astype(BF16)
    done_q = hand_out(r.sq, r.fq, z * 2 + e, row_self, lambda at: {**at, "z": y, "e": xl})
    e1 = scatter1.total(True)
    rows = r.x[...].astype(F32)
    r1 = lax.rsqrt(jnp.mean(rows * rows, axis=-1, keepdims=True) + EPS)
    unit1 = rows * r1
    r.gx[...] = r.gh[...] + r1 * (
        e1 - unit1 * jnp.mean(e1 * unit1, axis=-1, keepdims=True)
    )
    write("gx")

    def rows_of(landed, s):
        pieces = [landed[2 * k + s % 2, s // 2] for k in range(4)]
        return jnp.concatenate(pieces, axis=0).astype(F32)

    out_f.finish()
    r.feeds[...] = jnp.zeros((3, 64, FEED), BF16)
    lane = lax.broadcasted_iota(jnp.int32, (64, WIDE), 1)
    for s in range(8):
        part = rows_of(r.ff, s)
        start, many, rest = window(s)
        for n in range(3):
            piece = jnp.where(lane < SLICE, part[:, n * WIDE : (n + 1) * WIDE], 0.0)
            if many > WIDE:
                piece = jnp.concatenate([piece, jnp.zeros((64, 128), F32)], axis=1)
            if rest:
                piece = pltpu.roll(piece, rest, 1)
            r.feeds[n, :, start : start + many] += piece.astype(BF16)
        weighed = part[:, 2 * WIDE + SLICE : 2 * WIDE + SLICE + 1]
        gain_mlp = weighed + (gain_mlp if s else 0.0)
    write("feeds")
    done_o()
    for k in range(8):
        r.heads[3, :, k * 128 : (k + 1) * 128] = r.fo[k]
    done_q()
    for s in range(8):
        part = r.fq[s].astype(F32)
        for n in range(3):
            piece = part[:, n * 128 : (n + 1) * 128]
            r.heads[n, :, s * 128 : (s + 1) * 128] = piece.astype(BF16)
        gain_attn = part[:, 384:] + (gain_attn if s else 0.0)
    lane = lax.broadcasted_iota(jnp.int32, (64, 128), 1)
    r.grad_gains[...] = jnp.where(lane == 0, gain_attn, gain_mlp)
    write("heads")
    write("grad_gains")
    for zz in range(4):
        mix_copy(zz, 1).wait_send()
        pl.when(z != zz)(lambda: mix_copy(zz, 0).wait_send())
        dkv_copy(zz).wait_send()
        pl.when(z != zz)(lambda: scatter1.tile_copy(zz).wait_send())
    for at in range(len(links.started) - RING, len(links.started)):
        links.left(at)
    for copy in written:
        copy.wait()
    counts = links.fixed, links.landings, links.count_near
    assert counts == (SENDS, LANDINGS, LOCAL), counts


def rope_tables():
    positions = np.arange(2048, dtype=np.float32)[:, None]
    frequency = np.float32(10000.0) ** (
        np.float32(-2.0) * np.arange(32, dtype=np.float32) / np.float32(64)
    )
    angles = positions * frequency.astype(np.float32)[None, :]
    cosine, sine = np.cos(angles), np.sin(angles)
    cosines = np.concatenate([cosine] * 4, axis=1)
    sines = np.concatenate([-sine, sine, -sine, sine], axis=1)
    shape = (4, 2, 256, 128)
    return cosines.astype(np.float32).reshape(shape), sines.astype(np.float32).reshape(shape)


def per_device(
    tokens,
    blocks,
    w_query,
    w_key,
    w_value,
    w_out,
    w_gate,
    w_up,
    w_down,
    norm_attn,
    norm_mlp,
    cotangent,
):
    gains = jnp.stack([norm_attn, norm_mlp], axis=1)
    extra = jnp.concatenate([w_down.T, jnp.pad(gains, ((0, 0), (0, 126)))], axis=1).astype(F32)
    cosines, sines = rope_tables()
    anywhere = pl.BlockSpec(memory_space=pl.ANY)
    y, gx, heads, feeds, gains = pl.pallas_call(
        kernel,
        out_shape=[jax.ShapeDtypeStruct(*spec) for spec in OUTPUTS.values()],
        in_specs=[anywhere] * len(INPUTS),
        out_specs=[anywhere] * len(OUTPUTS),
        scratch_shapes=[pltpu.VMEM(*spec) for spec in HELD.values()]
        + [
            pltpu.SemaphoreType.DMA((SENDS,)),
            pltpu.SemaphoreType.DMA((LANDINGS,)),
            pltpu.SemaphoreType.DMA((LOCAL,)),
        ],
        compiler_params=pltpu.CompilerParams(
            collective_id=0, has_side_effects=True, vmem_limit_bytes=63 * 2**20
        ),
    )(
        tokens[0],
        cotangent[0],
        w_query,
        w_key,
        w_value,
        w_out,
        w_gate,
        w_up,
        extra,
        blocks.reshape(8, 1, 256),
        jnp.asarray(cosines),
        jnp.asarray(sines),
    )

    return (
        y[None],
        gx[None],
        *[heads[n].astype(F32) for n in range(4)],
        feeds[0].astype(F32),
        feeds[1].astype(F32),
        feeds[2].astype(F32).T,
        gains[:, 0],
        gains[:, 1],
    )


def solution(mesh):
    both = ("grp", "ctx")
    row = P(both, None)
    tokens = P("grp", "ctx", None)
    shard = P("ctx", None)
    return jax.shard_map(
        per_device,
        mesh=mesh,
        in_specs=(
            tokens,
            P("grp", None),
            *[row] * 6,
            P(None, both),
            P(both),
            P(both),
            tokens,
        ),
        out_specs=(tokens, tokens, *[shard] * 6, P(None, "ctx"), P("ctx"), P("ctx")),
        check_vma=False,
    )
```

```python
import functools
import types

import jax
import jax.numpy as jnp
import numpy as np
from jax import lax
from jax.experimental import pallas as pl
from jax.experimental.pallas import tpu as pltpu
from jax.sharding import PartitionSpec as P

MESH = pl.DeviceIdType.MESH
F32 = jnp.float32
BF16 = jnp.bfloat16
EPS = 1e-05
HD = 64
SLICE = 352
WIDE = 384
QKV, GATE, DOWN, OUT = 0, 384, 1152, 1536
NEAR = (0, 1, 3, 2)


def mm(left, right):
    return jnp.dot(left, right, preferred_element_type=F32)


def mt(left, right):
    return lax.dot_general(left, right, (((1,), (1,)), ((), ())), preferred_element_type=F32)


def tm(left, right):
    return lax.dot_general(left, right, (((0,), (0,)), ((), ())), preferred_element_type=F32)


def window(s):
    rest = s * SLICE % 128
    return s * SLICE - rest, WIDE if rest + SLICE <= WIDE else WIDE + 128, rest


def turn(values, cosine, sine):
    lane = lax.broadcasted_iota(jnp.int32, values.shape, 1)
    ahead = pltpu.roll(values, 96, 1)
    behind = pltpu.roll(values, 32, 1)
    return values * cosine + jnp.where(lax.rem(lane, 64) < 32, ahead, behind) * sine


HELD = dict(
    wsrc=((2, 8, 6656), F32),
    ff=((8, 4, 16, 1152), BF16),
    fq=((8, 64, 512), BF16),
    sq=((64, 512), BF16),
    sf=((4, 16, 1152), BF16),
    zf=((4, 16, 1152), BF16),
    fo=((8, 64, 128), BF16),
    relay=((4, 16, 1152), BF16),
    pair=((16, 6656), F32),
    wz=((4, 16, 2048), BF16),
    wrow=((4, 16, 2048), BF16),
    w=((2, 4, 4, 2, 16, 1536), BF16),
    wo=((2, 2, 4, 4, 2, 16, 512), BF16),
    u1=((4, 2, 128, 1024), BF16),
    gg=((4, 2, 128, 1024), BF16),
    u2=((4, 2, 128, 1024), BF16),
    db=((4, 2, 128, 1024), BF16),
    cos=((4, 256, 128), F32),
    sin=((4, 256, 128), F32),
    q=((4, 256, 128), BF16),
    kv=((4, 2, 2, 256, 128), BF16),
    score=((2, 4, 256, 512), F32),
    kt=((4, 128, 512), BF16),
    u1t=((1024, 1024), BF16),
    dkv=((4, 2, 256, 256), F32),
    top=((2, 256, 128), F32),
    acc=((2, 256, 128), F32),
    mix=((4, 256, 128), F32),
    mixb=((4, 2, 128, 128), BF16),
    mixin=((4, 2, 128, 128), BF16),
    lse=((4, 256, 128), F32),
    hidden=((128, 1024), F32),
    unit2=((128, 1024), F32),
    r2=((128, 1), F32),
    dgu=((4, 256, 2 * WIDE), BF16),
    act=((16, 64, WIDE), BF16),
    gh=((128, 1024), F32),
    dmixb=((4, 2, 128, 128), BF16),
    dmix=((4, 2, 128, 128), BF16),
    dq=((4, 256, 128), F32),
    dqt=((128, 256), F32),
    dkvs=((4, 2, 256, 128), BF16),
    dkvr=((4, 2, 256, 128), BF16),
    dqkv=((4, 256, 384), BF16),
    go=((2, 8, 64, 128), BF16),
    gor=((15, 64, 128), BF16),
    so=((64, 128), BF16),
)
for kind in ("e2", "out", "e1"):
    HELD[kind + "p"] = ((4, 2, 128, 1024), BF16)
    HELD[kind + "d"] = ((4, 128, 1024), BF16)
    HELD[kind + "r"] = ((3, 128, 1024), BF16)
SPLIT = {"f": (512, 640), "q": (256, 128)}
ROWS = {"f": (4, 4, 4, 16), "q": (4, 4, 64)}
for kind, (by_x, by_y) in SPLIT.items():
    HELD["g" + kind] = (ROWS[kind] + (by_x + by_y,), BF16)
    one, two = ((4, 4, 16), (4, 16)) if kind == "f" else ((4, 64), (64,))
    for axis, width in (("x", by_x), ("y", by_y)):
        HELD["r1" + axis + kind] = ((3,) + one + (width,), BF16)
        HELD["r2" + axis + kind] = ((3,) + two + (width,), BF16)
INPUTS = dict(
    x=((128, 1024), BF16),
    g=((128, 1024), BF16),
    wq=((8, 1024), BF16),
    wk=((8, 1024), BF16),
    wv=((8, 1024), BF16),
    wo8=((8, 1024), BF16),
    wg=((8, 8 * SLICE), BF16),
    wu=((8, 8 * SLICE), BF16),
    extra=((8, 8 * SLICE + 128), F32),
    ids=((8, 1, 256), jnp.int32),
    cosines=((4, 2, 256, 128), F32),
    sines=((4, 2, 256, 128), F32),
)
TABLES = ("cosines", "sines")
FEED = 8 * SLICE
OUTPUTS = dict(
    y=((128, 1024), BF16),
    gx=((128, 1024), F32),
    heads=((4, 64, 1024), BF16),
    feeds=((3, 64, FEED), BF16),
    grad_gains=((8, 128), F32),
)
for given in (INPUTS, OUTPUTS):
    HELD.update({name: spec for name, spec in given.items() if name not in TABLES})
RING, SENDS, LANDINGS, LOCAL = 48, 81, 68, 20


def device(at):
    return (at["xl"] * 4 + at["y"], at["z"] * 4 + at["xh"] * 2 + at["e"])


class Links:
    def __init__(self, send, recv, near):
        self.send, self.recv, self.near = send, recv, near
        self.fixed, self.landings, self.count_near = RING, 0, 0
        self.started = []

    def fixed_slots(self, many):
        self.fixed += many
        return self.fixed - many

    def landing(self, many=1):
        self.landings += many
        return self.landings - many

    def make(self, src, dst, peer, slot, land):
        return pltpu.make_async_remote_copy(
            src_ref=src,
            dst_ref=dst,
            send_sem=self.send.at[slot],
            recv_sem=self.recv.at[land],
            device_id=device(peer),
            device_id_type=MESH,
        )

    def go(self, src, dst, peer, land=None):
        at = len(self.started)
        if at >= RING:
            self.left(at - RING)
        copy = self.make(src, dst, peer, at % RING, self.landing() if land is None else land)
        copy.start()
        self.started.append(copy)
        return copy

    def left(self, at):
        if self.started[at] is not None:
            self.started[at].wait_send()
            self.started[at] = None

    def arrived(self, like, peer, land):
        self.make(like, like, peer, 0, land).wait_recv()

    def here(self, src, dst):
        copy = pltpu.make_async_copy(src, dst, self.near.at[self.count_near])
        self.count_near += 1
        copy.start()
        return copy


def kernel(*refs):
    n_in, n_out = len(INPUTS), len(OUTPUTS)
    given = dict(zip(INPUTS, refs[:n_in]))
    result = dict(zip(OUTPUTS, refs[n_in : n_in + n_out]))
    held = dict(zip(HELD, refs[n_in + n_out : n_in + n_out + len(HELD)]))
    r = types.SimpleNamespace(**held)
    links = Links(*refs[n_in + n_out + len(HELD) :])
    grp, ctx = lax.axis_index("grp"), lax.axis_index("ctx")
    me = {
        "xl": lax.div(grp, 4),
        "y": lax.rem(grp, 4),
        "z": lax.div(ctx, 4),
        "xh": lax.rem(lax.div(ctx, 2), 2),
        "e": lax.rem(ctx, 2),
    }
    xl, y, z, xh, e = (me[k] for k in ("xl", "y", "z", "xh", "e"))
    x = xh * 2 + xl

    def other_core(at):
        return {**at, "e": 1 - at["e"]}

    def along_z(by):
        return {**me, "z": lax.rem(z + by + 4, 4)}

    def in_plane(dx, dy):
        to = lax.rem(x + dx, 4)
        return {**me, "xl": lax.rem(to, 2), "xh": lax.div(to, 2), "y": lax.rem(y + dy, 4)}

    def group(dxl, dy):
        return {**me, "xl": lax.rem(xl + dxl, 2), "y": lax.rem(y + dy, 4)}

    partner = other_core(me)
    across = in_plane(2, 0)
    plane = sorted(
        ((dx, dy) for dx in range(4) for dy in range(4) if dx or dy),
        key=lambda d: -min(d[0], 4 - d[0]) - min(d[1], 4 - d[1]),
    )
    groups = [(dxl, dy) for dxl in range(2) for dy in range(4)]

    came_in = {
        name: links.here(given[name], held[name]) for name in INPUTS if name not in TABLES
    }
    written = []

    def write(name):
        written.append(links.here(held[name], result[name]))

    sem = pltpu.get_barrier_semaphore()

    def greet(peer):
        pl.semaphore_signal(sem, inc=1, device_id=device(peer), device_id_type=MESH)

    row_self = jnp.logical_and(z == y, xl == e)
    head_self = xh == e
    peers = [partner] + [along_z(i) for i in (1, 2, 3)] + [other_core(along_z(i)) for i in (1, 2, 3)]
    peers += [in_plane(*d) for d in plane]
    peers += [other_core(group(0, dy)) for dy in (1, 2, 3)]
    for peer in peers:
        greet(peer)
    for d in groups:
        by_head = {**group(*d), "xh": e, "e": xh}
        by_row = {**me, "xl": e, "y": z, "z": lax.rem(z + d[1], 4), "e": lax.rem(e + d[0], 2)}
        for own, source in ((row_self, by_row), (head_self, by_head)):
            if d != (0, 0):
                greet(source)
            else:
                pl.when(jnp.logical_not(own))(functools.partial(greet, source))
    others = 16 - row_self.astype(jnp.int32) - head_self.astype(jnp.int32)
    tables = [
        links.here(given["cosines"].at[:, xh], r.cos),
        links.here(given["sines"].at[:, xh], r.sin),
    ]
    for copy in came_in.values():
        copy.wait()
    extra = r.extra[...]
    gains = {"attn": extra[:, FEED : FEED + 1], "mlp": extra[:, FEED + 1 : FEED + 2]}
    lane = lax.broadcasted_iota(jnp.int32, (8, WIDE), 1)
    wide = {
        GATE: (r.wg[...].astype(F32) * gains["mlp"], gains["mlp"]),
        GATE + WIDE: (r.wu[...].astype(F32) * gains["mlp"], gains["attn"]),
        DOWN: (extra[:, :FEED], 0.0),
    }
    narrow = [w[...].astype(F32) * gains["attn"] for w in (r.wq, r.wk, r.wv)]
    for s in range(8):
        base = s // 2 * OUT
        for n, whole in enumerate(narrow):
            part = whole[:, s * 128 : (s + 1) * 128]
            r.wsrc[s % 2, :, base + n * 128 : base + (n + 1) * 128] = part
        start, many, rest = window(s)
        for at, (whole, fill) in wide.items():
            part = whole[:, start : start + many]
            if rest:
                part = pltpu.roll(part, many - rest, 1)[:, :WIDE]
            part = jnp.where(lane < SLICE, part, jnp.where(lane == SLICE, fill, 0.0))
            r.wsrc[s % 2, :, base + at : base + at + WIDE] = part
    for h in range(2):
        r.wsrc[h, :, 4 * OUT :] = r.wo8[:, h * 512 : (h + 1) * 512].astype(F32)
    own_rows = pl.ds(pl.multiple_of(e * 8, 8), 8)
    r.pair[own_rows, :] = r.wsrc.at[e][...]

    rows = r.x[...].astype(F32)
    r1 = lax.rsqrt(jnp.mean(rows * rows, axis=-1, keepdims=True) + EPS)
    r.u1.at[z, e][...] = (rows * r1).astype(BF16)
    r.gg.at[z, e][...] = r.g[...]
    pl.semaphore_wait(sem, len(peers) + others)

    class Gather:
        def __init__(self, buf):
            self.buf = buf
            self.land = links.landing(2)

        def start(self):
            mine = self.buf.at[z, e]
            for i in (2, 1, 3):
                links.go(mine, mine, along_z(i), self.land)
            links.go(mine, mine, partner, self.land + 1)

        def pass_on(self):
            links.arrived(self.buf.at[pl.ds(0, 3), 0], partner, self.land)
            for i in (1, 2, 3):
                block = self.buf.at[lax.rem(z + i, 4), e]
                links.go(block, block, partner, self.land + 1)

        def ready(self):
            links.arrived(self.buf.at[:, 0], partner, self.land + 1)

    class QuickGather:
        def __init__(self, buf):
            self.buf = buf
            self.out = {0: None}
            self.over = {}

        def start(self):
            mine = self.buf.at[z, e]
            for i in (1, 3):
                self.out[i] = links.go(mine, mine, along_z(i))
            self.over[0] = links.go(mine, mine, partner)
            self.land = links.landing()

        def pass_on(self, i):
            block = self.buf.at[lax.rem(z - i + 4, 4), e]
            if i == 2:
                links.arrived(block, partner, self.land)
            else:
                self.out[i].wait_recv()
                half = block.at[pl.ds(0 if i == 1 else 64, 64)]
                links.go(half, half, along_z(i), self.land)
            self.over[i] = links.go(block, block, partner)

        def ready(self, i):
            self.over[i].wait_recv()

    class Scatter:
        def __init__(self, kind):
            self.p, self.d, self.r = (held[kind + k] for k in "pdr")
            self.over = {}
            self.land = links.landing()

        def put(self, i, value):
            zz = lax.rem(z - i + 4, 4)
            self.p.at[zz][...] = value.astype(BF16).reshape(2, 128, 1024)
            self.over[i] = links.go(self.p.at[zz, 1 - e], self.d.at[zz], partner)

        def send(self, i):
            zz = lax.rem(z - i + 4, 4)
            if i:
                self.over[i].wait_recv()
                mine = self.p.at[zz, e]
                mine[...] = (mine[...].astype(F32) + self.d.at[zz][...].astype(F32)).astype(BF16)
                links.go(mine, self.r.at[i - 1], along_z(-i), self.land)

        def tile(self, zz, value):
            self.p[zz] = value.astype(BF16).reshape(2, 128, 1024)
            self.over[zz] = links.go(self.p.at[zz, 1 - e], self.d.at[zz], partner)

        def tile_copy(self, zz):
            by = lax.rem(z - zz + 4, 4)
            there = self.r.at[jnp.maximum(by - 1, 0)]
            return links.make(
                self.p.at[zz, e], there, {**me, "z": zz}, self.slots + zz, self.land
            )

        def tile_send(self, zz):
            self.over[zz].wait_recv()

            def away():
                mine = self.p.at[zz, e]
                mine[...] = (mine[...].astype(F32) + self.d[zz].astype(F32)).astype(BF16)
                self.tile_copy(zz).start()

            pl.when(z != zz)(away)

        def total(self, waited=False):
            if not waited:
                self.over[0].wait_recv()
            result = self.p.at[z, e][...].astype(F32) + self.d.at[z][...].astype(F32)
            links.arrived(self.r, partner, self.land)
            for i in range(3):
                result = result + self.r[i].astype(F32)
            return result

    class Spread:
        def __init__(self, buf, along_x, along_y):
            self.own = [buf.at[xl, y, :, xh, :, along_x], buf.at[xl, y, :, xh, :, along_y]]
            self.line = [buf.at[:, y, :, :, :, along_x], buf.at[xl, :, :, xh, :, along_y]]
            three, both = pl.ds(0, 3), (along_x, along_y)
            self.three_own = [buf.at[0, three, :, 0, :, cols] for cols in both]
            self.three_lines = [buf.at[:, three, :, :, :, cols] for cols in both]
            self.land = links.landing(4)

        def start(self):
            for d in (2, 1, 3):
                links.go(self.own[0], self.own[0], in_plane(d, 0), self.land)
                links.go(self.own[1], self.own[1], in_plane(0, d), self.land + 1)

        def pass_on(self, k):
            links.arrived(self.three_own[k], partner, self.land + k)
            for d in (2, 1, 3):
                to = in_plane(d, 0) if k else in_plane(0, d)
                links.go(self.line[k], self.line[k], to, self.land + 2 + k)

        def wait(self):
            for k in range(2):
                links.arrived(self.three_lines[k], partner, self.land + 2 + k)

    class PlaneSum:
        def __init__(self, kind):
            self.by_x = pl.ds(0, SPLIT[kind][0])
            self.by_y = pl.ds(*SPLIT[kind])
            self.g = held["g" + kind]
            self.one = held["r1x" + kind], held["r1y" + kind]
            self.two = held["r2x" + kind], held["r2y" + kind]
            self.feed = kind == "f"
            self.land = links.landing(4)

        def part(self, at_x, at_y, cols):
            if self.feed:
                return self.g.at[:, at_x, at_y, :, cols]
            return self.g.at[at_y, at_x, :, cols]

        def start(self):
            every = slice(None)
            for d in (2, 1, 3):
                there = self.part(lax.rem(x + d, 4), every, self.by_x)
                links.go(there, self.one[0].at[d - 1], in_plane(d, 0), self.land)
                there = self.part(every, lax.rem(y + d, 4), self.by_y)
                links.go(there, self.one[1].at[d - 1], in_plane(0, d), self.land + 1)

        def add(self, mine, landed):
            result = mine[...].astype(F32)
            for d in range(3):
                result = result + landed[d].astype(F32)
            return result

        def middle(self):
            every = slice(None)
            for k in range(2):
                links.arrived(self.one[k], partner, self.land + k)
            mine = self.part(x, every, self.by_x)
            mine[...] = self.add(mine, self.one[0]).astype(BF16)
            mine = self.part(every, y, self.by_y)
            mine[...] = self.add(mine, self.one[1]).astype(BF16)
            for d in (2, 1, 3):
                there = self.part(x, lax.rem(y + d, 4), self.by_x)
                links.go(there, self.two[0].at[d - 1], in_plane(0, d), self.land + 2)
                there = self.part(lax.rem(x + d, 4), y, self.by_y)
                links.go(there, self.two[1].at[d - 1], in_plane(d, 0), self.land + 3)

        def last(self):
            for k in range(2):
                links.arrived(self.two[k], partner, self.land + 2 + k)
            return [
                self.add(self.part(x, y, cols), landed)
                for cols, landed in zip((self.by_x, self.by_y), self.two)
            ]

    class StagedOut:
        def __init__(self, src, dst, relay):
            self.src, self.dst, self.relay = src, dst, relay
            self.slot = y * 2 + e
            self.land = links.landing(2)
            self.fixed = links.fixed_slots(1)
            self.near = links.near.at[links.count_near]
            links.count_near += 1

        def along_y(self, src, at_e):
            mine = self.dst.at[self.slot]
            for dy in (2, 1, 3):
                links.go(src, mine, {**group(0, dy), "e": at_e}, self.land + 1)
            near = pltpu.make_async_copy(src, mine, self.near)
            over = links.make(src, mine, partner, self.fixed, self.land + 1)
            pl.when(e == at_e)(near.start)
            pl.when(e != at_e)(over.start)
            return near, over

        def start(self):
            links.go(self.src, self.relay, group(1, 0), self.land)
            self.along_y(self.src, xl)

        def pass_on(self):
            links.arrived(self.relay, partner, self.land)
            self.local = self.along_y(self.relay, 1 - xl)

        def finish(self):
            near, over = self.local
            near.wait()
            over.wait_send()
            links.arrived(self.dst.at[pl.ds(0, 7)], partner, self.land + 1)

    def hand_out(src, dst, slot, self_is, place):
        first, land = links.fixed_slots(8), links.landing()
        mine = dst.at[slot]
        copies = [
            links.make(src, mine, place(group(*d)), first + n, land)
            for n, d in enumerate(groups)
        ]
        near = pltpu.make_async_copy(src, mine, links.near.at[links.count_near])
        links.count_near += 1
        for copy in copies[1:]:
            copy.start()
        pl.when(self_is)(near.start)
        pl.when(jnp.logical_not(self_is))(copies[0].start)

        def finish():
            def with_own():
                near.wait()
                links.arrived(dst.at[pl.ds(0, 7)], partner, land)

            def without():
                copies[0].wait_send()
                links.arrived(dst, partner, land)

            pl.when(self_is)(with_own)
            pl.when(jnp.logical_not(self_is))(without)
            for copy in copies[1:]:
                copy.wait_send()

        return finish

    swap = links.go(r.wsrc.at[1 - e], r.pair.at[own_rows, :], partner)
    swap.wait_recv()
    for zz in range(4):
        r.wz[zz, :, :OUT] = r.pair[:, zz * OUT : (zz + 1) * OUT].astype(BF16)
        r.wz[zz, :, OUT:] = r.pair[:, 4 * OUT :].astype(BF16)
    land = links.landing()
    for i in (2, 1, 3):
        links.go(r.wz.at[lax.rem(z + i, 4)], r.wrow.at[z], along_z(i), land)
    gather1 = Gather(r.u1)
    gather1.start()
    r.wrow.at[z][...] = r.wz.at[z][...]
    links.arrived(r.wrow.at[pl.ds(0, 3)], partner, land)
    r.w.at[xl, y, :, xh][...] = r.wrow[:, :, :OUT]
    r.wo.at[e, xl, y, :, xh][...] = r.wrow[:, :, OUT:]
    spread_qkv = Spread(r.w, pl.ds(QKV, 128), pl.ds(QKV + 128, 256))
    spread_out = Spread(r.wo.at[e], pl.ds(0, 384), pl.ds(384, 128))
    spread_feed = Spread(r.w, pl.ds(GATE, 768), pl.ds(GATE + 768, 384))
    for spread in (spread_qkv, spread_out, spread_feed):
        spread.start()
    spread_qkv.pass_on(0)
    spread_qkv.pass_on(1)
    gather1.pass_on()
    spread_out.pass_on(0)
    spread_feed.pass_on(0)
    gather_g = Gather(r.gg)
    gather_g.start()
    for copy in tables:
        copy.wait()
    gather1.ready()
    spread_qkv.wait()

    w_qkv = r.w[:, :, :, :, :, QKV:GATE].reshape(1024, GATE - QKV)
    came_kv = []
    for zz in range(4):
        qkv = mm(r.u1[zz].reshape(256, 1024), w_qkv)
        cosine, sine = r.cos[zz], r.sin[zz]
        r.kv.at[zz, xh, 0][...] = turn(qkv[:, 128:256], cosine, sine).astype(BF16)
        r.kv.at[zz, xh, 1][...] = qkv[:, 256:].astype(BF16)
        tile = r.kv.at[zz, xh]
        came_kv.append(links.go(tile, tile, across))
        r.q[zz] = (turn(qkv[:, :128], cosine, sine).astype(BF16) * 0.125).astype(BF16)

    first = lax.broadcasted_iota(jnp.int32, (256, 128), 1) < HD

    def halves(pair):
        zero = jnp.zeros_like(pair)
        return jnp.where(first, pair, zero), jnp.where(first, zero, pair)

    def ids_of(row):
        row = row.astype(F32)
        return row, jnp.broadcast_to(row, (128, row.shape[1])).T[:, :1]

    def pair_ids(p):
        return jnp.concatenate([r.ids[2 * p], r.ids[2 * p + 1]], axis=1)

    def key_tiles(qi, body):
        def whole(p, _):
            body(p, 2, False)
            return 0

        if qi:
            lax.fori_loop(0, qi, whole, 0)
        body(qi, 2, True)
        if qi < 3:
            pl.when(xh == 1)(lambda: body(qi + 1, 1, True))

    mix_slots, mix_land = links.fixed_slots(8), links.landing(2)

    def mix_copy(qi, far):
        at_e = 1 - e if far else e
        to = {**me, "z": qi, "e": at_e}
        src = r.mixb.at[qi, at_e]
        return links.make(
            src, r.mixin.at[z, e], to, mix_slots + 2 * qi + far, mix_land + far
        )

    def attend(qi):
        queries = halves(r.q[qi])
        _, query_ids = ids_of(r.ids.at[2 * qi + xh][...])
        r.top[...] = jnp.full((2, 256, 128), -3e38, F32)

        def one(p, tiles, masked):
            wide = 256 * tiles
            keys = r.kv.at[p, pl.ds(0, tiles), 0][...].reshape(wide, 128)
            for h in range(2):
                score = mt(queries[h], keys)
                if masked:
                    seen = pair_ids(p)[:, :wide].astype(F32) <= query_ids
                    score = jnp.where(seen, score, -1e30)
                r.score.at[h, p, :, pl.ds(0, wide)][...] = score
                top = r.top[h]
                for k in range(wide // 128):
                    top = jnp.maximum(top, score[:, k * 128 : (k + 1) * 128])
                r.top[h] = top

        key_tiles(qi, one)
        tops = [jnp.max(r.top[h], axis=1, keepdims=True) for h in range(2)]
        r.top[...] = jnp.zeros((2, 256, 128), F32)
        r.acc[...] = jnp.zeros((2, 256, 128), F32)

        def two(p, tiles, masked):
            wide = 256 * tiles
            values = r.kv.at[p, pl.ds(0, tiles), 1][...].reshape(wide, 128)
            for h in range(2):
                weight = jnp.exp(r.score.at[h, p, :, pl.ds(0, wide)][...] - tops[h])
                total = r.top[h]
                for k in range(wide // 128):
                    total = total + weight[:, k * 128 : (k + 1) * 128]
                r.top[h] = total
                r.acc[h] += mm(weight.astype(BF16), values)

        key_tiles(qi, two)
        sums = [jnp.sum(r.top[h], axis=1, keepdims=True) for h in range(2)]
        mixed = jnp.where(first, r.acc[0] / sums[0], r.acc[1] / sums[1])
        r.mix.at[qi][...] = mixed
        r.lse.at[qi][...] = jnp.where(
            first, tops[0] + jnp.log(sums[0]), tops[1] + jnp.log(sums[1])
        )
        r.mixb.at[qi][...] = mixed.astype(BF16).reshape(2, 128, 128)
        mix_copy(qi, 1).start()
        pl.when(z != qi)(lambda: mix_copy(qi, 0).start())


    def turn_units(b, _):
        cols = pl.ds(pl.multiple_of(b * 256, 256), 256)
        r.u1t[cols, :] = r.u1[:, :, :, cols].reshape(1024, 256).T
        return 0

    lax.fori_loop(0, 4, turn_units, 0)
    came_kv[0].wait_recv()
    for qi in range(4):
        if qi < 3:
            came_kv[qi + 1].wait_recv()
        if qi == 1:
            spread_out.pass_on(1)
        if qi == 2:
            spread_feed.pass_on(1)
        attend(qi)
        if qi == 1:
            gather_g.pass_on()
    r.mixin.at[z, e][...] = r.mixb.at[z, e][...]

    spread_out.wait()
    half = links.go(r.wo.at[e], r.wo.at[e], partner)
    links.arrived(r.mixin.at[pl.ds(0, 3), 0], partner, mix_land)
    links.arrived(r.mixin.at[:, 0], partner, mix_land + 1)
    half.wait_recv()
    mixed = jnp.concatenate([r.mixin[s // 2, s % 2] for s in range(8)], axis=1)
    hidden = r.x[...].astype(F32) + jnp.concatenate(
        [mm(mixed, r.wo[h].reshape(1024, 512)) for h in range(2)], axis=1
    )
    r2 = lax.rsqrt(jnp.mean(hidden * hidden, axis=-1, keepdims=True) + EPS)
    unit2 = hidden * r2
    r.hidden[...] = hidden
    r.unit2[...] = unit2
    r.r2[...] = r2
    r.u2.at[z, e][...] = unit2.astype(BF16)
    gather2 = QuickGather(r.u2)
    gather2.start()
    gather_g.ready()

    def turn_grads(b, _):
        cols = pl.ds(pl.multiple_of(b * 256, 256), 256)
        turned = r.gg[:, :, :, cols].reshape(1024, 256).T
        r.e1p.at[b][...] = turned.reshape(2, 128, 1024)
        return 0

    lax.fori_loop(0, 4, turn_grads, 0)
    spread_feed.wait()
    w_down = r.w[:, :, :, :, :, DOWN:OUT].reshape(1024, WIDE)

    def down_back(zz, _):
        back = mm(r.gg.at[zz][...].reshape(256, 1024), w_down)
        r.score.at[0, zz, :, :WIDE][...] = back
        return 0

    lax.fori_loop(0, 4, down_back, 0)

    w_up = r.w[:, :, :, :, :, GATE:DOWN].reshape(1024, 2 * WIDE)
    real = lax.broadcasted_iota(jnp.int32, (256, WIDE), 1) < SLICE
    scatter2, scatter_y = Scatter("e2"), Scatter("out")
    for at, i in enumerate(NEAR):
        if at == 1:
            gather2.pass_on(1)
            gather2.pass_on(3)
        if at == 3:
            gather2.pass_on(2)
        gather2.ready(i)
        zz = lax.rem(z - i + 4, 4)
        sums = mm(r.u2.at[zz][...].reshape(256, 1024), w_up)
        gate, up = sums[:, :WIDE], sums[:, WIDE:]
        sigmoid = 1.0 / (1.0 + jnp.exp(-gate))
        swish = gate * sigmoid
        back = r.score.at[0, zz, :, :WIDE][...]
        act = jnp.where(real, swish * up, 0.0).astype(BF16)
        r.act.at[pl.ds(4 * zz, 4)][...] = act.reshape(4, 64, WIDE)
        d_gate = back * up * sigmoid * (1.0 + gate * (1.0 - sigmoid))
        d_gate = jnp.where(real, d_gate, 0.0).astype(BF16)
        d_up = jnp.where(real, back * swish, 0.0).astype(BF16)
        r.dgu.at[zz][...] = jnp.concatenate([d_gate, d_up], axis=1)
        scatter2.put(i, mt(r.dgu.at[zz][...], w_up))
        if at:
            scatter2.send(NEAR[at - 1])
    scatter2.send(NEAR[3])

    gain_lane = SLICE

    def feed_grads(b, _):
        cols = pl.ds(pl.multiple_of(b * 256, 256), 256)
        units = r.u2[:, :, :, cols].reshape(1024, 256)
        grads = tm(units, r.dgu[...].reshape(1024, 2 * WIDE))
        weights = r.w.at[lax.div(b, 2), pl.ds(2 * lax.rem(b, 2), 2), :, :, :, GATE:DOWN]
        weights = weights[...].reshape(256, 2 * WIDE).astype(F32)
        gain = weights[:, gain_lane : gain_lane + 1]
        lane = lax.broadcasted_iota(jnp.int32, (256, 2 * WIDE), 1)
        keep = lax.rem(lane, WIDE) < SLICE
        weighed = jnp.sum(jnp.where(keep, weights * grads, 0.0), axis=1, keepdims=True) / gain
        shape = (4, 4, 16, -1)
        r.gf.at[b, :, :, :, : 2 * WIDE][...] = (grads * gain).astype(BF16).reshape(shape)
        downs = mm(r.e1p.at[b][...].reshape(256, 1024), r.act[...].reshape(1024, WIDE))
        lane = lax.broadcasted_iota(jnp.int32, (256, WIDE), 1)
        downs = jnp.where(lane == gain_lane, weighed, downs)
        r.gf.at[b, :, :, :, 2 * WIDE :][...] = downs.astype(BF16).reshape(shape)
        return 0

    lax.fori_loop(0, 4, feed_grads, 0)
    sum_f = PlaneSum("f")
    sum_f.start()

    def down_out(i):
        zz = lax.rem(z - i + 4, 4)
        scatter_y.put(i, mt(r.act.at[pl.ds(4 * zz, 4)][...].reshape(256, WIDE), w_down))

    e2 = scatter2.total()
    unit2 = r.unit2[...]
    grad_hidden = r.g[...].astype(F32) + r.r2[...] * (
        e2 - unit2 * jnp.mean(e2 * unit2, axis=-1, keepdims=True)
    )
    r.gh[...] = grad_hidden
    branch = grad_hidden.astype(BF16)
    r.db.at[z, e][...] = branch
    d_mixed = mt(branch[:, :512], r.wo[0].reshape(1024, 512)) + mt(
        branch[:, 512:], r.wo[1].reshape(1024, 512)
    )
    for s in range(8):
        r.dmixb[s // 2, s % 2] = d_mixed[:, s * 128 : (s + 1) * 128].astype(BF16)
    came_mix = links.landing()
    for i in NEAR:
        to = along_z(i)
        for to_e, peer in ((1 - e, other_core(to)), (e, to)):
            if i or peer is not to:
                src = r.dmixb.at[to["z"], to_e]
                links.go(src, r.dmix.at[z, e], peer, came_mix)
    r.dmix.at[z, e][...] = r.dmixb.at[z, e][...]

    gather_b = Gather(r.db)
    gather_b.start()
    for at, i in enumerate(NEAR):
        down_out(i)

    def out_grads():
        grads = tm(r.mixb[...].reshape(1024, 128), r.db[...].reshape(1024, 1024))
        grads = grads.astype(BF16)
        for j in range(2):
            for k in range(8):
                r.go[j, k] = grads[j * 64 : (j + 1) * 64, k * 128 : (k + 1) * 128]
        land = links.landing()
        for n, d in enumerate(plane):
            to = in_plane(*d)
            src = r.go.at[to["xh"], to["xl"] * 4 + to["y"]]
            links.go(src, r.gor.at[n], to, land)
        return land

    for p in range(4):
        r.kt[p] = r.kv[p, :, 0].reshape(512, 128).T

    links.arrived(r.gor.at[pl.ds(0, 14)], partner, came_mix)
    r.dkv[...] = jnp.zeros((4, 2, 256, 256), F32)
    dkv_slots, dkv_land = links.fixed_slots(4), links.landing(4)

    def dkv_copy(zz):
        return links.make(
            r.dkvs.at[zz], r.dkvr.at[zz], across, dkv_slots + zz, dkv_land + zz
        )

    def give(zz):
        both = r.dkv.at[zz, 1 - xh][...].astype(BF16)
        r.dkvs.at[zz, 0][...] = both[:, :128]
        r.dkvs.at[zz, 1][...] = both[:, 128:]
        dkv_copy(zz).start()

    def attend_back(qi):
        queries = halves(r.q[qi])
        grads = r.dmix[qi].reshape(256, 128)
        product = (grads.astype(F32) * r.mix[qi]).T
        grads = halves(grads)
        dots = [jnp.sum(product[k : k + HD], axis=0, keepdims=True) for k in (0, HD)]
        logs = r.lse[qi].T
        logs = [logs[k : k + 1] for k in (0, HD)]
        query_ids = r.ids.at[2 * qi + xh][...].astype(F32)
        def one(p, tiles, masked):
            wide = 256 * tiles
            keys, values = (
                r.kv.at[p, pl.ds(0, tiles), k][...].reshape(wide, 128) for k in range(2)
            )
            keys_turned = r.kt.at[p, :, pl.ds(0, wide)][...]
            d_key, d_value = 0.0, 0.0
            for h in range(2):
                score = mt(keys, queries[h])
                if masked:
                    _, key_ids = ids_of(pair_ids(p)[:, :wide])
                    score = jnp.where(key_ids <= query_ids, score, -1e30)
                prob = jnp.exp(score - logs[h])
                d_score = (prob * (mt(values, grads[h]) - dots[h])).astype(BF16)
                d_value += mm(prob.astype(BF16), grads[h])
                d_key += mm(d_score, queries[h])
                r.dqt[h * HD : (h + 1) * HD] += mm(
                    keys_turned[h * HD : (h + 1) * HD], d_score
                )
            both = jnp.concatenate([d_key, d_value], axis=1).reshape(tiles, 256, 256)
            r.dkv.at[p, pl.ds(0, tiles)][...] += both

        r.dqt[...] = jnp.zeros((128, 256), F32)
        key_tiles(qi, one)
        r.dq[qi] = (r.dqt[...] * 0.125).T
        if qi < 3:
            give(qi + 1)

    attend_back(3)
    for i in NEAR[1:]:
        scatter_y.send(i)
    sum_f.middle()
    attend_back(2)
    r.sf[...] = jnp.concatenate(sum_f.last(), axis=-1).astype(BF16)
    land_sf = links.landing()
    for i in (2, 1, 3):
        to = along_z(i)
        links.go(r.sf.at[to["z"]], r.zf.at[z], to, land_sf)
    r.zf.at[z][...] = r.sf.at[z][...]
    gather_b.pass_on()
    attend_back(1)
    gather_b.ready()
    sum_o = out_grads()
    attend_back(0)
    give(0)
    links.arrived(r.zf.at[pl.ds(0, 3)], partner, land_sf)
    out_f = StagedOut(r.zf, r.ff, r.relay)
    out_f.start()

    scatter1 = Scatter("e1")
    scatter1.slots = links.fixed_slots(4)
    for zz in (3, 2, 1, 0):
        dkv_copy(zz).wait_recv()
        cosine, sine = r.cos[zz], -r.sin[zz]
        d_tile = r.dkv.at[zz, xh][...]
        d_key = d_tile[:, :128] + r.dkvr[zz, 0].astype(F32)
        d_value = d_tile[:, 128:] + r.dkvr[zz, 1].astype(F32)
        r.dqkv[zz] = jnp.concatenate(
            [
                turn(r.dq[zz], cosine, sine).astype(BF16),
                turn(d_key, cosine, sine).astype(BF16),
                d_value.astype(BF16),
            ],
            axis=1,
        )

    def attn_gains(rows):
        at = GATE + WIDE + 256
        last = rows[..., at : at + 128]
        return last.reshape(-1, 128).astype(F32)[:, gain_lane - 256 : gain_lane - 255]

    def qkv_grads(b, _):
        cols = pl.ds(pl.multiple_of(b * 256, 256), 256)
        grads = mm(r.u1t[cols, :], r.dqkv[...].reshape(1024, 384))
        rows = r.w.at[lax.div(b, 2), pl.ds(2 * lax.rem(b, 2), 2)]
        r.gq.at[b][...] = (grads * attn_gains(rows)).astype(BF16).reshape(4, 64, 384)
        return 0

    lax.fori_loop(0, 4, qkv_grads, 0)
    sum_q = PlaneSum("q")
    sum_q.start()
    for zz in (3, 2, 1, 0):
        scatter1.tile(zz, mt(r.dqkv[zz], w_qkv))
        if zz < 3:
            scatter1.tile_send(zz + 1)
    scatter1.tile_send(0)
    out_f.pass_on()
    sum_q.middle()
    r.y[...] = (r.hidden[...] + scatter_y.total()).astype(BF16)
    write("y")

    total = r.go.at[xh, grp][...].astype(F32)
    links.arrived(r.gor, partner, sum_o)
    for n in range(15):
        total = total + r.gor[n].astype(F32)
    r.so[...] = total.astype(BF16)
    done_o = hand_out(r.so, r.fo, grp, head_self, lambda at: {**at, "xh": e, "e": xh})
    summed = jnp.concatenate(sum_q.last(), axis=-1)
    block = 4 * y + x
    rows = r.w.at[lax.div(block, 8), lax.rem(lax.div(block, 2), 4), pl.ds(2 * lax.rem(block, 2), 2)]
    gain = attn_gains(rows)
    weights = rows[:, :, :, :GATE].reshape(64, GATE).astype(F32)
    weighed = jnp.sum(weights * summed, axis=1, keepdims=True) / (gain * gain)
    r.sq[:, :GATE] = summed.astype(BF16)
    r.sq[:, GATE:] = jnp.broadcast_to(weighed, (64, 128)).astype(BF16)
    done_q = hand_out(r.sq, r.fq, z * 2 + e, row_self, lambda at: {**at, "z": y, "e": xl})
    e1 = scatter1.total(True)
    rows = r.x[...].astype(F32)
    r1 = lax.rsqrt(jnp.mean(rows * rows, axis=-1, keepdims=True) + EPS)
    unit1 = rows * r1
    r.gx[...] = r.gh[...] + r1 * (
        e1 - unit1 * jnp.mean(e1 * unit1, axis=-1, keepdims=True)
    )
    write("gx")

    def rows_of(landed, s):
        pieces = [landed[2 * k + s % 2, s // 2] for k in range(4)]
        return jnp.concatenate(pieces, axis=0).astype(F32)

    out_f.finish()
    r.feeds[...] = jnp.zeros((3, 64, FEED), BF16)
    lane = lax.broadcasted_iota(jnp.int32, (64, WIDE), 1)
    for s in range(8):
        part = rows_of(r.ff, s)
        start, many, rest = window(s)
        for n in range(3):
            piece = jnp.where(lane < SLICE, part[:, n * WIDE : (n + 1) * WIDE], 0.0)
            if many > WIDE:
                piece = jnp.concatenate([piece, jnp.zeros((64, 128), F32)], axis=1)
            if rest:
                piece = pltpu.roll(piece, rest, 1)
            r.feeds[n, :, start : start + many] += piece.astype(BF16)
        weighed = part[:, 2 * WIDE + SLICE : 2 * WIDE + SLICE + 1]
        gain_mlp = weighed + (gain_mlp if s else 0.0)
    write("feeds")
    done_o()
    for k in range(8):
        r.heads[3, :, k * 128 : (k + 1) * 128] = r.fo[k]
    done_q()
    for s in range(8):
        part = r.fq[s].astype(F32)
        for n in range(3):
            piece = part[:, n * 128 : (n + 1) * 128]
            r.heads[n, :, s * 128 : (s + 1) * 128] = piece.astype(BF16)
        gain_attn = part[:, 384:] + (gain_attn if s else 0.0)
    lane = lax.broadcasted_iota(jnp.int32, (64, 128), 1)
    r.grad_gains[:, :64] = jnp.where(lane == 0, gain_attn, gain_mlp).T[:8]
    write("heads")
    write("grad_gains")
    for zz in range(4):
        mix_copy(zz, 1).wait_send()
        pl.when(z != zz)(lambda: mix_copy(zz, 0).wait_send())
        dkv_copy(zz).wait_send()
        pl.when(z != zz)(lambda: scatter1.tile_copy(zz).wait_send())
    for at in range(len(links.started) - RING, len(links.started)):
        links.left(at)
    for copy in written:
        copy.wait()
    counts = links.fixed, links.landings, links.count_near
    assert counts == (SENDS, LANDINGS, LOCAL), counts


def rope_tables():
    positions = np.arange(2048, dtype=np.float32)[:, None]
    frequency = np.float32(10000.0) ** (
        np.float32(-2.0) * np.arange(32, dtype=np.float32) / np.float32(64)
    )
    angles = positions * frequency.astype(np.float32)[None, :]
    cosine, sine = np.cos(angles), np.sin(angles)
    cosines = np.concatenate([cosine] * 4, axis=1)
    sines = np.concatenate([-sine, sine, -sine, sine], axis=1)
    shape = (4, 2, 256, 128)
    return cosines.astype(np.float32).reshape(shape), sines.astype(np.float32).reshape(shape)


def per_device(
    tokens,
    blocks,
    w_query,
    w_key,
    w_value,
    w_out,
    w_gate,
    w_up,
    w_down,
    norm_attn,
    norm_mlp,
    cotangent,
):
    gains = jnp.stack([norm_attn, norm_mlp], axis=1)
    extra = jnp.concatenate([w_down.T, jnp.pad(gains, ((0, 0), (0, 126)))], axis=1).astype(F32)
    cosines, sines = rope_tables()
    anywhere = pl.BlockSpec(memory_space=pl.ANY)
    y, gx, heads, feeds, gains = pl.pallas_call(
        kernel,
        out_shape=[jax.ShapeDtypeStruct(*spec) for spec in OUTPUTS.values()],
        in_specs=[anywhere] * len(INPUTS),
        out_specs=[anywhere] * len(OUTPUTS),
        scratch_shapes=[pltpu.VMEM(*spec) for spec in HELD.values()]
        + [
            pltpu.SemaphoreType.DMA((SENDS,)),
            pltpu.SemaphoreType.DMA((LANDINGS,)),
            pltpu.SemaphoreType.DMA((LOCAL,)),
        ],
        compiler_params=pltpu.CompilerParams(
            collective_id=0, has_side_effects=True, vmem_limit_bytes=63 * 2**20
        ),
    )(
        tokens[0],
        cotangent[0],
        w_query,
        w_key,
        w_value,
        w_out,
        w_gate,
        w_up,
        extra,
        blocks.reshape(8, 1, 256),
        jnp.asarray(cosines),
        jnp.asarray(sines),
    )

    return (
        y[None],
        gx[None],
        *[heads[n].astype(F32) for n in range(4)],
        feeds[0].astype(F32),
        feeds[1].astype(F32),
        feeds[2].astype(F32).T,
        gains[0, :64],
        gains[1, :64],
    )


def solution(mesh):
    both = ("grp", "ctx")
    row = P(both, None)
    tokens = P("grp", "ctx", None)
    shard = P("ctx", None)
    return jax.shard_map(
        per_device,
        mesh=mesh,
        in_specs=(
            tokens,
            P("grp", None),
            *[row] * 6,
            P(None, both),
            P(both),
            P(both),
            tokens,
        ),
        out_specs=(tokens, tokens, *[shard] * 6, P(None, "ctx"), P("ctx"), P("ctx")),
        check_vma=False,
    )
```
